256 devices in a mesh: lat: 16 (over y_lo, z), lon: 16 (over y_hi, x, core).
Axes of the slice: x: 4, y: 4 (y_hi: 2, y_lo: 2; y = y_hi * 2 + y_lo), z: 8, core: 2. Of those that a mesh axis runs over, the one named last changes fastest.
Arguments:
- tokens: bfloat16 [128, 128, 2560], P('lon', 'lat'), may hold values from -6 to 6
- w_qkv: bfloat16 [16, 480, 2560], P('lat'), may hold values from -0.125 to 0.125
- key_mask: int32 [128, 128], replicated, may hold values 0 or 1
- band_of_row: int32 [128], replicated, may hold values from 0 to 31, as said below
- radius: int32 [16], replicated, may hold values from 1 to 4, as said below
- qk_scale: float32 [16], replicated, may hold values from 24 to 64
Outputs:
- attended: bfloat16 [16, 128, 20480], P('lat', 'lon')
The draws below stay inside these ranges and needn't reach their ends.
Inputs may be any that keep to these rules, and one draw needn't show every extreme that they name: `band_of_row`: band numbers never fall along the rows; every aligned block of 8 rows holds exactly two bands, each a run of consecutive rows inside the block, and band numbers count up from 0 without gaps. Some head has radius 4.
All inputs are finite; a program needn't handle non-finite values.
Results may differ from the reference program's by a relative error of at most 0.012.
Values may be sent and summed in bfloat16 or wider, within the bound.
No kernel may reach another device: no remote copies, remote signals or barrier semaphores. Data moves between devices by JAX's collectives and lax.ppermute only.
A program may use at most 192 MiB of HBM per device.

```python
import math
import jax
import jax.numpy as jnp
from jax import lax

D = 2560
HEADS = 16
HEAD_DIM = 160
BLOCK_ROWS = 8
WIN = 4
NROW = 128
NCOL = 128


def draw_band_of_row(key, part):
    key = jax.random.fold_in(key, 11)
    block_count = NROW // BLOCK_ROWS
    splits = jax.random.randint(key, (block_count,), 1, BLOCK_ROWS)
    row_ids = jnp.arange(NROW)
    block_ids = row_ids // BLOCK_ROWS
    inner = row_ids % BLOCK_ROWS
    upper = (inner >= splits[block_ids]).astype(jnp.int32)
    return (2 * block_ids + upper).astype(jnp.int32)


def draw_radius(key, part):
    key = jax.random.fold_in(key, 23)
    first_key, second_key = jax.random.split(key)
    values = jax.random.randint(first_key, (HEADS,), 1, WIN + 1)
    chosen = jax.random.randint(second_key, (), 0, HEADS)
    return jnp.where(jnp.arange(HEADS) == chosen, WIN, values).astype(jnp.int32)


def set_ends(drawn, rng, smallest, top_value):
    index_at = [jax.random.randint(jax.random.fold_in(rng, axis), (), 0, length) for axis, length in enumerate(drawn.shape)]
    main_axis = drawn.shape.index(max(drawn.shape))
    neighbour = index_at[:main_axis] + [(index_at[main_axis] + 1) % drawn.shape[main_axis]] + index_at[main_axis + 1:]
    return drawn.at[tuple(index_at)].set(smallest).at[tuple(neighbour)].set(top_value)


def levels(own_key, shape, pieces, smallest, top_value):
    def one(dim, blocks):
        heights = jax.random.uniform(jax.random.fold_in(jax.random.fold_in(own_key, 6), dim), (blocks,), jnp.float32, smallest / len(pieces), top_value / len(pieces))
        return jnp.repeat(jnp.exp(heights), shape[dim] // blocks).reshape((-1,) + (1,) * (len(shape) - dim - 1))

    loudness = one(*pieces[0])
    for cut in pieces[1:]:
        loudness = loudness * one(*cut)
    return loudness


def noise(stream_key, extent, spread, most, cuts=(), held_as=jnp.bfloat16):
    drawn = spread * jax.random.normal(stream_key, extent, jnp.float32)
    if cuts:
        drawn = drawn * levels(stream_key, extent, cuts, -0.22, 0.18)
    return jnp.clip(drawn, -most, most).astype(held_as)


def setup_inputs(seed: int = 0) -> dict:
    streams_of = jax.random.split(jax.random.key(seed), 7)
    tokens = noise(streams_of[0], (NCOL, NROW, D), 1.0, 6.0, ((0, 16), (1, 16)))
    w_qkv = noise(streams_of[1], (HEADS, 3 * HEAD_DIM, D), D ** -0.5, 0.125, ((0, 16),))
    key_mask = set_ends((jax.random.randint(streams_of[2], (NCOL, NROW), 0, 4) < 3).astype(jnp.int32), jax.random.fold_in(streams_of[2], 1), 0, 1)
    band_of_row = draw_band_of_row(jax.random.fold_in(streams_of[6], 71), 0)
    radius = draw_radius(jax.random.fold_in(streams_of[6], 71), 0)
    qk_scale = jnp.clip(jnp.exp(jax.random.uniform(streams_of[5], (HEADS,), jnp.float32, math.log(24.0), math.log(64.0))), 24.0, 64.0)
    return dict(tokens=tokens, w_qkv=w_qkv, key_mask=key_mask, band_of_row=band_of_row, radius=radius, qk_scale=qk_scale)


epsilon = 1e-06

def rms_last(values):
    return values * lax.rsqrt(lax.optimization_barrier(jnp.mean(values * values, axis=-1, keepdims=True)) + epsilon)

def rounded_float(weights):
    return lax.optimization_barrier(weights.astype(jnp.bfloat16)).astype(jnp.float32)

def reference(tokens, w_qkv, key_mask, band_of_row, radius, qk_scale):
    n_cols, n_rows, model_width = tokens.shape
    blocks = n_rows // BLOCK_ROWS
    normed = rms_last(tokens.astype(jnp.float32)).astype(jnp.bfloat16).reshape(n_cols * n_rows, model_width)
    mask_pad = jnp.pad(key_mask, ((0, 0), (WIN, WIN)))
    col_ids = jnp.arange(n_cols, dtype=jnp.int32)
    col_gap = jnp.abs((col_ids[None, :] - col_ids[:, None] + n_cols // 2) % n_cols - n_cols // 2)
    inner_rows = jnp.arange(BLOCK_ROWS, dtype=jnp.int32)
    outer_rows = jnp.arange(2 * BLOCK_ROWS, dtype=jnp.int32)
    row_gap = jnp.abs(outer_rows[None, :] - WIN - inner_rows[:, None])
    diagonal = inner_rows[:, None] == inner_rows[None, :]
    same_col = col_ids[:, None] == col_ids[None, :]
    zonal_self = same_col[:, None, :, None] & diagonal[None, :, None, :]
    window_self = (col_gap == 0)[:, None, :, None] & (row_gap == 0)[None, :, None, :]

    def one_head(head_inputs):
        weight_rows, reach, score_scale = head_inputs
        projected = jnp.dot(normed, weight_rows.T, preferred_element_type=jnp.float32)
        projected = projected.reshape(n_cols, n_rows, 3 * HEAD_DIM)
        queries = rms_last(projected[..., :HEAD_DIM]).astype(jnp.bfloat16)
        key_rows = rms_last(projected[..., HEAD_DIM:2 * HEAD_DIM]).astype(jnp.bfloat16)
        value_rows = projected[..., 2 * HEAD_DIM:].astype(jnp.bfloat16)
        key_pad = jnp.pad(key_rows, ((0, 0), (WIN, WIN), (0, 0)))
        value_pad = jnp.pad(value_rows, ((0, 0), (WIN, WIN), (0, 0)))
        factor = score_scale / HEAD_DIM
        within = (col_gap <= reach)[:, None, :, None] & (row_gap <= reach)[None, :, None, :]

        def attend(query_part, key_part, value_part, allowed):
            scores = jnp.einsum('cid,kjd->cikj', query_part, key_part)
            weights = jnp.where(allowed, jnp.exp(scores * factor), 0.0)
            denominator = lax.optimization_barrier(jnp.sum(weights, axis=(2, 3)))
            summed = jnp.einsum('cikj,kjd->cid', rounded_float(weights), value_part)
            return summed / denominator[..., None]

        def one_block(block):
            first_row = block * BLOCK_ROWS
            query_block = lax.dynamic_slice_in_dim(queries, first_row, BLOCK_ROWS, 1).astype(jnp.float32)
            key_block = lax.dynamic_slice_in_dim(key_rows, first_row, BLOCK_ROWS, 1).astype(jnp.float32)
            value_block = lax.dynamic_slice_in_dim(value_rows, first_row, BLOCK_ROWS, 1).astype(jnp.float32)
            band_block = lax.dynamic_slice_in_dim(band_of_row, first_row, BLOCK_ROWS, 0)
            same_band = band_block[:, None] == band_block[None, :]
            usable_zone = lax.dynamic_slice_in_dim(key_mask, first_row, BLOCK_ROWS, 1) == 1
            zonal_ok = same_band[None, :, None, :] & (usable_zone[None, None, :, :] | zonal_self)
            zonal = attend(query_block, key_block, value_block, zonal_ok).astype(jnp.bfloat16)
            key_wide = lax.dynamic_slice_in_dim(key_pad, first_row, 2 * BLOCK_ROWS, 1).astype(jnp.float32)
            value_wide = lax.dynamic_slice_in_dim(value_pad, first_row, 2 * BLOCK_ROWS, 1).astype(jnp.float32)
            usable_wide = lax.dynamic_slice_in_dim(mask_pad, first_row, 2 * BLOCK_ROWS, 1) == 1
            window_ok = within & (usable_wide[None, None, :, :] | window_self)
            window = attend(query_block, key_wide, value_wide, window_ok)
            return (window + zonal.astype(jnp.float32)).astype(jnp.bfloat16)
        mixed = lax.map(one_block, jnp.arange(blocks, dtype=jnp.int32))
        return jnp.transpose(mixed, (1, 0, 2, 3)).reshape(n_cols, n_rows * HEAD_DIM)
    return lax.map(one_head, (w_qkv, radius, qk_scale))
```

```python
import functools

import jax
import jax.numpy as jnp
from jax import lax
from jax.experimental import pallas as pl
from jax.experimental.pallas import tpu as pltpu
from jax.sharding import Mesh, PartitionSpec as P

HEAD_DIM = 160
QKV = 3 * HEAD_DIM
ROWS = 8
WIN = 4
COLS = 128
HALF = COLS // 2
KEY_ROWS = ROWS + 2 * WIN
EPS = 1e-06
BIG = 1e30
LOG2E = 1.4426950408889634
LAT, LON = 16, 16
AXES = ("y_lo", "z", "y_hi", "x", "core")
SIZES = (2, 8, 2, 4, 2)
NT = (((1,), (1,)), ((), ()))
MIB = 1024 * 1024


def place_of(block):
    y_lo, rest = block // 8, block % 8
    side, k = rest // 4, rest % 4
    return y_lo, side ^ y_lo, k if side == 0 else 3 - k


def block_of(y_lo, y_hi, x):
    side = y_hi ^ y_lo
    return y_lo * 8 + side * 4 + jnp.where(side == 0, x, 3 - x)


def flat(*pairs):
    index = 0
    for coordinate, size in pairs:
        index = index * size + coordinate
    return index


def spread_perm():
    pairs = []
    for y_lo in range(2):
        for z in range(8):
            for y_hi in range(2):
                for x in range(4):
                    _, to_y_hi, to_x = place_of(y_lo * 8 + z)
                    pairs.append(
                        (
                            flat((y_lo, 2), (z, 8), (y_hi, 2), (x, 4)),
                            flat((y_lo, 2), (y_hi * 4 + x, 8), (to_y_hi, 2), (to_x, 4)),
                        )
                    )
    return pairs


def neighbour_perm(step, cross):
    pairs = []
    for block in range(16):
        if not 0 <= block + step < 16:
            continue
        for core in range(2):
            here, there = place_of(block), place_of(block + step)
            source = flat((here[0], 2), (here[1], 2), (here[2], 4), (core, 2))
            target = flat((there[0], 2), (there[1], 2), (there[2], 4), (core ^ cross, 2))
            pairs.append((source, target))
    return pairs


def return_perm(k):
    pairs = []
    for y_lo in range(2):
        for s in range(8):
            for core in range(2):
                source = flat((y_lo, 2), (s, 8), (core, 2))
                pairs.append((source, flat((core, 2), (s ^ k, 8), (y_lo, 2))))
    return pairs


SWAP = [(0, 1), (1, 0)]


def project_kernel(flag_ref, *refs):
    shards, (own_ref, other_ref) = refs[:8], refs[8:10]
    keep, send, keep_top, keep_bottom, send_top, send_bottom, x_ref = refs[10:]
    for i in range(8):
        x_ref[64 * i : 64 * (i + 1), :] = shards[i][...]
    lane = lax.broadcasted_iota(jnp.int32, (1, QKV), 1)
    is_q = lane < HEAD_DIM
    is_k = (lane >= HEAD_DIM) & (lane < 2 * HEAD_DIM)
    for w_ref, own in ((own_ref, 1), (other_ref, 0)):
        p = lax.dot_general(x_ref[...], w_ref[...], NT, preferred_element_type=jnp.float32)
        squares = p * p
        q_mean = jnp.sum(jnp.where(is_q, squares, 0.0), axis=-1, keepdims=True) / HEAD_DIM
        k_mean = jnp.sum(jnp.where(is_k, squares, 0.0), axis=-1, keepdims=True) / HEAD_DIM
        scale = jnp.where(is_q, lax.rsqrt(q_mean + EPS), jnp.where(is_k, lax.rsqrt(k_mean + EPS), 1.0))
        p = (p * scale).reshape(8, ROWS, 8, QKV)
        for r in range(ROWS):
            row = p[:, r].reshape(HALF, QKV).astype(jnp.bfloat16)

            def store(whole, top, bottom):
                whole[r] = row
                if r < WIN:
                    top[r] = row[:, 128:]
                else:
                    bottom[r - WIN] = row[:, 128:]

            @pl.when(flag_ref[0] == own)
            def _():
                store(keep, keep_top, keep_bottom)

            @pl.when(flag_ref[0] != own)
            def _():
                store(send, send_top, send_bottom)


def project(flag, shards, own, other):
    whole = jax.ShapeDtypeStruct((ROWS, HALF, QKV), jnp.bfloat16)
    edge = jax.ShapeDtypeStruct((WIN, HALF, QKV - 128), jnp.bfloat16)
    vmem = pl.BlockSpec(memory_space=pltpu.VMEM)
    return pl.pallas_call(
        project_kernel,
        out_shape=[whole, whole, edge, edge, edge, edge],
        in_specs=[pl.BlockSpec(memory_space=pltpu.SMEM)] + [vmem] * 10,
        out_specs=[vmem] * 6,
        scratch_shapes=[pltpu.VMEM((512, own.shape[1]), jnp.bfloat16)],
        compiler_params=pltpu.CompilerParams(vmem_limit_bytes=32 * MIB),
        cost_estimate=pl.CostEstimate(
            flops=2 * 512 * 960 * 2560, bytes_accessed=8 * MIB, transcendentals=0
        ),
        name="project",
    )(flag, *shards, own, other)


def attend_kernel(ints, factor_ref, keep, other, keep_t, other_t, keep_b, other_b, bias, band, *refs):
    chunks, (ks, vs, masks, out) = refs[:8], refs[8:]
    z, core, radius, main = ints[0], ints[1], ints[2], ints[3]
    factor = factor_ref[0]
    ones = jnp.where(lax.broadcasted_iota(jnp.int32, (HALF, 96), 1) == 0, 1.0, 0.0).astype(jnp.bfloat16)

    def place(row, half, key, value):
        at = pl.ds(row * COLS + half * HALF, HALF)
        ks[at, :] = key
        vs[at, :HEAD_DIM] = value
        vs[at, HEAD_DIM:] = ones

    for half, (body, top, bottom) in enumerate(((keep, keep_t, keep_b), (other, other_t, other_b))):
        for r in range(ROWS):
            whole = body[r]
            place(WIN + r, half, whole[:, HEAD_DIM : 2 * HEAD_DIM], whole[:, 2 * HEAD_DIM :])
        for r in range(WIN):
            for edge, row in ((top, r), (bottom, r + WIN + ROWS)):
                whole = edge[r]
                place(row, half, whole[:, 32 : 32 + HEAD_DIM], whole[:, 32 + HEAD_DIM :])

    def column(shape, dim):
        at = lax.broadcasted_iota(jnp.int32, shape, dim)
        return ((z + (at >> 3)) & 7) * 16 + (core ^ (at >> 6)) * 8 + (at & 7)

    gap = (column((COLS, COLS), 0) - column((COLS, COLS), 1) + radius) & (COLS - 1)
    near = jnp.where(gap <= 2 * radius, 1.0, 0.0)
    for d in range(WIN + 1):
        masks[d] = jnp.where(radius >= d, near, 0.0)
    eye = lax.broadcasted_iota(jnp.int32, (COLS, COLS), 0) == lax.broadcasted_iota(jnp.int32, (COLS, COLS), 1)

    for r in range(ROWS):
        query = jnp.concatenate([keep[r][:, :HEAD_DIM], other[r][:, :HEAD_DIM]], axis=0)
        zonal_parts, window_parts = [], []
        for row in range(KEY_ROWS):
            inside = WIN <= row < WIN + ROWS
            near_row = abs(row - WIN - r) <= WIN
            if not (inside or near_row):
                continue
            scores = lax.dot_general(
                query, ks[row * COLS : (row + 1) * COLS, :], NT, preferred_element_type=jnp.float32
            )
            shift = bias[row : row + 1, :]
            if row - WIN == r:
                shift = jnp.where(eye, 0.0, shift)
            weights = jnp.exp2(scores * factor + shift)
            if inside:
                same = band[r * ROWS + row - WIN]
                zonal_parts.append((weights * same).astype(jnp.bfloat16))
            if near_row:
                window_parts.append((weights * masks[abs(row - WIN - r)]).astype(jnp.bfloat16))
        zonal = jnp.dot(
            jnp.concatenate(zonal_parts, axis=1),
            vs[WIN * COLS : (WIN + ROWS) * COLS, :],
            preferred_element_type=jnp.float32,
        )
        window = jnp.dot(
            jnp.concatenate(window_parts, axis=1),
            vs[r * COLS : (r + 2 * WIN + 1) * COLS, :],
            preferred_element_type=jnp.float32,
        )
        zonal = zonal[:, :HEAD_DIM] / zonal[:, HEAD_DIM : HEAD_DIM + 1]
        window = window[:, :HEAD_DIM] / window[:, HEAD_DIM : HEAD_DIM + 1]
        total = window + zonal.astype(jnp.bfloat16).astype(jnp.float32)
        out[:, :, :, r * HEAD_DIM : (r + 1) * HEAD_DIM] = total.reshape(2, 8, 8, HEAD_DIM)
    for k in range(8):
        group = ints[4 + k]
        chunks[k][0] = out[main, group].astype(jnp.bfloat16)
        chunks[k][1] = out[1 - main, group].astype(jnp.bfloat16)


def attend(ints, factor, parts, bias, band):
    smem = pl.BlockSpec(memory_space=pltpu.SMEM)
    vmem = pl.BlockSpec(memory_space=pltpu.VMEM)
    chunk = jax.ShapeDtypeStruct((2, 8, ROWS * HEAD_DIM), jnp.bfloat16)
    return pl.pallas_call(
        attend_kernel,
        out_shape=[chunk] * 8,
        in_specs=[smem, smem] + [vmem] * 7 + [smem],
        out_specs=[vmem] * 8,
        scratch_shapes=[
            pltpu.VMEM((KEY_ROWS * COLS, HEAD_DIM), jnp.bfloat16),
            pltpu.VMEM((KEY_ROWS * COLS, 256), jnp.bfloat16),
            pltpu.VMEM((WIN + 1, COLS, COLS), jnp.float32),
            pltpu.VMEM((2, 8, 8, ROWS * HEAD_DIM), jnp.float32),
        ],
        compiler_params=pltpu.CompilerParams(vmem_limit_bytes=32 * MIB),
        cost_estimate=pl.CostEstimate(
            flops=3 * 10**9, bytes_accessed=4 * MIB, transcendentals=2 * 10**6
        ),
        name="attend",
    )(ints, factor, *parts, bias, band)


def assemble_kernel(at, *refs):
    mains, got, out = refs[:8], refs[8], refs[9]
    width = ROWS * HEAD_DIM
    for k in range(8):
        out[0, :, pl.ds(pl.multiple_of(at[k] * width, 128), width)] = mains[k][0]
        out[0, :, pl.ds(pl.multiple_of(at[8 + k] * width, 128), width)] = got[k]


def assemble(at, mains, got):
    vmem = pl.BlockSpec(memory_space=pltpu.VMEM)
    return pl.pallas_call(
        assemble_kernel,
        out_shape=jax.ShapeDtypeStruct((1, 8, LAT * ROWS * HEAD_DIM), jnp.bfloat16),
        in_specs=[pl.BlockSpec(memory_space=pltpu.SMEM)] + [vmem] * 9,
        out_specs=vmem,
        name="assemble",
    )(at, *mains, got)


def body(tokens, w_qkv, key_mask, band_of_row, radius, qk_scale):
    y_lo, z, y_hi, x, core = (lax.axis_index(a) for a in AXES)
    sector = y_hi * 4 + x
    block = block_of(y_lo, y_hi, x)
    head = core * 8 + z
    model = tokens.shape[-1]

    wide = tokens.astype(jnp.float32)
    normed = wide * lax.rsqrt(jnp.mean(wide * wide, axis=-1, keepdims=True) + EPS)
    normed = jnp.transpose(normed.astype(jnp.bfloat16), (1, 0, 2)).reshape(64, model)
    first = lax.ppermute(normed, ("y_lo", "z", "y_hi", "x"), spread_perm())

    own = w_qkv[0]
    rows = QKV // 2
    half = lax.dynamic_slice_in_dim(own, core * rows, rows, 0)
    mine = lax.ppermute(half, "y_lo", SWAP)
    theirs = lax.ppermute(mine, "core", SWAP)
    other = jnp.concatenate(
        [jnp.where(core == 0, mine, theirs), jnp.where(core == 0, theirs, mine)], axis=0
    )

    up = [(i, (i + 1) % 8) for i in range(8)]
    down = [(i, (i - 1) % 8) for i in range(8)]
    shards = [first] + [None] * 7
    a = b = first
    for k in range(1, 4):
        a = lax.ppermute(a, "z", up)
        b = lax.ppermute(b, "z", down)
        shards[8 - k] = a
        shards[k] = b
    a = lax.ppermute(a[:32], "z", up)
    b = lax.ppermute(b[32:], "z", down)
    shards[4] = jnp.concatenate([a, b], axis=0)

    flag = jnp.where(core == y_lo, 1, 0).astype(jnp.int32).reshape(1)
    keep, send, keep_top, keep_bottom, send_top, send_bottom = project(flag, shards, own, other)

    ring = ("y_lo", "y_hi", "x", "core")
    received = lax.ppermute(send, "core", SWAP)
    keep_t = lax.ppermute(keep_bottom, ring, neighbour_perm(1, 0))
    keep_b = lax.ppermute(keep_top, ring, neighbour_perm(-1, 0))
    other_t = lax.ppermute(send_bottom, ring, neighbour_perm(1, 1))
    other_b = lax.ppermute(send_top, ring, neighbour_perm(-1, 1))

    padded = jnp.pad(key_mask, ((0, 0), (WIN, WIN)))
    usable = lax.dynamic_slice_in_dim(padded, block * ROWS, KEY_ROWS, 1)
    usable = usable.reshape(8, 2, 8, KEY_ROWS)
    twice = jnp.concatenate([usable, usable], axis=0)
    usable = lax.dynamic_slice_in_dim(twice, z, 8, 0)
    usable = jnp.where(core == 0, usable, usable[:, ::-1])
    bias = jnp.where(jnp.transpose(usable, (3, 1, 0, 2)).reshape(KEY_ROWS, COLS) == 1, 0.0, -BIG)
    ids = lax.dynamic_slice_in_dim(band_of_row, block * ROWS, ROWS, 0)
    band = (ids[:, None] == ids[None, :]).astype(jnp.float32).reshape(ROWS * ROWS)

    groups = [((sector ^ k) - z) & 7 for k in range(8)]
    reach = lax.dynamic_index_in_dim(radius, head, keepdims=False)
    ints = jnp.stack([z, core, reach, core ^ y_lo] + groups).astype(jnp.int32)
    factor = lax.dynamic_slice_in_dim(qk_scale, head, 1, 0) / HEAD_DIM * LOG2E
    parts = (keep, received, keep_t, other_t, keep_b, other_b)
    chunks = attend(ints, factor, parts, bias, band)

    landed = [lax.ppermute(chunks[k], ring, return_perm(k)) for k in range(8)]
    give = jnp.stack([part[1] for part in landed])
    got = lax.ppermute(give, "core", SWAP)
    at = []
    for from_y_lo in (core, 1 - core):
        for k in range(8):
            source = sector ^ k
            at.append(block_of(from_y_lo, source >> 2, source & 3))
    return assemble(jnp.stack(at).astype(jnp.int32), landed, got)


def solution(mesh):
    wide = Mesh(mesh.devices.reshape(SIZES), AXES)
    lat, lon = ("y_lo", "z"), ("y_hi", "x", "core")
    in_specs = (P(lon, lat, None), P(lat, None, None), P(), P(), P(), P())
    out_specs = P(lat, lon, None)
    return jax.shard_map(body, mesh=wide, in_specs=in_specs, out_specs=out_specs, check_vma=False)
```

```python
import jax
import jax.numpy as jnp
from jax import lax
from jax.experimental import pallas as pl
from jax.experimental.pallas import tpu as pltpu
from jax.sharding import Mesh, PartitionSpec as P

HEAD_DIM = 160
QKV = 3 * HEAD_DIM
ROWS = 8
WIN = 4
COLS = 128
HALF = COLS // 2
KEY_ROWS = ROWS + 2 * WIN
EPS = 1e-06
BIG = 1e30
LOG2E = 1.4426950408889634
LAT, LON = 16, 16
AXES = ("y_lo", "z", "y_hi", "x", "core")
SIZES = (2, 8, 2, 4, 2)
NT = (((1,), (1,)), ((), ()))
MIB = 1024 * 1024
SMEM = pl.BlockSpec(memory_space=pltpu.SMEM)
VMEM = pl.BlockSpec(memory_space=pltpu.VMEM)


def place_of(block):
    y_lo, rest = block // 8, block % 8
    side, k = rest // 4, rest % 4
    return y_lo, side ^ y_lo, k if side == 0 else 3 - k


def block_of(y_lo, y_hi, x):
    side = y_hi ^ y_lo
    return y_lo * 8 + side * 4 + jnp.where(side == 0, x, 3 - x)


def flat(*pairs):
    index = 0
    for coordinate, size in pairs:
        index = index * size + coordinate
    return index


def spread_perm():
    pairs = []
    for y_lo in range(2):
        for z in range(8):
            _, to_y_hi, to_x = place_of(y_lo * 8 + z)
            for s in range(8):
                for core in range(2):
                    to_z = (s + 2 * z + core) % 8
                    source = flat((y_lo, 2), (z, 8), (s, 8), (core, 2))
                    target = flat((y_lo, 2), (to_z, 8), (to_y_hi, 2), (to_x, 4), (core, 2))
                    pairs.append((source, target))
    return pairs


def neighbour_perm(step):
    pairs = []
    for block in range(16):
        if 0 <= block + step < 16:
            here, there = place_of(block), place_of(block + step)
            pairs.append(
                (
                    flat((here[0], 2), (here[1], 2), (here[2], 4)),
                    flat((there[0], 2), (there[1], 2), (there[2], 4)),
                )
            )
    return pairs


def return_perm(k):
    pairs = []
    for y_lo in range(2):
        for s in range(8):
            for core in range(2):
                source = flat((y_lo, 2), (s, 8), (core, 2))
                pairs.append((source, flat((core, 2), (s ^ k, 8), (y_lo, 2))))
    return pairs


SWAP = [(0, 1), (1, 0)]


def project_kernel(flag_ref, *refs):
    pieces, (own_ref, other_ref) = refs[:16], refs[16:18]
    keep, send, x_ref = refs[18:]
    for i in range(16):
        x_ref[32 * i : 32 * (i + 1), :] = pieces[i][...]
    lane = lax.broadcasted_iota(jnp.int32, (1, QKV), 1)
    is_q = lane < HEAD_DIM
    is_k = (lane >= HEAD_DIM) & (lane < 2 * HEAD_DIM)
    for w_ref, own in ((own_ref, 1), (other_ref, 0)):
        p = lax.dot_general(x_ref[...], w_ref[...], NT, preferred_element_type=jnp.float32)
        squares = p * p
        q_mean = jnp.sum(jnp.where(is_q, squares, 0.0), axis=-1, keepdims=True) / HEAD_DIM
        k_mean = jnp.sum(jnp.where(is_k, squares, 0.0), axis=-1, keepdims=True) / HEAD_DIM
        scale = jnp.where(is_q, lax.rsqrt(q_mean + EPS), jnp.where(is_k, lax.rsqrt(k_mean + EPS), 1.0))
        p = (p * scale).reshape(8, ROWS, 8, QKV)
        for r in range(ROWS):
            row = p[:, r].reshape(HALF, QKV).astype(jnp.bfloat16)

            @pl.when(flag_ref[0] == own)
            def _():
                keep[r] = row

            @pl.when(flag_ref[0] != own)
            def _():
                send[r] = row


def project(flag, pieces, own, other):
    whole = jax.ShapeDtypeStruct((ROWS, HALF, QKV), jnp.bfloat16)
    return pl.pallas_call(
        project_kernel,
        out_shape=[whole, whole],
        in_specs=[SMEM] + [VMEM] * 18,
        out_specs=[VMEM] * 2,
        scratch_shapes=[pltpu.VMEM((512, own.shape[1]), jnp.bfloat16)],
        compiler_params=pltpu.CompilerParams(vmem_limit_bytes=32 * MIB),
        cost_estimate=pl.CostEstimate(
            flops=2 * 512 * 960 * 2560, bytes_accessed=8 * MIB, transcendentals=0
        ),
        name="project",
    )(flag, *pieces, own, other)


def edges_kernel(keep, other, top, bottom):
    for r in range(WIN):
        for edge, row, turn in ((top, r, 16), (bottom, r + WIN, HALF - 16)):
            whole = jnp.concatenate([keep[row][:, HEAD_DIM:], other[row][:, HEAD_DIM:]], axis=1)
            edge[r, : HALF - turn] = whole[turn:]
            edge[r, HALF - turn :] = whole[:turn]


def edges(keep, other):
    edge = jax.ShapeDtypeStruct((WIN, HALF, 4 * HEAD_DIM), jnp.bfloat16)
    return pl.pallas_call(
        edges_kernel,
        out_shape=[edge, edge],
        in_specs=[VMEM] * 2,
        out_specs=[VMEM] * 2,
        cost_estimate=pl.CostEstimate(flops=0, bytes_accessed=MIB, transcendentals=0),
        name="edges",
    )(keep, other)


def put(ks, vs, row, half, key, value):
    at = pl.ds(row * COLS + half * HALF, HALF)
    ks[at, :] = key
    vs[at, :HEAD_DIM] = value
    first = lax.broadcasted_iota(jnp.int32, (HALF, 256 - HEAD_DIM), 1) == 0
    vs[at, HEAD_DIM:] = jnp.where(first, 1.0, 0.0).astype(jnp.bfloat16)


def fill_masks(ints, masks):
    base, core, radius = ints[0], ints[1], ints[2]

    def column(dim):
        at = lax.broadcasted_iota(jnp.int32, (COLS, COLS), dim)
        side = core ^ (at >> 6)
        return ((base + (at >> 3) - side) & 7) * 16 + side * 8 + (at & 7)

    gap = (column(0) - column(1) + radius) & (COLS - 1)
    near = jnp.where(gap <= 2 * radius, 1.0, 0.0)
    for d in range(WIN + 1):
        masks[d] = jnp.where(radius >= d, near, 0.0)


def query_of(keep, other, r):
    return jnp.concatenate([keep[r][:, :HEAD_DIM], other[r][:, :HEAD_DIM]], axis=0)


def scores_of(query, ks, row):
    keys = ks[row * COLS : (row + 1) * COLS, :]
    return lax.dot_general(query, keys, NT, preferred_element_type=jnp.float32)


def inner_kernel(ints, factor_ref, keep, other, bias, band, zonal_ref, window_ref, ks, vs, masks):
    factor = factor_ref[0]
    for half, part in enumerate((keep, other)):
        for r in range(ROWS):
            whole = part[r]
            put(ks, vs, r, half, whole[:, HEAD_DIM : 2 * HEAD_DIM], whole[:, 2 * HEAD_DIM :])
    fill_masks(ints, masks)
    eye = lax.broadcasted_iota(jnp.int32, (COLS, COLS), 0) == lax.broadcasted_iota(jnp.int32, (COLS, COLS), 1)
    for r in range(ROWS):
        query = query_of(keep, other, r)
        low, high = max(0, r - WIN), min(ROWS, r + WIN + 1)
        zonal_parts, window_parts = [], []
        for row in range(ROWS):
            shift = bias[WIN + row : WIN + row + 1, :]
            if row == r:
                shift = jnp.where(eye, 0.0, shift)
            weights = jnp.exp2(scores_of(query, ks, row) * factor + shift)
            zonal_parts.append((weights * band[r * ROWS + row]).astype(jnp.bfloat16))
            if low <= row < high:
                window_parts.append((weights * masks[abs(row - r)]).astype(jnp.bfloat16))
        zonal = jnp.dot(jnp.concatenate(zonal_parts, axis=1), vs[...], preferred_element_type=jnp.float32)
        window_ref[r] = jnp.dot(
            jnp.concatenate(window_parts, axis=1),
            vs[low * COLS : high * COLS, :],
            preferred_element_type=jnp.float32,
        )
        zonal_ref[r] = (zonal[:, :HEAD_DIM] / zonal[:, HEAD_DIM : HEAD_DIM + 1]).astype(jnp.bfloat16)


def inner(ints, factor, keep, other, bias, band):
    return pl.pallas_call(
        inner_kernel,
        out_shape=[
            jax.ShapeDtypeStruct((ROWS, COLS, HEAD_DIM), jnp.bfloat16),
            jax.ShapeDtypeStruct((ROWS, COLS, 256), jnp.float32),
        ],
        in_specs=[SMEM, SMEM] + [VMEM] * 3 + [SMEM],
        out_specs=[VMEM] * 2,
        scratch_shapes=[
            pltpu.VMEM((ROWS * COLS, HEAD_DIM), jnp.bfloat16),
            pltpu.VMEM((ROWS * COLS, 256), jnp.bfloat16),
            pltpu.VMEM((WIN + 1, COLS, COLS), jnp.float32),
        ],
        compiler_params=pltpu.CompilerParams(vmem_limit_bytes=32 * MIB),
        cost_estimate=pl.CostEstimate(
            flops=3 * 10**9, bytes_accessed=4 * MIB, transcendentals=10**6
        ),
        name="inner",
    )(ints, factor, keep, other, bias, band)


def outer_kernel(ints, factor_ref, keep, other, top, bottom, bias, zonal_ref, window_ref, *refs):
    chunks, (ks, vs, masks, out) = refs[:8], refs[8:]
    factor = factor_ref[0]
    for edge, first in ((top, 0), (bottom, WIN)):
        for r in range(WIN):
            whole = edge[r]
            for half in range(2):
                at = half * 2 * HEAD_DIM
                key, value = whole[:, at : at + HEAD_DIM], whole[:, at + HEAD_DIM : at + 2 * HEAD_DIM]
                put(ks, vs, first + r, half, key, value)
    fill_masks(ints, masks)
    for r in range(ROWS):
        query = query_of(keep, other, r)
        rows = range(r, WIN) if r < WIN else range(WIN, r + 1)
        parts = []
        for row in rows:
            gap = r + WIN - row if r < WIN else ROWS + row - WIN - r
            line = row if r < WIN else row + ROWS
            weights = jnp.exp2(scores_of(query, ks, row) * factor + bias[line : line + 1, :])
            parts.append((weights * masks[gap]).astype(jnp.bfloat16))
        values = vs[rows[0] * COLS : (rows[-1] + 1) * COLS, :]
        window = window_ref[r] + jnp.dot(
            jnp.concatenate(parts, axis=1), values, preferred_element_type=jnp.float32
        )
        window = window[:, :HEAD_DIM] / window[:, HEAD_DIM : HEAD_DIM + 1]
        total = window + zonal_ref[r].astype(jnp.float32)
        out[:, :, :, r * HEAD_DIM : (r + 1) * HEAD_DIM] = total.reshape(2, 8, 8, HEAD_DIM)
    for k in range(8):
        chunks[k][0] = out[ints[3], ints[4 + k]].astype(jnp.bfloat16)
        chunks[k][1] = out[1 - ints[3], ints[12 + k]].astype(jnp.bfloat16)


def outer(ints, factor, keep, other, top, bottom, bias, zonal, window):
    chunk = jax.ShapeDtypeStruct((2, 8, ROWS * HEAD_DIM), jnp.bfloat16)
    return pl.pallas_call(
        outer_kernel,
        out_shape=[chunk] * 8,
        in_specs=[SMEM, SMEM] + [VMEM] * 7,
        out_specs=[VMEM] * 8,
        scratch_shapes=[
            pltpu.VMEM((2 * WIN * COLS, HEAD_DIM), jnp.bfloat16),
            pltpu.VMEM((2 * WIN * COLS, 256), jnp.bfloat16),
            pltpu.VMEM((WIN + 1, COLS, COLS), jnp.float32),
            pltpu.VMEM((2, 8, 8, ROWS * HEAD_DIM), jnp.float32),
        ],
        compiler_params=pltpu.CompilerParams(vmem_limit_bytes=32 * MIB),
        cost_estimate=pl.CostEstimate(
            flops=10**9, bytes_accessed=4 * MIB, transcendentals=10**6
        ),
        name="outer",
    )(ints, factor, keep, other, top, bottom, bias, zonal, window)


def assemble_kernel(at, *refs):
    mains, got, out = refs[:8], refs[8], refs[9]
    width = ROWS * HEAD_DIM
    for k in range(8):
        out[0, :, pl.ds(pl.multiple_of(at[k] * width, 128), width)] = mains[k][0]
        out[0, :, pl.ds(pl.multiple_of(at[8 + k] * width, 128), width)] = got[k]


def assemble(at, mains, got):
    return pl.pallas_call(
        assemble_kernel,
        out_shape=jax.ShapeDtypeStruct((1, 8, LAT * ROWS * HEAD_DIM), jnp.bfloat16),
        in_specs=[SMEM] + [VMEM] * 9,
        out_specs=VMEM,
        name="assemble",
    )(at, *mains, got)


def body(tokens, w_qkv, key_mask, band_of_row, radius, qk_scale):
    y_lo, z, y_hi, x, core = (lax.axis_index(a) for a in AXES)
    sector = y_hi * 4 + x
    block = block_of(y_lo, y_hi, x)
    head = core * 8 + z
    model = tokens.shape[-1]

    wide = tokens.astype(jnp.float32)
    normed = wide * lax.rsqrt(jnp.mean(wide * wide, axis=-1, keepdims=True) + EPS)
    normed = jnp.transpose(normed.astype(jnp.bfloat16), (1, 0, 2)).reshape(64, model)
    first = [lax.ppermute(normed[at : at + 32], AXES, spread_perm()) for at in (0, 32)]

    own = w_qkv[0]
    rows = QKV // 2
    half = lax.dynamic_slice_in_dim(own, core * rows, rows, 0)
    *first, half = lax.optimization_barrier((*first, half))
    mine = lax.ppermute(half, "y_lo", SWAP)

    up = [(i, (i + 1) % 8) for i in range(8)]
    down = [(i, (i - 1) % 8) for i in range(8)]
    shards = [first] + [[None, None] for _ in range(7)]
    a, b = list(first), list(first)
    for k in range(1, 5):
        for h in range(2):
            if k < 4 or h == 0:
                a[h] = shards[8 - k][h] = lax.ppermute(a[h], "z", up)
            if k < 4 or h == 1:
                b[h] = shards[k][h] = lax.ppermute(b[h], "z", down)
        if k == 3:
            mine, *both = lax.optimization_barrier((mine, *a, *b))
            a, b = both[:2], both[2:]
            theirs = lax.ppermute(mine, "core", SWAP)
    other_w = jnp.concatenate(
        [jnp.where(core == 0, mine, theirs), jnp.where(core == 0, theirs, mine)], axis=0
    )
    pieces = [shards[i][h] for i in range(8) for h in range(2)]

    flag = jnp.where(core == y_lo, 1, 0).astype(jnp.int32).reshape(1)
    keep, send = project(flag, pieces, own, other_w)
    other = lax.ppermute(send, "core", SWAP)
    top_rows, bottom_rows = edges(keep, other)
    ring = ("y_lo", "y_hi", "x")
    top = lax.ppermute(bottom_rows, ring, neighbour_perm(1))
    bottom = lax.ppermute(top_rows, ring, neighbour_perm(-1))

    base = (z - 2 * block) & 7
    padded = jnp.pad(key_mask, ((0, 0), (WIN, WIN)))
    usable = lax.dynamic_slice_in_dim(padded, block * ROWS, KEY_ROWS, 1)
    usable = usable.reshape(8, 2, 8, KEY_ROWS)
    twice = jnp.concatenate([usable, usable], axis=0)
    halves = []
    for side in (core, 1 - core):
        start = ((base - side) & 7, side, 0, 0)
        halves.append(lax.dynamic_slice(twice, start, (8, 1, 8, KEY_ROWS)).reshape(HALF, KEY_ROWS))
    usable = jnp.transpose(jnp.concatenate(halves, axis=0))
    bias = jnp.where(usable == 1, 0.0, -BIG)
    ids = lax.dynamic_slice_in_dim(band_of_row, block * ROWS, ROWS, 0)
    band = (ids[:, None] == ids[None, :]).astype(jnp.float32).reshape(ROWS * ROWS)

    groups = [((sector ^ k) - base + side) & 7 for side in (y_lo, 1 - y_lo) for k in range(8)]
    reach = lax.dynamic_index_in_dim(radius, head, keepdims=False)
    ints = jnp.stack([base, core, reach, core ^ y_lo] + groups).astype(jnp.int32)
    factor = lax.dynamic_slice_in_dim(qk_scale, head, 1, 0) / HEAD_DIM * LOG2E
    zonal, window = inner(ints, factor, keep, other, bias, band)
    chunks = outer(ints, factor, keep, other, top, bottom, bias, zonal, window)

    corners = ("y_lo", "y_hi", "x", "core")
    landed = [lax.ppermute(chunks[k], corners, return_perm(k)) for k in range(8)]
    give = jnp.stack([part[1] for part in landed])
    got = lax.ppermute(give, "core", SWAP)
    at = []
    for from_y_lo in (core, 1 - core):
        for k in range(8):
            source = sector ^ k
            at.append(block_of(from_y_lo, source >> 2, source & 3))
    return assemble(jnp.stack(at).astype(jnp.int32), landed, got)


def solution(mesh):
    wide = Mesh(mesh.devices.reshape(SIZES), AXES)
    lat, lon = ("y_lo", "z"), ("y_hi", "x", "core")
    in_specs = (P(lon, lat, None), P(lat, None, None), P(), P(), P(), P())
    out_specs = P(lat, lon, None)
    return jax.shard_map(body, mesh=wide, in_specs=in_specs, out_specs=out_specs, check_vma=False)
```

```python
import jax
import jax.numpy as jnp
from jax import lax
from jax.experimental import pallas as pl
from jax.experimental.pallas import tpu as pltpu
from jax.sharding import Mesh, PartitionSpec as P

HEAD_DIM = 160
QKV = 3 * HEAD_DIM
ROWS = 8
WIN = 4
COLS = 128
HALF = COLS // 2
KEY_ROWS = ROWS + 2 * WIN
EPS = 1e-06
BIG = 1e30
LOG2E = 1.4426950408889634
LAT, LON = 16, 16
AXES = ("y_lo", "z", "y_hi", "x", "core")
SIZES = (2, 8, 2, 4, 2)
NT = (((1,), (1,)), ((), ()))
MIB = 1024 * 1024
SMEM = pl.BlockSpec(memory_space=pltpu.SMEM)
VMEM = pl.BlockSpec(memory_space=pltpu.VMEM)


def place_of(block):
    y_lo, rest = block // 8, block % 8
    side, k = rest // 4, rest % 4
    return y_lo, side ^ y_lo, k if side == 0 else 3 - k


def block_of(y_lo, y_hi, x):
    side = y_hi ^ y_lo
    return y_lo * 8 + side * 4 + jnp.where(side == 0, x, 3 - x)


def flat(*pairs):
    index = 0
    for coordinate, size in pairs:
        index = index * size + coordinate
    return index


def spread_perm():
    pairs = []
    for y_lo in range(2):
        for z in range(8):
            _, to_y_hi, to_x = place_of(y_lo * 8 + z)
            for s in range(8):
                for core in range(2):
                    to_z = (s + 2 * z + core) % 8
                    source = flat((y_lo, 2), (z, 8), (s, 8), (core, 2))
                    target = flat((y_lo, 2), (to_z, 8), (to_y_hi, 2), (to_x, 4), (core, 2))
                    pairs.append((source, target))
    return pairs


def neighbour_perm(step):
    pairs = []
    for block in range(16):
        if 0 <= block + step < 16:
            here, there = place_of(block), place_of(block + step)
            pairs.append(
                (
                    flat((here[0], 2), (here[1], 2), (here[2], 4)),
                    flat((there[0], 2), (there[1], 2), (there[2], 4)),
                )
            )
    return pairs


def return_perm(k):
    pairs = []
    for y_lo in range(2):
        for s in range(8):
            for core in range(2):
                source = flat((y_lo, 2), (s, 8), (core, 2))
                pairs.append((source, flat((core, 2), (s ^ k, 8), (y_lo, 2))))
    return pairs


SWAP = [(0, 1), (1, 0)]


def gather(pieces, x_ref):
    for i in range(16):
        x_ref[32 * i : 32 * (i + 1), :] = pieces[i][...]


def normalized(p):
    lane = lax.broadcasted_iota(jnp.int32, (1, QKV), 1)
    is_q = lane < HEAD_DIM
    is_k = (lane >= HEAD_DIM) & (lane < 2 * HEAD_DIM)
    squares = p * p
    q_mean = jnp.sum(jnp.where(is_q, squares, 0.0), axis=-1, keepdims=True) / HEAD_DIM
    k_mean = jnp.sum(jnp.where(is_k, squares, 0.0), axis=-1, keepdims=True) / HEAD_DIM
    scale = jnp.where(is_q, lax.rsqrt(q_mean + EPS), jnp.where(is_k, lax.rsqrt(k_mean + EPS), 1.0))
    p = (p * scale).reshape(8, ROWS, 8, QKV)
    return [p[:, r].reshape(HALF, QKV).astype(jnp.bfloat16) for r in range(ROWS)]


def project_own_kernel(*refs):
    pieces, w_ref, rows, x_ref = refs[:16], refs[16], refs[17], refs[18]
    gather(pieces, x_ref)
    p = lax.dot_general(x_ref[...], w_ref[...], NT, preferred_element_type=jnp.float32)
    for r, row in enumerate(normalized(p)):
        rows[r] = row


def project_own(pieces, own):
    return pl.pallas_call(
        project_own_kernel,
        out_shape=jax.ShapeDtypeStruct((ROWS, HALF, QKV), jnp.bfloat16),
        in_specs=[VMEM] * 17,
        out_specs=VMEM,
        scratch_shapes=[pltpu.VMEM((512, own.shape[1]), jnp.bfloat16)],
        compiler_params=pltpu.CompilerParams(vmem_limit_bytes=16 * MIB),
        cost_estimate=pl.CostEstimate(
            flops=2 * 512 * 480 * 2560, bytes_accessed=5 * MIB, transcendentals=0
        ),
        name="project_own",
    )(*pieces, own)


def project_other_kernel(flags, *refs):
    pieces, (mine, theirs, own_rows), (keep, send, top, bottom, x_ref) = refs[:16], refs[16:19], refs[19:]
    gather(pieces, x_ref)
    width = mine.shape[1]
    near = pl.ds(pl.multiple_of(flags[1] * width, width), width)
    far = pl.ds(pl.multiple_of((1 - flags[1]) * width, width), width)
    p = lax.dot_general(x_ref[:, near], mine[...], NT, preferred_element_type=jnp.float32)
    p += lax.dot_general(x_ref[:, far], theirs[...], NT, preferred_element_type=jnp.float32)
    for r, row in enumerate(normalized(p)):

        def store(first, second):
            keep[r] = first
            send[r] = second
            edge = top if r < WIN else bottom
            edge[r % WIN] = jnp.concatenate([first[:, HEAD_DIM:], second[:, HEAD_DIM:]], axis=1)

        @pl.when(flags[0] == 1)
        def _():
            store(own_rows[r], row)

        @pl.when(flags[0] != 1)
        def _():
            store(row, own_rows[r])


def project_other(flags, pieces, mine, theirs, own_rows):
    whole = jax.ShapeDtypeStruct((ROWS, HALF, QKV), jnp.bfloat16)
    edge = jax.ShapeDtypeStruct((WIN, HALF, 4 * HEAD_DIM), jnp.bfloat16)
    return pl.pallas_call(
        project_other_kernel,
        out_shape=[whole, whole, edge, edge],
        in_specs=[SMEM] + [VMEM] * 19,
        out_specs=[VMEM] * 4,
        scratch_shapes=[pltpu.VMEM((512, 2 * mine.shape[1]), jnp.bfloat16)],
        compiler_params=pltpu.CompilerParams(vmem_limit_bytes=16 * MIB),
        cost_estimate=pl.CostEstimate(
            flops=2 * 512 * 480 * 2560, bytes_accessed=5 * MIB, transcendentals=0
        ),
        name="project_other",
    )(flags, *pieces, mine, theirs, own_rows)


def put(ks, vs, first, key, value):
    at = pl.ds(first, key.shape[0])
    ks[at, :] = key
    vs[at, :HEAD_DIM] = value
    is_one = lax.broadcasted_iota(jnp.int32, (key.shape[0], 256 - HEAD_DIM), 1) == 0
    vs[at, HEAD_DIM:] = jnp.where(is_one, 1.0, 0.0).astype(jnp.bfloat16)


def fill_masks(ints, masks):
    base, core, radius = ints[0], ints[1], ints[2]

    def column(dim):
        at = lax.broadcasted_iota(jnp.int32, (COLS, COLS), dim)
        side = core ^ (at >> 6)
        return ((base + (at >> 3) - side) & 7) * 16 + side * 8 + (at & 7)

    gap = (column(0) - column(1) + radius) & (COLS - 1)
    near = jnp.where(gap <= 2 * radius, 1.0, 0.0)
    for d in range(WIN + 1):
        masks[d] = jnp.where(radius >= d, near, 0.0)


def query_of(keep, other, r):
    return jnp.concatenate([keep[r][:, :HEAD_DIM], other[r][:, :HEAD_DIM]], axis=0)


def scores_of(query, ks, row):
    keys = ks[row * COLS : (row + 1) * COLS, :]
    return lax.dot_general(query, keys, NT, preferred_element_type=jnp.float32)


def inner_kernel(ints, factor_ref, keep, other, bias, band, zonal_ref, window_ref, ks, vs, masks):
    factor = factor_ref[0]
    for half, part in enumerate((keep, other)):
        for r in range(ROWS):
            whole = part[r]
            put(ks, vs, r * COLS + half * HALF, whole[:, HEAD_DIM : 2 * HEAD_DIM], whole[:, 2 * HEAD_DIM :])
    fill_masks(ints, masks)
    eye = lax.broadcasted_iota(jnp.int32, (COLS, COLS), 0) == lax.broadcasted_iota(jnp.int32, (COLS, COLS), 1)
    for r in range(ROWS):
        query = query_of(keep, other, r)
        low, high = max(0, r - WIN), min(ROWS, r + WIN + 1)
        zonal_parts, window_parts = [], []
        for row in range(ROWS):
            shift = bias[WIN + row : WIN + row + 1, :]
            if row == r:
                shift = jnp.where(eye, 0.0, shift)
            weights = jnp.exp2(scores_of(query, ks, row) * factor + shift)
            zonal_parts.append((weights * band[r * ROWS + row]).astype(jnp.bfloat16))
            if low <= row < high:
                window_parts.append((weights * masks[abs(row - r)]).astype(jnp.bfloat16))
        zonal = jnp.dot(jnp.concatenate(zonal_parts, axis=1), vs[...], preferred_element_type=jnp.float32)
        window_ref[r] = jnp.dot(
            jnp.concatenate(window_parts, axis=1),
            vs[low * COLS : high * COLS, :],
            preferred_element_type=jnp.float32,
        )
        zonal_ref[r] = (zonal[:, :HEAD_DIM] / zonal[:, HEAD_DIM : HEAD_DIM + 1]).astype(jnp.bfloat16)


def inner(ints, factor, keep, other, bias, band):
    return pl.pallas_call(
        inner_kernel,
        out_shape=[
            jax.ShapeDtypeStruct((ROWS, COLS, HEAD_DIM), jnp.bfloat16),
            jax.ShapeDtypeStruct((ROWS, COLS, 256), jnp.float32),
        ],
        in_specs=[SMEM, SMEM] + [VMEM] * 3 + [SMEM],
        out_specs=[VMEM] * 2,
        scratch_shapes=[
            pltpu.VMEM((ROWS * COLS, HEAD_DIM), jnp.bfloat16),
            pltpu.VMEM((ROWS * COLS, 256), jnp.bfloat16),
            pltpu.VMEM((WIN + 1, COLS, COLS), jnp.float32),
        ],
        compiler_params=pltpu.CompilerParams(vmem_limit_bytes=16 * MIB),
        cost_estimate=pl.CostEstimate(
            flops=3 * 10**9, bytes_accessed=4 * MIB, transcendentals=10**6
        ),
        name="inner",
    )(ints, factor, keep, other, bias, band)


def outer_kernel(ints, factor_ref, keep, other, top, top_far, bottom, bottom_far, bias, zonal_ref, window_ref, *refs):
    chunks, (ks, vs, masks, out) = refs[:8], refs[8:]
    factor = factor_ref[0]
    for edge, half, first, turn in ((top, 0, 0, 16), (top_far, 1, 0, 16), (bottom, 0, WIN, 48), (bottom_far, 1, WIN, 48)):
        at = half * 2 * HEAD_DIM
        for r in range(WIN):
            whole = edge[r][:, at : at + 2 * HEAD_DIM]
            to = (first + r) * COLS + half * HALF
            for part, start in ((whole[: HALF - turn], to + turn), (whole[HALF - turn :], to)):
                put(ks, vs, start, part[:, :HEAD_DIM], part[:, HEAD_DIM:])
    fill_masks(ints, masks)
    for r in range(ROWS):
        query = query_of(keep, other, r)
        rows = range(r, WIN) if r < WIN else range(WIN, r + 1)
        parts = []
        for row in rows:
            gap = r + WIN - row if r < WIN else ROWS + row - WIN - r
            line = row if r < WIN else row + ROWS
            weights = jnp.exp2(scores_of(query, ks, row) * factor + bias[line : line + 1, :])
            parts.append((weights * masks[gap]).astype(jnp.bfloat16))
        values = vs[rows[0] * COLS : (rows[-1] + 1) * COLS, :]
        window = window_ref[r] + jnp.dot(
            jnp.concatenate(parts, axis=1), values, preferred_element_type=jnp.float32
        )
        window = window[:, :HEAD_DIM] / window[:, HEAD_DIM : HEAD_DIM + 1]
        total = window + zonal_ref[r].astype(jnp.float32)
        out[:, :, :, r * HEAD_DIM : (r + 1) * HEAD_DIM] = total.reshape(2, 8, 8, HEAD_DIM)
    for k in range(8):
        chunks[k][0] = out[ints[3], ints[4 + k]].astype(jnp.bfloat16)
        chunks[k][1] = out[1 - ints[3], ints[12 + k]].astype(jnp.bfloat16)


def outer(ints, factor, *operands):
    chunk = jax.ShapeDtypeStruct((2, 8, ROWS * HEAD_DIM), jnp.bfloat16)
    return pl.pallas_call(
        outer_kernel,
        out_shape=[chunk] * 8,
        in_specs=[SMEM, SMEM] + [VMEM] * 9,
        out_specs=[VMEM] * 8,
        scratch_shapes=[
            pltpu.VMEM((2 * WIN * COLS, HEAD_DIM), jnp.bfloat16),
            pltpu.VMEM((2 * WIN * COLS, 256), jnp.bfloat16),
            pltpu.VMEM((WIN + 1, COLS, COLS), jnp.float32),
            pltpu.VMEM((2, 8, 8, ROWS * HEAD_DIM), jnp.float32),
        ],
        compiler_params=pltpu.CompilerParams(vmem_limit_bytes=16 * MIB),
        cost_estimate=pl.CostEstimate(
            flops=10**9, bytes_accessed=4 * MIB, transcendentals=10**6
        ),
        name="outer",
    )(ints, factor, *operands)


def assemble_kernel(at, *refs):
    mains, got, out = refs[:8], refs[8], refs[9]
    width = ROWS * HEAD_DIM
    for k in range(8):
        out[0, :, pl.ds(pl.multiple_of(at[k] * width, 128), width)] = mains[k][0]
        out[0, :, pl.ds(pl.multiple_of(at[8 + k] * width, 128), width)] = got[k]


def assemble(at, mains, got):
    return pl.pallas_call(
        assemble_kernel,
        out_shape=jax.ShapeDtypeStruct((1, 8, LAT * ROWS * HEAD_DIM), jnp.bfloat16),
        in_specs=[SMEM] + [VMEM] * 9,
        out_specs=VMEM,
        compiler_params=pltpu.CompilerParams(vmem_limit_bytes=4 * MIB),
        cost_estimate=pl.CostEstimate(flops=0, bytes_accessed=MIB, transcendentals=0),
        name="assemble",
    )(at, *mains, got)


def body(tokens, w_qkv, key_mask, band_of_row, radius, qk_scale):
    y_lo, z, y_hi, x, core = (lax.axis_index(a) for a in AXES)
    sector = y_hi * 4 + x
    block = block_of(y_lo, y_hi, x)
    head = core * 8 + z
    model = tokens.shape[-1]

    wide = tokens.astype(jnp.float32)
    normed = wide * lax.rsqrt(jnp.mean(wide * wide, axis=-1, keepdims=True) + EPS)
    normed = jnp.transpose(normed.astype(jnp.bfloat16), (1, 0, 2)).reshape(64, model)
    first = lax.ppermute(normed, AXES, spread_perm())

    base = (z - 2 * block) & 7
    padded = jnp.pad(key_mask, ((0, 0), (WIN, WIN)))
    usable = lax.dynamic_slice_in_dim(padded, block * ROWS, KEY_ROWS, 1)
    usable = usable.reshape(8, 2, 8, KEY_ROWS)
    twice = jnp.concatenate([usable, usable], axis=0)
    halves = []
    for side in (core, 1 - core):
        start = ((base - side) & 7, side, 0, 0)
        halves.append(lax.dynamic_slice(twice, start, (8, 1, 8, KEY_ROWS)).reshape(HALF, KEY_ROWS))
    usable = jnp.transpose(jnp.concatenate(halves, axis=0))
    bias = jnp.where(usable == 1, 0.0, -BIG)
    ids = lax.dynamic_slice_in_dim(band_of_row, block * ROWS, ROWS, 0)
    band = (ids[:, None] == ids[None, :]).astype(jnp.float32).reshape(ROWS * ROWS)
    groups = [((sector ^ k) - base + side) & 7 for side in (y_lo, 1 - y_lo) for k in range(8)]
    reach = lax.dynamic_index_in_dim(radius, head, keepdims=False)
    ints = jnp.stack([base, core, reach, core ^ y_lo] + groups).astype(jnp.int32)
    factor = lax.dynamic_slice_in_dim(qk_scale, head, 1, 0) / HEAD_DIM * LOG2E
    at = []
    for from_y_lo in (core, 1 - core):
        for k in range(8):
            source = sector ^ k
            at.append(block_of(from_y_lo, source >> 2, source & 3))
    at = jnp.stack(at).astype(jnp.int32)
    flags = jnp.stack([core == y_lo, core]).astype(jnp.int32)

    own = w_qkv[0]
    half = lax.dynamic_slice_in_dim(own, core * (model // 2), model // 2, 1)
    first, half, bias, band, ints, factor, at, flags = lax.optimization_barrier(
        (first, half, bias, band, ints, factor, at, flags)
    )
    mine = lax.ppermute(half, "y_lo", SWAP)

    up = [(i, (i + 1) % 8) for i in range(8)]
    down = [(i, (i - 1) % 8) for i in range(8)]
    shards = [[first[:32], first[32:]]] + [[None, None] for _ in range(7)]
    a, b = list(shards[0]), list(shards[0])
    for k in range(1, 5):
        for h in range(2):
            if k < 4 or h == 0:
                a[h] = shards[8 - k][h] = lax.ppermute(a[h], "z", up)
            if k < 4 or h == 1:
                b[h] = shards[k][h] = lax.ppermute(b[h], "z", down)
    last = ((4, 0), (4, 1), (5, 1), (3, 0))
    mine, *ends = lax.optimization_barrier((mine, *(shards[i][h] for i, h in last)))
    for (i, h), end in zip(last, ends):
        shards[i][h] = end
    theirs = lax.ppermute(mine, "core", SWAP)
    pieces = [shards[i][h] for i in range(8) for h in range(2)]

    own_rows = project_own(pieces, own)
    keep, send, top_rows, bottom_rows = project_other(flags, pieces, mine, theirs, own_rows)
    ring = ("y_lo", "y_hi", "x")
    top = lax.ppermute(bottom_rows, ring, neighbour_perm(1))
    bottom = lax.ppermute(top_rows, ring, neighbour_perm(-1))
    other = lax.ppermute(send, "core", SWAP)
    zonal, window = inner(ints, factor, keep, other, bias, band)
    top, bottom, window = lax.optimization_barrier((top, bottom, window))
    top_far = lax.ppermute(top, "core", SWAP)
    bottom_far = lax.ppermute(bottom, "core", SWAP)
    chunks = outer(ints, factor, keep, other, top, top_far, bottom, bottom_far, bias, zonal, window)

    corners = ("y_lo", "y_hi", "x", "core")
    landed = [lax.ppermute(chunks[k], corners, return_perm(k)) for k in range(8)]
    give = jnp.stack([part[1] for part in landed])
    got = lax.ppermute(give, "core", SWAP)
    return assemble(at, landed, got)


def solution(mesh):
    wide = Mesh(mesh.devices.reshape(SIZES), AXES)
    lat, lon = ("y_lo", "z"), ("y_hi", "x", "core")
    in_specs = (P(lon, lat, None), P(lat, None, None), P(), P(), P(), P())
    out_specs = P(lat, lon, None)
    return jax.shard_map(body, mesh=wide, in_specs=in_specs, out_specs=out_specs, check_vma=False)
```

```python
import jax
import jax.numpy as jnp
from jax import lax
from jax.experimental import pallas as pl
from jax.experimental.pallas import tpu as pltpu
from jax.sharding import Mesh, PartitionSpec as P

HEAD_DIM = 160
QKV = 3 * HEAD_DIM
ROWS = 8
WIN = 4
COLS = 128
HALF = COLS // 2
KEY_ROWS = ROWS + 2 * WIN
EPS = 1e-06
BIG = 1e30
LOG2E = 1.4426950408889634
LAT, LON = 16, 16
AXES = ("y_lo", "z", "y_hi", "x", "core")
SIZES = (2, 8, 2, 4, 2)
NT = (((1,), (1,)), ((), ()))
MIB = 1024 * 1024
SMEM = pl.BlockSpec(memory_space=pltpu.SMEM)
VMEM = pl.BlockSpec(memory_space=pltpu.VMEM)


def place_of(block):
    y_lo, rest = block // 8, block % 8
    side, k = rest // 4, rest % 4
    return y_lo, side ^ y_lo, k if side == 0 else 3 - k


def block_of(y_lo, y_hi, x):
    side = y_hi ^ y_lo
    return y_lo * 8 + side * 4 + jnp.where(side == 0, x, 3 - x)


def flat(*pairs):
    index = 0
    for coordinate, size in pairs:
        index = index * size + coordinate
    return index


def spread_perm():
    pairs = []
    for y_lo in range(2):
        for z in range(8):
            _, to_y_hi, to_x = place_of(y_lo * 8 + z)
            for s in range(8):
                for core in range(2):
                    to_z = (s + 2 * z + 4 * core) % 8
                    source = flat((y_lo, 2), (z, 8), (s, 8), (core, 2))
                    target = flat((y_lo, 2), (to_z, 8), (to_y_hi, 2), (to_x, 4), (core, 2))
                    pairs.append((source, target))
    return pairs


def neighbour_perm(step):
    pairs = []
    for block in range(16):
        if 0 <= block + step < 16:
            here, there = place_of(block), place_of(block + step)
            pairs.append(
                (
                    flat((here[0], 2), (here[1], 2), (here[2], 4)),
                    flat((there[0], 2), (there[1], 2), (there[2], 4)),
                )
            )
    return pairs


def return_perm(k):
    pairs = []
    for y_lo in range(2):
        for s in range(8):
            for core in range(2):
                source = flat((y_lo, 2), (s, 8), (core, 2))
                pairs.append((source, flat((core, 2), (s ^ k, 8), (y_lo, 2))))
    return pairs


SWAP = [(0, 1), (1, 0)]


def normalized(p):
    lane = lax.broadcasted_iota(jnp.int32, (1, QKV), 1)
    is_q = lane < HEAD_DIM
    is_k = (lane >= HEAD_DIM) & (lane < 2 * HEAD_DIM)
    squares = p * p
    q_mean = jnp.sum(jnp.where(is_q, squares, 0.0), axis=-1, keepdims=True) / HEAD_DIM
    k_mean = jnp.sum(jnp.where(is_k, squares, 0.0), axis=-1, keepdims=True) / HEAD_DIM
    scale = jnp.where(is_q, lax.rsqrt(q_mean + EPS), jnp.where(is_k, lax.rsqrt(k_mean + EPS), 1.0))
    groups = p.shape[0] // (8 * ROWS)
    p = (p * scale).reshape(groups, ROWS, 8, QKV)
    return [p[:, r].reshape(8 * groups, QKV).astype(jnp.bfloat16) for r in range(ROWS)]


def project_kernel(flags, *refs):
    pieces, (own, mine, theirs), (keep, send, top, bottom, x_ref) = refs[:-8], refs[-8:-5], refs[-5:]
    for i, piece in enumerate(pieces):
        x_ref[32 * i : 32 * (i + 1), :] = piece[...]
    width = mine.shape[1]
    near = pl.ds(pl.multiple_of(flags[1] * width, width), width)
    far = pl.ds(pl.multiple_of((1 - flags[1]) * width, width), width)
    p = lax.dot_general(x_ref[...], own[...], NT, preferred_element_type=jnp.float32)
    own_rows = normalized(p)
    p = lax.dot_general(x_ref[:, near], mine[...], NT, preferred_element_type=jnp.float32)
    p += lax.dot_general(x_ref[:, far], theirs[...], NT, preferred_element_type=jnp.float32)
    other_rows = normalized(p)

    def store(first, second):
        for r in range(ROWS):
            keep[r] = first[r]
            send[r] = second[r]
            edge = top if r < WIN else bottom
            edge[r % WIN] = jnp.concatenate([first[r][:, HEAD_DIM:], second[r][:, HEAD_DIM:]], axis=1)

    @pl.when(flags[0] == 1)
    def _():
        store(own_rows, other_rows)

    @pl.when(flags[0] != 1)
    def _():
        store(other_rows, own_rows)


def project(flags, pieces, own, mine, theirs, cost):
    tokens = 32 * len(pieces)
    whole = jax.ShapeDtypeStruct((ROWS, tokens // 8, QKV), jnp.bfloat16)
    edge = jax.ShapeDtypeStruct((WIN, tokens // 8, 4 * HEAD_DIM), jnp.bfloat16)
    return pl.pallas_call(
        project_kernel,
        out_shape=[whole, whole, edge, edge],
        in_specs=[SMEM] + [VMEM] * (len(pieces) + 3),
        out_specs=[VMEM] * 4,
        scratch_shapes=[pltpu.VMEM((tokens, own.shape[1]), jnp.bfloat16)],
        compiler_params=pltpu.CompilerParams(vmem_limit_bytes=20 * MIB),
        cost_estimate=pl.CostEstimate(
            flops=cost, bytes_accessed=MIB, transcendentals=0
        ),
        name=f"project_{tokens}",
    )(flags, *pieces, own, mine, theirs)


def put(ks, vs, first, key, value):
    at = pl.ds(first, key.shape[0])
    ks[at, :] = key
    vs[at, :HEAD_DIM] = value
    is_one = lax.broadcasted_iota(jnp.int32, (key.shape[0], 256 - HEAD_DIM), 1) == 0
    vs[at, HEAD_DIM:] = jnp.where(is_one, 1.0, 0.0).astype(jnp.bfloat16)


def group_of(i):
    return i ^ ((i >> 1) & 2)


def columns(base, core, shape, dim):
    at = lax.broadcasted_iota(jnp.int32, shape, dim)
    side = core ^ (at >> 6)
    return ((base + group_of((at >> 3) & 7) - 4 * side) & 7) * 16 + side * 8 + (at & 7)


def fill_masks(masks, first, query_base, key_base, core, radius):
    square = (COLS, COLS)
    gap = (columns(query_base, core, square, 0) - columns(key_base, core, square, 1) + radius) & (COLS - 1)
    near = jnp.where(gap <= 2 * radius, 1.0, 0.0)
    for d in range(WIN + 1):
        masks[first + d] = jnp.where(radius >= d, near, 0.0)


def shifts(usable, key_base, core):
    square = (COLS, COLS)
    there = lax.broadcasted_iota(jnp.int32, square, 0) == columns(key_base, core, square, 1)
    moved = jnp.dot(usable[...], jnp.where(there, 1.0, 0.0), preferred_element_type=jnp.float32)
    return jnp.where(moved > 0.5, 0.0, -BIG)


def query_of(parts, r):
    return jnp.concatenate([part[r][:, :HEAD_DIM] for part in parts], axis=0)


def scores_of(query, ks, row):
    keys = ks[row * COLS : (row + 1) * COLS, :]
    return lax.dot_general(query, keys, NT, preferred_element_type=jnp.float32)


def inner_kernel(ints, factor_ref, band, usable, *refs):
    parts, (zonal_ref, window_ref, ks, vs, masks) = refs[:4], refs[4:]
    factor = factor_ref[0]
    start = 0
    for part in parts:
        for r in range(ROWS):
            whole = part[r]
            put(ks, vs, r * COLS + start, whole[:, HEAD_DIM : 2 * HEAD_DIM], whole[:, 2 * HEAD_DIM :])
        start += part.shape[1]
    fill_masks(masks, 0, ints[0], ints[0], ints[1], ints[2])
    bias = shifts(usable, ints[0], ints[1])
    eye = lax.broadcasted_iota(jnp.int32, (COLS, COLS), 0) == lax.broadcasted_iota(jnp.int32, (COLS, COLS), 1)
    for r in range(ROWS):
        query = query_of(parts, r)
        low, high = max(0, r - WIN), min(ROWS, r + WIN + 1)
        zonal_parts, window_parts = [], []
        for row in range(ROWS):
            shift = bias[WIN + row : WIN + row + 1, :]
            if row == r:
                shift = jnp.where(eye, 0.0, shift)
            weights = jnp.exp2(scores_of(query, ks, row) * factor + shift)
            zonal_parts.append((weights * band[r * ROWS + row]).astype(jnp.bfloat16))
            if low <= row < high:
                window_parts.append((weights * masks[abs(row - r)]).astype(jnp.bfloat16))
        zonal = jnp.dot(jnp.concatenate(zonal_parts, axis=1), vs[...], preferred_element_type=jnp.float32)
        window_ref[r] = jnp.dot(
            jnp.concatenate(window_parts, axis=1),
            vs[low * COLS : high * COLS, :],
            preferred_element_type=jnp.float32,
        )
        zonal_ref[r] = (zonal[:, :HEAD_DIM] / zonal[:, HEAD_DIM : HEAD_DIM + 1]).astype(jnp.bfloat16)


def inner(ints, factor, band, usable, parts):
    return pl.pallas_call(
        inner_kernel,
        out_shape=[
            jax.ShapeDtypeStruct((ROWS, COLS, HEAD_DIM), jnp.bfloat16),
            jax.ShapeDtypeStruct((ROWS, COLS, 256), jnp.float32),
        ],
        in_specs=[SMEM] * 3 + [VMEM] * 5,
        out_specs=[VMEM] * 2,
        scratch_shapes=[
            pltpu.VMEM((ROWS * COLS, HEAD_DIM), jnp.bfloat16),
            pltpu.VMEM((ROWS * COLS, 256), jnp.bfloat16),
            pltpu.VMEM((WIN + 1, COLS, COLS), jnp.float32),
        ],
        compiler_params=pltpu.CompilerParams(vmem_limit_bytes=16 * MIB),
        cost_estimate=pl.CostEstimate(flops=10**7, bytes_accessed=10**5, transcendentals=0),
        name="inner",
    )(ints, factor, band, usable, *parts)


def outer_kernel(ints, factor_ref, usable, zonal_ref, window_ref, *refs):
    parts, edges, chunks, (ks, vs, masks, out) = refs[:4], refs[4:12], refs[12:20], refs[20:]
    factor = factor_ref[0]
    base, core, radius = ints[0], ints[1], ints[2]
    for side in range(2):
        start = 0
        for e, edge in enumerate(edges[4 * side : 4 * side + 4]):
            at = 2 * HEAD_DIM * (e // 2)
            for r in range(WIN):
                whole = edge[r][:, at : at + 2 * HEAD_DIM]
                put(ks, vs, (side * WIN + r) * COLS + start, whole[:, :HEAD_DIM], whole[:, HEAD_DIM:])
            start += edge.shape[1]
    fill_masks(masks, 0, base, base + 2, core, radius)
    fill_masks(masks, WIN + 1, base, base - 2, core, radius)
    above, below = shifts(usable, base + 2, core), shifts(usable, base - 2, core)
    for r in range(ROWS):
        query = query_of(parts, r)
        rows = range(r, WIN) if r < WIN else range(WIN, r + 1)
        window_parts = []
        for row in rows:
            gap = r + WIN - row if r < WIN else ROWS + row - WIN - r
            shift = above[row : row + 1, :] if r < WIN else below[row + ROWS : row + ROWS + 1, :]
            weights = jnp.exp2(scores_of(query, ks, row) * factor + shift)
            mask = masks[gap] if r < WIN else masks[WIN + 1 + gap]
            window_parts.append((weights * mask).astype(jnp.bfloat16))
        values = vs[rows[0] * COLS : (rows[-1] + 1) * COLS, :]
        window = window_ref[r] + jnp.dot(
            jnp.concatenate(window_parts, axis=1), values, preferred_element_type=jnp.float32
        )
        window = window[:, :HEAD_DIM] / window[:, HEAD_DIM : HEAD_DIM + 1]
        total = window + zonal_ref[r].astype(jnp.float32)
        out[:, :, :, r * HEAD_DIM : (r + 1) * HEAD_DIM] = total.reshape(2, 8, 8, HEAD_DIM)
    for k in range(8):
        chunks[k][0] = out[ints[3], ints[4 + k]].astype(jnp.bfloat16)
        chunks[k][1] = out[1 - ints[3], ints[12 + k]].astype(jnp.bfloat16)


def outer(ints, factor, usable, zonal, window, parts, edges):
    chunk = jax.ShapeDtypeStruct((2, 8, ROWS * HEAD_DIM), jnp.bfloat16)
    return pl.pallas_call(
        outer_kernel,
        out_shape=[chunk] * 8,
        in_specs=[SMEM, SMEM] + [VMEM] * 15,
        out_specs=[VMEM] * 8,
        scratch_shapes=[
            pltpu.VMEM((2 * WIN * COLS, HEAD_DIM), jnp.bfloat16),
            pltpu.VMEM((2 * WIN * COLS, 256), jnp.bfloat16),
            pltpu.VMEM((2 * WIN + 2, COLS, COLS), jnp.float32),
            pltpu.VMEM((2, 8, 8, ROWS * HEAD_DIM), jnp.float32),
        ],
        compiler_params=pltpu.CompilerParams(vmem_limit_bytes=16 * MIB),
        cost_estimate=pl.CostEstimate(
            flops=10**9, bytes_accessed=4 * MIB, transcendentals=10**6
        ),
        name="outer",
    )(ints, factor, usable, zonal, window, *parts, *edges)


def assemble_kernel(at, *refs):
    mains, got, out = refs[:8], refs[8], refs[9]
    width = ROWS * HEAD_DIM
    for k in range(8):
        out[0, :, pl.ds(pl.multiple_of(at[k] * width, 128), width)] = mains[k][0]
        out[0, :, pl.ds(pl.multiple_of(at[8 + k] * width, 128), width)] = got[k]


def assemble(at, mains, got):
    return pl.pallas_call(
        assemble_kernel,
        out_shape=jax.ShapeDtypeStruct((1, 8, LAT * ROWS * HEAD_DIM), jnp.bfloat16),
        in_specs=[SMEM] + [VMEM] * 9,
        out_specs=VMEM,
        compiler_params=pltpu.CompilerParams(vmem_limit_bytes=4 * MIB),
        cost_estimate=pl.CostEstimate(flops=0, bytes_accessed=MIB, transcendentals=0),
        name="assemble",
    )(at, *mains, got)


def body(tokens, w_qkv, key_mask, band_of_row, radius, qk_scale):
    y_lo, z, y_hi, x, core = (lax.axis_index(a) for a in AXES)
    sector = y_hi * 4 + x
    block = block_of(y_lo, y_hi, x)
    head = core * 8 + z
    model = tokens.shape[-1]

    wide = tokens.astype(jnp.float32)
    normed = wide * lax.rsqrt(jnp.mean(wide * wide, axis=-1, keepdims=True) + EPS)
    normed = jnp.transpose(normed.astype(jnp.bfloat16), (1, 0, 2)).reshape(64, model)
    first = lax.ppermute(normed, AXES, spread_perm())

    own = w_qkv[0]
    half = lax.dynamic_slice_in_dim(own, core * (model // 2), model // 2, 1)
    mine = lax.ppermute(half, "y_lo", SWAP)

    base = (z - 2 * block) & 7
    padded = jnp.pad(key_mask, ((0, 0), (WIN, WIN)))
    usable = lax.dynamic_slice_in_dim(padded, block * ROWS, KEY_ROWS, 1)
    usable = jnp.transpose(usable).astype(jnp.float32)
    ids = lax.dynamic_slice_in_dim(band_of_row, block * ROWS, ROWS, 0)
    band = (ids[:, None] == ids[None, :]).astype(jnp.float32).reshape(ROWS * ROWS)
    groups = [
        group_of(((sector ^ k) - base + 4 * side) & 7) for side in (y_lo, 1 - y_lo) for k in range(8)
    ]
    reach = lax.dynamic_index_in_dim(radius, head, keepdims=False)
    ints = jnp.stack([base, core, reach, core ^ y_lo] + groups).astype(jnp.int32)
    factor = lax.dynamic_slice_in_dim(qk_scale, head, 1, 0) / HEAD_DIM * LOG2E
    at = []
    for from_y_lo in (core, 1 - core):
        for k in range(8):
            source = sector ^ k
            at.append(block_of(from_y_lo, source >> 2, source & 3))
    at = jnp.stack(at).astype(jnp.int32)
    flags = jnp.stack([core == y_lo, core]).astype(jnp.int32)

    first, usable, band, ints, factor, at, flags = lax.optimization_barrier(
        (first, usable, band, ints, factor, at, flags)
    )

    up = [(i, (i + 1) % 8) for i in range(8)]
    down = [(i, (i - 1) % 8) for i in range(8)]
    shards = [[first[:32], first[32:]]] + [[None, None] for _ in range(7)]
    a, b = list(shards[0]), list(shards[0])
    for k in range(1, 5):
        for h in range(2):
            if k < 4 or h == 0:
                a[h] = shards[8 - k][h] = lax.ppermute(a[h], "z", up)
            if k < 4 or h == 1:
                b[h] = shards[k][h] = lax.ppermute(b[h], "z", down)
    tied = [(i, h) for i in (3, 5) for h in range(2)]
    mine, *values = lax.optimization_barrier((mine, *(shards[i][h] for i, h in tied)))
    for (i, h), value in zip(tied, values):
        shards[i][h] = value
    theirs = lax.ppermute(mine, "core", SWAP)

    ring = ("y_lo", "y_hi", "x")
    keeps, others, tops, bottoms = [], [], [], []
    for group, cost in (((0, 1, 2, 3, 6, 7), 2 * 10**10), ((4, 5), 10**8)):
        pieces = [shards[i][h] for i in group for h in range(2)]
        keep, send, top_rows, bottom_rows = project(flags, pieces, own, mine, theirs, cost)
        keeps.append(keep)
        tops.append(lax.ppermute(bottom_rows, ring, neighbour_perm(1)))
        bottoms.append(lax.ppermute(top_rows, ring, neighbour_perm(-1)))
        others.append(lax.ppermute(send, "core", SWAP))
    parts = keeps + others
    zonal, window = inner(ints, factor, band, usable, parts)
    edges = []
    for halo in (tops, bottoms):
        *halo, window = lax.optimization_barrier((*halo, window))
        edges += [*halo, *(lax.ppermute(part, "core", SWAP) for part in halo)]
    chunks = outer(ints, factor, usable, zonal, window, parts, edges)

    corners = ("y_lo", "y_hi", "x", "core")
    landed = [lax.ppermute(chunks[k], corners, return_perm(k)) for k in range(8)]
    give = jnp.stack([part[1] for part in landed])
    got = lax.ppermute(give, "core", SWAP)
    return assemble(at, landed, got)


def solution(mesh):
    wide = Mesh(mesh.devices.reshape(SIZES), AXES)
    lat, lon = ("y_lo", "z"), ("y_hi", "x", "core")
    in_specs = (P(lon, lat, None), P(lat, None, None), P(), P(), P(), P())
    out_specs = P(lat, lon, None)
    return jax.shard_map(body, mesh=wide, in_specs=in_specs, out_specs=out_specs, check_vma=False)
```

```python
import jax
import jax.numpy as jnp
from jax import lax
from jax.experimental import pallas as pl
from jax.experimental.pallas import tpu as pltpu
from jax.sharding import Mesh, PartitionSpec as P

HEAD_DIM = 160
QKV = 3 * HEAD_DIM
ROWS = 8
WIN = 4
COLS = 128
HALF = COLS // 2
KEY_ROWS = ROWS + 2 * WIN
EPS = 1e-06
BIG = 1e30
LOG2E = 1.4426950408889634
LAT, LON = 16, 16
AXES = ("y_lo", "z", "y_hi", "x", "core")
SIZES = (2, 8, 2, 4, 2)
NT = (((1,), (1,)), ((), ()))
MIB = 1024 * 1024
SMEM = pl.BlockSpec(memory_space=pltpu.SMEM)
VMEM = pl.BlockSpec(memory_space=pltpu.VMEM)


def place_of(block):
    y_lo, rest = block // 8, block % 8
    side, k = rest // 4, rest % 4
    return y_lo, side ^ y_lo, k if side == 0 else 3 - k


def block_of(y_lo, y_hi, x):
    side = y_hi ^ y_lo
    return y_lo * 8 + side * 4 + jnp.where(side == 0, x, 3 - x)


def flat(*pairs):
    index = 0
    for coordinate, size in pairs:
        index = index * size + coordinate
    return index


def spread_perm():
    pairs = []
    for y_lo in range(2):
        for z in range(8):
            _, to_y_hi, to_x = place_of(y_lo * 8 + z)
            for s in range(8):
                for core in range(2):
                    to_z = (s + 2 * z + 4 * core) % 8
                    source = flat((y_lo, 2), (z, 8), (s, 8), (core, 2))
                    target = flat((y_lo, 2), (to_z, 8), (to_y_hi, 2), (to_x, 4), (core, 2))
                    pairs.append((source, target))
    return pairs


def ring_perm():
    pairs = []
    for z in range(8):
        for core in range(2):
            there = (z + 1 - 2 * core) % 8
            pairs.append((flat((z, 8), (core, 2)), flat((there, 8), (core, 2))))
    return pairs


def neighbour_perm():
    pairs = []
    for block in range(16):
        for core in range(2):
            if 0 <= block + 1 - 2 * core < 16:
                here, there = place_of(block), place_of(block + 1 - 2 * core)
                source = flat((here[0], 2), (here[1], 2), (here[2], 4), (core, 2))
                target = flat((there[0], 2), (there[1], 2), (there[2], 4), (core, 2))
                pairs.append((source, target))
    return pairs


def return_perm(k):
    pairs = []
    for y_lo in range(2):
        for s in range(8):
            for core in range(2):
                source = flat((y_lo, 2), (s, 8), (core, 2))
                pairs.append((source, flat((core, 2), (s ^ k, 8), (y_lo, 2))))
    return pairs


SWAP = [(0, 1), (1, 0)]


def normalized(p):
    lane = lax.broadcasted_iota(jnp.int32, (1, QKV), 1)
    is_q = lane < HEAD_DIM
    is_k = (lane >= HEAD_DIM) & (lane < 2 * HEAD_DIM)
    squares = p * p
    q_mean = jnp.sum(jnp.where(is_q, squares, 0.0), axis=-1, keepdims=True) / HEAD_DIM
    k_mean = jnp.sum(jnp.where(is_k, squares, 0.0), axis=-1, keepdims=True) / HEAD_DIM
    scale = jnp.where(is_q, lax.rsqrt(q_mean + EPS), jnp.where(is_k, lax.rsqrt(k_mean + EPS), 1.0))
    groups = p.shape[0] // (8 * ROWS)
    p = (p * scale).reshape(groups, ROWS, 8, QKV)
    return [p[:, r].reshape(8 * groups, QKV).astype(jnp.bfloat16) for r in range(ROWS)]


def project_kernel(flags, *refs):
    pieces, (own, mine, theirs), (keep, send, edge, give, x_ref) = refs[:8], refs[8:11], refs[11:]
    for g, piece in enumerate(pieces):
        x_ref[64 * g : 64 * (g + 1), :] = piece[...]
    width = mine.shape[1]
    near = pl.ds(pl.multiple_of(flags[1] * width, width), width)
    far = pl.ds(pl.multiple_of((1 - flags[1]) * width, width), width)
    p = lax.dot_general(x_ref[...], own[...], NT, preferred_element_type=jnp.float32)
    own_rows = normalized(p)
    p = lax.dot_general(x_ref[:, near], mine[...], NT, preferred_element_type=jnp.float32)
    p += lax.dot_general(x_ref[:, far], theirs[...], NT, preferred_element_type=jnp.float32)
    other_rows = normalized(p)

    def store(first, second):
        for r in range(ROWS):
            keep[r] = first[r]
            send[r] = second[r]

    @pl.when(flags[0] == 1)
    def _():
        store(own_rows, other_rows)

    @pl.when(flags[0] != 1)
    def _():
        store(other_rows, own_rows)

    def store_edges(top, bottom):
        for r in range(ROWS):
            row = jnp.concatenate([keep[r][:, HEAD_DIM:], send[r][:, HEAD_DIM:]], axis=1)
            (top if r < WIN else bottom)[r % WIN] = row

    @pl.when(flags[1] == 0)
    def _():
        store_edges(give, edge)

    @pl.when(flags[1] != 0)
    def _():
        store_edges(edge, give)


def project(flags, pieces, own, mine, theirs):
    whole = jax.ShapeDtypeStruct((ROWS, HALF, QKV), jnp.bfloat16)
    part = jax.ShapeDtypeStruct((WIN, HALF, 4 * HEAD_DIM), jnp.bfloat16)
    return pl.pallas_call(
        project_kernel,
        out_shape=[whole, whole, part, part],
        in_specs=[SMEM] + [VMEM] * 11,
        out_specs=[VMEM] * 4,
        scratch_shapes=[pltpu.VMEM((512, own.shape[1]), jnp.bfloat16)],
        compiler_params=pltpu.CompilerParams(vmem_limit_bytes=20 * MIB),
        cost_estimate=pl.CostEstimate(
            flops=2 * 512 * 960 * 2560, bytes_accessed=8 * MIB, transcendentals=0
        ),
        name="project",
    )(flags, *pieces, own, mine, theirs)


def put(ks, vs, first, key, value):
    at = pl.ds(first, key.shape[0])
    ks[at, :] = key
    vs[at, :HEAD_DIM] = value
    is_one = lax.broadcasted_iota(jnp.int32, (key.shape[0], 256 - HEAD_DIM), 1) == 0
    vs[at, HEAD_DIM:] = jnp.where(is_one, 1.0, 0.0).astype(jnp.bfloat16)


def columns(base, core, shape, dim):
    at = lax.broadcasted_iota(jnp.int32, shape, dim)
    side = core ^ (at >> 6)
    g = (at >> 3) & 7
    j = (g + 1) >> 1
    ch = side ^ jnp.where(g == 0, 0, 1 - (g & 1))
    sector = (base + jnp.where(side == 1, j, -j) - 4 * ch) & 7
    return sector * 16 + ch * 8 + (at & 7)


def group_at(sector, ch, base, core):
    i = (sector - base + 4 * ch) & 7
    side = jnp.where((i & 3) == 0, ch, jnp.where(i < 4, 1, 0))
    j = jnp.minimum(i, 8 - i)
    g = jnp.where(i == 0, 0, 2 * j - jnp.where(ch == side, 1, 0))
    return 8 * (side ^ core) + g


def fill_masks(masks, first, query_base, key_base, core, radius):
    square = (COLS, COLS)
    gap = (columns(query_base, core, square, 0) - columns(key_base, core, square, 1) + radius) & (COLS - 1)
    near = jnp.where(gap <= 2 * radius, 1.0, 0.0)
    for d in range(WIN + 1):
        masks[first + d] = jnp.where(radius >= d, near, 0.0)


def shifts(usable, key_base, core):
    square = (COLS, COLS)
    there = lax.broadcasted_iota(jnp.int32, square, 0) == columns(key_base, core, square, 1)
    moved = jnp.dot(usable[...], jnp.where(there, 1.0, 0.0), preferred_element_type=jnp.float32)
    return jnp.where(moved > 0.5, 0.0, -BIG)


def query_of(parts, r):
    return jnp.concatenate([part[r][:, :HEAD_DIM] for part in parts], axis=0)


def scores_of(query, ks, row):
    keys = ks[row * COLS : (row + 1) * COLS, :]
    return lax.dot_general(query, keys, NT, preferred_element_type=jnp.float32)


def inner_kernel(ints, factor_ref, band, usable, *refs):
    parts, (zonal_ref, window_ref, ks, vs, masks) = refs[:2], refs[2:]
    factor = factor_ref[0]
    start = 0
    for part in parts:
        for r in range(ROWS):
            whole = part[r]
            put(ks, vs, r * COLS + start, whole[:, HEAD_DIM : 2 * HEAD_DIM], whole[:, 2 * HEAD_DIM :])
        start += part.shape[1]
    fill_masks(masks, 0, ints[0], ints[0], ints[1], ints[2])
    bias = shifts(usable, ints[0], ints[1])
    eye = lax.broadcasted_iota(jnp.int32, (COLS, COLS), 0) == lax.broadcasted_iota(jnp.int32, (COLS, COLS), 1)
    for r in range(ROWS):
        query = query_of(parts, r)
        low, high = max(0, r - WIN), min(ROWS, r + WIN + 1)
        zonal_parts, window_parts = [], []
        for row in range(ROWS):
            shift = bias[WIN + row : WIN + row + 1, :]
            if row == r:
                shift = jnp.where(eye, 0.0, shift)
            weights = jnp.exp2(scores_of(query, ks, row) * factor + shift)
            zonal_parts.append((weights * band[r * ROWS + row]).astype(jnp.bfloat16))
            if low <= row < high:
                window_parts.append((weights * masks[abs(row - r)]).astype(jnp.bfloat16))
        zonal = jnp.dot(jnp.concatenate(zonal_parts, axis=1), vs[...], preferred_element_type=jnp.float32)
        window_ref[r] = jnp.dot(
            jnp.concatenate(window_parts, axis=1),
            vs[low * COLS : high * COLS, :],
            preferred_element_type=jnp.float32,
        )
        zonal_ref[r] = (zonal[:, :HEAD_DIM] / zonal[:, HEAD_DIM : HEAD_DIM + 1]).astype(jnp.bfloat16)


def inner(ints, factor, band, usable, parts):
    return pl.pallas_call(
        inner_kernel,
        out_shape=[
            jax.ShapeDtypeStruct((ROWS, COLS, HEAD_DIM), jnp.bfloat16),
            jax.ShapeDtypeStruct((ROWS, COLS, 256), jnp.float32),
        ],
        in_specs=[SMEM] * 3 + [VMEM] * 3,
        out_specs=[VMEM] * 2,
        scratch_shapes=[
            pltpu.VMEM((ROWS * COLS, HEAD_DIM), jnp.bfloat16),
            pltpu.VMEM((ROWS * COLS, 256), jnp.bfloat16),
            pltpu.VMEM((WIN + 1, COLS, COLS), jnp.float32),
        ],
        compiler_params=pltpu.CompilerParams(vmem_limit_bytes=16 * MIB),
        cost_estimate=pl.CostEstimate(flops=10**7, bytes_accessed=10**5, transcendentals=0),
        name="inner",
    )(ints, factor, band, usable, *parts)


def outer_kernel(ints, factor_ref, usable, zonal_ref, window_ref, *refs):
    parts, (own, oth, far_own, far_oth), chunks, (ks, vs, masks, out) = refs[:2], refs[2:6], refs[6:14], refs[14:]
    factor = factor_ref[0]
    base, core, radius = ints[0], ints[1], ints[2]
    for edge, side, half, second in ((own, core, 0, 0), (oth, core, 1, 1), (far_own, 1 - core, 1, 1), (far_oth, 1 - core, 0, 0)):
        at = 2 * HEAD_DIM * second
        for r in range(WIN):
            whole = edge[r][:, at : at + 2 * HEAD_DIM]
            first = pl.multiple_of(side * (WIN * COLS) + r * COLS + half * HALF, HALF)
            put(ks, vs, first, whole[:, :HEAD_DIM], whole[:, HEAD_DIM:])
    fill_masks(masks, 0, base, base + 2, core, radius)
    fill_masks(masks, WIN + 1, base, base - 2, core, radius)
    above, below = shifts(usable, base + 2, core), shifts(usable, base - 2, core)
    for r in range(ROWS):
        query = query_of(parts, r)
        rows = range(r, WIN) if r < WIN else range(WIN, r + 1)
        window_parts = []
        for row in rows:
            gap = r + WIN - row if r < WIN else ROWS + row - WIN - r
            shift = above[row : row + 1, :] if r < WIN else below[row + ROWS : row + ROWS + 1, :]
            weights = jnp.exp2(scores_of(query, ks, row) * factor + shift)
            mask = masks[gap] if r < WIN else masks[WIN + 1 + gap]
            window_parts.append((weights * mask).astype(jnp.bfloat16))
        values = vs[rows[0] * COLS : (rows[-1] + 1) * COLS, :]
        window = window_ref[r] + jnp.dot(
            jnp.concatenate(window_parts, axis=1), values, preferred_element_type=jnp.float32
        )
        window = window[:, :HEAD_DIM] / window[:, HEAD_DIM : HEAD_DIM + 1]
        total = window + zonal_ref[r].astype(jnp.float32)
        out[:, :, r * HEAD_DIM : (r + 1) * HEAD_DIM] = total.reshape(16, 8, HEAD_DIM)
    for k in range(8):
        chunks[k][0] = out[ints[3 + k]].astype(jnp.bfloat16)
        chunks[k][1] = out[ints[11 + k]].astype(jnp.bfloat16)


def outer(ints, factor, usable, zonal, window, parts, edges):
    chunk = jax.ShapeDtypeStruct((2, 8, ROWS * HEAD_DIM), jnp.bfloat16)
    return pl.pallas_call(
        outer_kernel,
        out_shape=[chunk] * 8,
        in_specs=[SMEM, SMEM] + [VMEM] * 9,
        out_specs=[VMEM] * 8,
        scratch_shapes=[
            pltpu.VMEM((2 * WIN * COLS, HEAD_DIM), jnp.bfloat16),
            pltpu.VMEM((2 * WIN * COLS, 256), jnp.bfloat16),
            pltpu.VMEM((2 * WIN + 2, COLS, COLS), jnp.float32),
            pltpu.VMEM((16, 8, ROWS * HEAD_DIM), jnp.float32),
        ],
        compiler_params=pltpu.CompilerParams(vmem_limit_bytes=16 * MIB),
        cost_estimate=pl.CostEstimate(
            flops=10**9, bytes_accessed=4 * MIB, transcendentals=10**6
        ),
        name="outer",
    )(ints, factor, usable, zonal, window, *parts, *edges)


def assemble_kernel(at, *refs):
    mains, got, out = refs[:8], refs[8], refs[9]
    width = ROWS * HEAD_DIM
    for k in range(8):
        out[0, :, pl.ds(pl.multiple_of(at[k] * width, 128), width)] = mains[k][0]
        out[0, :, pl.ds(pl.multiple_of(at[8 + k] * width, 128), width)] = got[k]


def assemble(at, mains, got):
    return pl.pallas_call(
        assemble_kernel,
        out_shape=jax.ShapeDtypeStruct((1, 8, LAT * ROWS * HEAD_DIM), jnp.bfloat16),
        in_specs=[SMEM] + [VMEM] * 9,
        out_specs=VMEM,
        compiler_params=pltpu.CompilerParams(vmem_limit_bytes=4 * MIB),
        cost_estimate=pl.CostEstimate(flops=0, bytes_accessed=MIB, transcendentals=0),
        name="assemble",
    )(at, *mains, got)


def body(tokens, w_qkv, key_mask, band_of_row, radius, qk_scale):
    y_lo, z, y_hi, x, core = (lax.axis_index(a) for a in AXES)
    sector = y_hi * 4 + x
    block = block_of(y_lo, y_hi, x)
    head = core * 8 + z
    model = tokens.shape[-1]

    wide = tokens.astype(jnp.float32)
    normed = wide * lax.rsqrt(jnp.mean(wide * wide, axis=-1, keepdims=True) + EPS)
    normed = jnp.transpose(normed.astype(jnp.bfloat16), (1, 0, 2)).reshape(64, model)
    first = lax.ppermute(normed, AXES, spread_perm())

    own = w_qkv[0]
    half = lax.dynamic_slice_in_dim(own, core * (model // 2), model // 2, 1)
    mine = lax.ppermute(half, "y_lo", SWAP)

    base = (z - 2 * block) & 7
    padded = jnp.pad(key_mask, ((0, 0), (WIN, WIN)))
    usable = lax.dynamic_slice_in_dim(padded, block * ROWS, KEY_ROWS, 1)
    usable = jnp.transpose(usable).astype(jnp.float32)
    ids = lax.dynamic_slice_in_dim(band_of_row, block * ROWS, ROWS, 0)
    band = (ids[:, None] == ids[None, :]).astype(jnp.float32).reshape(ROWS * ROWS)
    groups = [
        group_at(sector ^ k, side, base, core) for side in (y_lo, 1 - y_lo) for k in range(8)
    ]
    reach = lax.dynamic_index_in_dim(radius, head, keepdims=False)
    ints = jnp.stack([base, core, reach] + groups).astype(jnp.int32)
    factor = lax.dynamic_slice_in_dim(qk_scale, head, 1, 0) / HEAD_DIM * LOG2E
    at = []
    for from_y_lo in (core, 1 - core):
        for k in range(8):
            source = sector ^ k
            at.append(block_of(from_y_lo, source >> 2, source & 3))
    at = jnp.stack(at).astype(jnp.int32)
    flags = jnp.stack([core == y_lo, core]).astype(jnp.int32)

    first, usable, band, ints, factor, at, flags = lax.optimization_barrier(
        (first, usable, band, ints, factor, at, flags)
    )

    a, b = first, lax.ppermute(first, "core", SWAP)
    pieces = [first]
    for k in range(1, 5):
        a = lax.ppermute(a, ("z", "core"), ring_perm())
        pieces.append(a)
        if k < 4:
            b = lax.ppermute(b, ("z", "core"), ring_perm())
            pieces.append(b)
    mine, *pieces[5:7] = lax.optimization_barrier((mine, *pieces[5:7]))
    theirs = lax.ppermute(mine, "core", SWAP)

    corners = ("y_lo", "y_hi", "x", "core")
    keep, send, edge, give = project(flags, pieces, own, mine, theirs)
    halo_own = lax.ppermute(edge, corners, neighbour_perm())
    halo_oth = lax.ppermute(lax.ppermute(give, "core", SWAP), corners, neighbour_perm())
    parts = keep, lax.ppermute(send, "core", SWAP)
    zonal, window = inner(ints, factor, band, usable, parts)
    halo_own, halo_oth, window = lax.optimization_barrier((halo_own, halo_oth, window))
    halos = [halo_own, halo_oth] + [lax.ppermute(halo, "core", SWAP) for halo in (halo_own, halo_oth)]
    chunks = outer(ints, factor, usable, zonal, window, parts, halos)

    landed = [lax.ppermute(chunks[k], corners, return_perm(k)) for k in range(8)]
    give = jnp.stack([part[1] for part in landed])
    got = lax.ppermute(give, "core", SWAP)
    return assemble(at, landed, got)


def solution(mesh):
    wide = Mesh(mesh.devices.reshape(SIZES), AXES)
    lat, lon = ("y_lo", "z"), ("y_hi", "x", "core")
    in_specs = (P(lon, lat, None), P(lat, None, None), P(), P(), P(), P())
    out_specs = P(lat, lon, None)
    return jax.shard_map(body, mesh=wide, in_specs=in_specs, out_specs=out_specs, check_vma=False)
```

```python
import jax
import jax.numpy as jnp
from jax import lax
from jax.experimental import pallas as pl
from jax.experimental.pallas import tpu as pltpu
from jax.sharding import Mesh, PartitionSpec as P

HEAD_DIM = 160
QKV = 3 * HEAD_DIM
ROWS = 8
WIN = 4
COLS = 128
HALF = COLS // 2
KEY_ROWS = ROWS + 2 * WIN
EPS = 1e-06
BIG = 1e30
LOG2E = 1.4426950408889634
LAT, LON = 16, 16
AXES = ("y_lo", "z", "y_hi", "x", "core")
SIZES = (2, 8, 2, 4, 2)
NT = (((1,), (1,)), ((), ()))
MIB = 1024 * 1024
SMEM = pl.BlockSpec(memory_space=pltpu.SMEM)
VMEM = pl.BlockSpec(memory_space=pltpu.VMEM)


def place_of(block):
    y_lo, rest = block // 8, block % 8
    side, k = rest // 4, rest % 4
    return y_lo, side ^ y_lo, k if side == 0 else 3 - k


def block_of(y_lo, y_hi, x):
    side = y_hi ^ y_lo
    return y_lo * 8 + side * 4 + jnp.where(side == 0, x, 3 - x)


def flat(*pairs):
    index = 0
    for coordinate, size in pairs:
        index = index * size + coordinate
    return index


def spread_perm():
    pairs = []
    for y_lo in range(2):
        for z in range(8):
            _, to_y_hi, to_x = place_of(y_lo * 8 + z)
            for s in range(8):
                for core in range(2):
                    to_z = (s + 2 * z + 4 * core) % 8
                    source = flat((y_lo, 2), (z, 8), (s, 8), (core, 2))
                    target = flat((y_lo, 2), (to_z, 8), (to_y_hi, 2), (to_x, 4), (core, 2))
                    pairs.append((source, target))
    return pairs


def ring_perm():
    pairs = []
    for z in range(8):
        for core in range(2):
            there = (z + 1 - 2 * core) % 8
            pairs.append((flat((z, 8), (core, 2)), flat((there, 8), (core, 2))))
    return pairs


def neighbour_perm():
    pairs = []
    for block in range(16):
        for core in range(2):
            if 0 <= block + 1 - 2 * core < 16:
                here, there = place_of(block), place_of(block + 1 - 2 * core)
                source = flat((here[0], 2), (here[1], 2), (here[2], 4), (core, 2))
                target = flat((there[0], 2), (there[1], 2), (there[2], 4), (core, 2))
                pairs.append((source, target))
    return pairs


def return_perm(k):
    pairs = []
    for y_lo in range(2):
        for y_hi in range(2):
            for core in range(2):
                source = flat((y_lo, 2), (y_hi, 2), (core, 2))
                pairs.append((source, flat((core, 2), (y_hi ^ k, 2), (y_lo, 2))))
    return pairs


SWAP = [(0, 1), (1, 0)]


def normalized(p):
    lane = lax.broadcasted_iota(jnp.int32, (1, QKV), 1)
    is_q = lane < HEAD_DIM
    is_k = (lane >= HEAD_DIM) & (lane < 2 * HEAD_DIM)
    squares = p * p
    q_mean = jnp.sum(jnp.where(is_q, squares, 0.0), axis=-1, keepdims=True) / HEAD_DIM
    k_mean = jnp.sum(jnp.where(is_k, squares, 0.0), axis=-1, keepdims=True) / HEAD_DIM
    scale = jnp.where(is_q, lax.rsqrt(q_mean + EPS), jnp.where(is_k, lax.rsqrt(k_mean + EPS), 1.0))
    groups = p.shape[0] // (8 * ROWS)
    p = (p * scale).reshape(groups, ROWS, 8, QKV)
    return [p[:, r].reshape(8 * groups, QKV).astype(jnp.bfloat16) for r in range(ROWS)]


def project_kernel(flags, *refs):
    pieces, (own, mine, theirs), (keep, send, edge, give, x_ref) = refs[:8], refs[8:11], refs[11:]
    for g, piece in enumerate(pieces):
        x_ref[64 * g : 64 * (g + 1), :] = piece[...]
    width = mine.shape[1]
    near = pl.ds(pl.multiple_of(flags[1] * width, width), width)
    far = pl.ds(pl.multiple_of((1 - flags[1]) * width, width), width)
    p = lax.dot_general(x_ref[...], own[...], NT, preferred_element_type=jnp.float32)
    own_rows = normalized(p)
    p = lax.dot_general(x_ref[:, near], mine[...], NT, preferred_element_type=jnp.float32)
    p += lax.dot_general(x_ref[:, far], theirs[...], NT, preferred_element_type=jnp.float32)
    other_rows = normalized(p)

    def store(first, second):
        for r in range(ROWS):
            keep[r] = first[r]
            send[r] = second[r]

    @pl.when(flags[0] == 1)
    def _():
        store(own_rows, other_rows)

    @pl.when(flags[0] != 1)
    def _():
        store(other_rows, own_rows)

    def store_edges(top, bottom):
        for r in range(ROWS):
            row = jnp.concatenate([keep[r][:, HEAD_DIM:], send[r][:, HEAD_DIM:]], axis=1)
            (top if r < WIN else bottom)[r % WIN] = row

    @pl.when(flags[1] == 0)
    def _():
        store_edges(give, edge)

    @pl.when(flags[1] != 0)
    def _():
        store_edges(edge, give)


def project(flags, pieces, own, mine, theirs):
    whole = jax.ShapeDtypeStruct((ROWS, HALF, QKV), jnp.bfloat16)
    part = jax.ShapeDtypeStruct((WIN, HALF, 4 * HEAD_DIM), jnp.bfloat16)
    return pl.pallas_call(
        project_kernel,
        out_shape=[whole, whole, part, part],
        in_specs=[SMEM] + [VMEM] * 11,
        out_specs=[VMEM] * 4,
        scratch_shapes=[pltpu.VMEM((512, own.shape[1]), jnp.bfloat16)],
        compiler_params=pltpu.CompilerParams(vmem_limit_bytes=20 * MIB),
        cost_estimate=pl.CostEstimate(
            flops=2 * 512 * 960 * 2560, bytes_accessed=8 * MIB, transcendentals=0
        ),
        name="project",
    )(flags, *pieces, own, mine, theirs)


def put(ks, vs, first, key, value):
    at = pl.ds(first, key.shape[0])
    ks[at, :] = key
    vs[at, :HEAD_DIM] = value
    is_one = lax.broadcasted_iota(jnp.int32, (key.shape[0], 256 - HEAD_DIM), 1) == 0
    vs[at, HEAD_DIM:] = jnp.where(is_one, 1.0, 0.0).astype(jnp.bfloat16)


def columns(base, core, shape, dim):
    at = lax.broadcasted_iota(jnp.int32, shape, dim)
    side = core ^ (at >> 6)
    g = (at >> 3) & 7
    j = (g + 1) >> 1
    ch = side ^ jnp.where(g == 0, 0, 1 - (g & 1))
    sector = (base + jnp.where(side == 1, j, -j) - 4 * ch) & 7
    return sector * 16 + ch * 8 + (at & 7)


def group_at(sector, ch, base, core):
    i = (sector - base + 4 * ch) & 7
    side = jnp.where((i & 3) == 0, ch, jnp.where(i < 4, 1, 0))
    j = jnp.minimum(i, 8 - i)
    g = jnp.where(i == 0, 0, 2 * j - jnp.where(ch == side, 1, 0))
    return 8 * (side ^ core) + g


def fill_masks(masks, first, query_base, key_base, core, radius):
    square = (COLS, COLS)
    gap = (columns(query_base, core, square, 0) - columns(key_base, core, square, 1) + radius) & (COLS - 1)
    near = jnp.where(gap <= 2 * radius, 1.0, 0.0)
    for d in range(WIN + 1):
        masks[first + d] = jnp.where(radius >= d, near, 0.0)


def shifts(usable, key_base, core):
    square = (COLS, COLS)
    there = lax.broadcasted_iota(jnp.int32, square, 0) == columns(key_base, core, square, 1)
    moved = jnp.dot(usable[...], jnp.where(there, 1.0, 0.0), preferred_element_type=jnp.float32)
    return jnp.where(moved > 0.5, 0.0, -BIG)


def query_of(parts, r):
    return jnp.concatenate([part[r][:, :HEAD_DIM] for part in parts], axis=0)


def scores_of(query, ks, row):
    keys = ks[row * COLS : (row + 1) * COLS, :]
    return lax.dot_general(query, keys, NT, preferred_element_type=jnp.float32)


def inner_kernel(ints, factor_ref, band, usable, *refs):
    parts, (zonal_ref, window_ref, ks, vs, masks) = refs[:2], refs[2:]
    factor = factor_ref[0]
    start = 0
    for part in parts:
        for r in range(ROWS):
            whole = part[r]
            put(ks, vs, r * COLS + start, whole[:, HEAD_DIM : 2 * HEAD_DIM], whole[:, 2 * HEAD_DIM :])
        start += part.shape[1]
    fill_masks(masks, 0, ints[0], ints[0], ints[1], ints[2])
    bias = shifts(usable, ints[0], ints[1])
    eye = lax.broadcasted_iota(jnp.int32, (COLS, COLS), 0) == lax.broadcasted_iota(jnp.int32, (COLS, COLS), 1)
    for r in range(ROWS):
        query = query_of(parts, r)
        low, high = max(0, r - WIN), min(ROWS, r + WIN + 1)
        zonal_parts, window_parts = [], []
        for row in range(ROWS):
            shift = bias[WIN + row : WIN + row + 1, :]
            if row == r:
                shift = jnp.where(eye, 0.0, shift)
            weights = jnp.exp2(scores_of(query, ks, row) * factor + shift)
            zonal_parts.append((weights * band[r * ROWS + row]).astype(jnp.bfloat16))
            if low <= row < high:
                window_parts.append((weights * masks[abs(row - r)]).astype(jnp.bfloat16))
        zonal = jnp.dot(jnp.concatenate(zonal_parts, axis=1), vs[...], preferred_element_type=jnp.float32)
        window_ref[r] = jnp.dot(
            jnp.concatenate(window_parts, axis=1),
            vs[low * COLS : high * COLS, :],
            preferred_element_type=jnp.float32,
        )
        zonal_ref[r] = (zonal[:, :HEAD_DIM] / zonal[:, HEAD_DIM : HEAD_DIM + 1]).astype(jnp.bfloat16)


def inner(ints, factor, band, usable, parts):
    return pl.pallas_call(
        inner_kernel,
        out_shape=[
            jax.ShapeDtypeStruct((ROWS, COLS, HEAD_DIM), jnp.bfloat16),
            jax.ShapeDtypeStruct((ROWS, COLS, 256), jnp.float32),
        ],
        in_specs=[SMEM] * 3 + [VMEM] * 3,
        out_specs=[VMEM] * 2,
        scratch_shapes=[
            pltpu.VMEM((ROWS * COLS, HEAD_DIM), jnp.bfloat16),
            pltpu.VMEM((ROWS * COLS, 256), jnp.bfloat16),
            pltpu.VMEM((WIN + 1, COLS, COLS), jnp.float32),
        ],
        compiler_params=pltpu.CompilerParams(vmem_limit_bytes=16 * MIB),
        cost_estimate=pl.CostEstimate(flops=10**7, bytes_accessed=10**5, transcendentals=0),
        name="inner",
    )(ints, factor, band, usable, *parts)


def outer_kernel(ints, factor_ref, usable, zonal_ref, window_ref, *refs):
    parts, (own, oth, far_own, far_oth), chunks, (ks, vs, masks, out) = refs[:2], refs[2:6], refs[6:8], refs[8:]
    factor = factor_ref[0]
    base, core, radius = ints[0], ints[1], ints[2]
    for edge, side, half, second in ((own, core, 0, 0), (oth, core, 1, 1), (far_own, 1 - core, 1, 1), (far_oth, 1 - core, 0, 0)):
        at = 2 * HEAD_DIM * second
        for r in range(WIN):
            whole = edge[r][:, at : at + 2 * HEAD_DIM]
            first = pl.multiple_of(side * (WIN * COLS) + r * COLS + half * HALF, HALF)
            put(ks, vs, first, whole[:, :HEAD_DIM], whole[:, HEAD_DIM:])
    fill_masks(masks, 0, base, base + 2, core, radius)
    fill_masks(masks, WIN + 1, base, base - 2, core, radius)
    above, below = shifts(usable, base + 2, core), shifts(usable, base - 2, core)
    for r in range(ROWS):
        query = query_of(parts, r)
        rows = range(r, WIN) if r < WIN else range(WIN, r + 1)
        window_parts = []
        for row in rows:
            gap = r + WIN - row if r < WIN else ROWS + row - WIN - r
            shift = above[row : row + 1, :] if r < WIN else below[row + ROWS : row + ROWS + 1, :]
            weights = jnp.exp2(scores_of(query, ks, row) * factor + shift)
            mask = masks[gap] if r < WIN else masks[WIN + 1 + gap]
            window_parts.append((weights * mask).astype(jnp.bfloat16))
        values = vs[rows[0] * COLS : (rows[-1] + 1) * COLS, :]
        window = window_ref[r] + jnp.dot(
            jnp.concatenate(window_parts, axis=1), values, preferred_element_type=jnp.float32
        )
        window = window[:, :HEAD_DIM] / window[:, HEAD_DIM : HEAD_DIM + 1]
        total = window + zonal_ref[r].astype(jnp.float32)
        out[:, :, r * HEAD_DIM : (r + 1) * HEAD_DIM] = total.reshape(16, 8, HEAD_DIM)
    for k in range(8):
        chunks[k // 4][k % 4, 0] = out[ints[3 + k]].astype(jnp.bfloat16)
        chunks[k // 4][k % 4, 1] = out[ints[11 + k]].astype(jnp.bfloat16)


def outer(ints, factor, usable, zonal, window, parts, edges):
    chunk = jax.ShapeDtypeStruct((4, 2, 8, ROWS * HEAD_DIM), jnp.bfloat16)
    return pl.pallas_call(
        outer_kernel,
        out_shape=[chunk] * 2,
        in_specs=[SMEM, SMEM] + [VMEM] * 9,
        out_specs=[VMEM] * 2,
        scratch_shapes=[
            pltpu.VMEM((2 * WIN * COLS, HEAD_DIM), jnp.bfloat16),
            pltpu.VMEM((2 * WIN * COLS, 256), jnp.bfloat16),
            pltpu.VMEM((2 * WIN + 2, COLS, COLS), jnp.float32),
            pltpu.VMEM((16, 8, ROWS * HEAD_DIM), jnp.float32),
        ],
        compiler_params=pltpu.CompilerParams(vmem_limit_bytes=16 * MIB),
        cost_estimate=pl.CostEstimate(
            flops=10**9, bytes_accessed=4 * MIB, transcendentals=10**6
        ),
        name="outer",
    )(ints, factor, usable, zonal, window, *parts, *edges)


def regroup_kernel(near, far, *parts):
    for k, part in enumerate(parts):
        part[0] = near[k + 1]
        part[1] = far[k + 1]


def regroup(near, far):
    part = jax.ShapeDtypeStruct((2, *near.shape[1:]), near.dtype)
    return pl.pallas_call(
        regroup_kernel,
        out_shape=[part] * 3,
        in_specs=[VMEM] * 2,
        out_specs=[VMEM] * 3,
        compiler_params=pltpu.CompilerParams(vmem_limit_bytes=4 * MIB),
        cost_estimate=pl.CostEstimate(flops=0, bytes_accessed=MIB, transcendentals=0),
        name="regroup",
    )(near, far)


def assemble_kernel(at, *refs):
    width, out = ROWS * HEAD_DIM, refs[10]
    for part in range(2):
        landed = refs[5 * part : 5 * part + 5]
        for k in range(8):
            kind, x = k // 4, k % 4
            value = landed[kind][0, part] if x == 0 else landed[x + 1][kind, part]
            out[0, :, pl.ds(pl.multiple_of(at[8 * part + k] * width, 128), width)] = value


def assemble(at, landed):
    return pl.pallas_call(
        assemble_kernel,
        out_shape=jax.ShapeDtypeStruct((1, 8, LAT * ROWS * HEAD_DIM), jnp.bfloat16),
        in_specs=[SMEM] + [VMEM] * 10,
        out_specs=VMEM,
        compiler_params=pltpu.CompilerParams(vmem_limit_bytes=4 * MIB),
        cost_estimate=pl.CostEstimate(flops=0, bytes_accessed=MIB, transcendentals=0),
        name="assemble",
    )(at, *landed)


def body(tokens, w_qkv, key_mask, band_of_row, radius, qk_scale):
    y_lo, z, y_hi, x, core = (lax.axis_index(a) for a in AXES)
    sector = y_hi * 4 + x
    block = block_of(y_lo, y_hi, x)
    head = core * 8 + z
    model = tokens.shape[-1]

    wide = tokens.astype(jnp.float32)
    normed = wide * lax.rsqrt(jnp.mean(wide * wide, axis=-1, keepdims=True) + EPS)
    normed = jnp.transpose(normed.astype(jnp.bfloat16), (1, 0, 2)).reshape(64, model)
    first = lax.ppermute(normed, AXES, spread_perm())

    own = w_qkv[0]
    half = lax.dynamic_slice_in_dim(own, core * (model // 2), model // 2, 1)
    mine = lax.ppermute(half, "y_lo", SWAP)

    base = (z - 2 * block) & 7
    padded = jnp.pad(key_mask, ((0, 0), (WIN, WIN)))
    usable = lax.dynamic_slice_in_dim(padded, block * ROWS, KEY_ROWS, 1)
    usable = jnp.transpose(usable).astype(jnp.float32)
    ids = lax.dynamic_slice_in_dim(band_of_row, block * ROWS, ROWS, 0)
    band = (ids[:, None] == ids[None, :]).astype(jnp.float32).reshape(ROWS * ROWS)
    groups = [
        group_at(sector ^ k, side, base, core) for side in (y_lo, 1 - y_lo) for k in range(8)
    ]
    reach = lax.dynamic_index_in_dim(radius, head, keepdims=False)
    ints = jnp.stack([base, core, reach] + groups).astype(jnp.int32)
    factor = lax.dynamic_slice_in_dim(qk_scale, head, 1, 0) / HEAD_DIM * LOG2E
    at = []
    for from_y_lo in (core, 1 - core):
        for k in range(8):
            source = sector ^ k
            at.append(block_of(from_y_lo, source >> 2, source & 3))
    at = jnp.stack(at).astype(jnp.int32)
    flags = jnp.stack([core == y_lo, core]).astype(jnp.int32)

    first, usable, band, ints, factor, at, flags = lax.optimization_barrier(
        (first, usable, band, ints, factor, at, flags)
    )

    a, b = first, lax.ppermute(first, "core", SWAP)
    pieces = [first]
    for k in range(1, 5):
        a = lax.ppermute(a, ("z", "core"), ring_perm())
        pieces.append(a)
        if k < 4:
            b = lax.ppermute(b, ("z", "core"), ring_perm())
            pieces.append(b)
    mine, *pieces[3:5] = lax.optimization_barrier((mine, *pieces[3:5]))
    theirs = lax.ppermute(mine, "core", SWAP)

    corners = ("y_lo", "y_hi", "x", "core")
    keep, send, edge, give = project(flags, pieces, own, mine, theirs)
    halo_own = lax.ppermute(edge, corners, neighbour_perm())
    halo_oth = lax.ppermute(lax.ppermute(give, "core", SWAP), corners, neighbour_perm())
    parts = keep, lax.ppermute(send, "core", SWAP)
    zonal, window = inner(ints, factor, band, usable, parts)
    halo_own, halo_oth, window = lax.optimization_barrier((halo_own, halo_oth, window))
    halos = [halo_own, halo_oth] + [lax.ppermute(halo, "core", SWAP) for halo in (halo_own, halo_oth)]
    chunks = outer(ints, factor, usable, zonal, window, parts, halos)

    near, far = (lax.ppermute(chunks[k], ("y_lo", "y_hi", "core"), return_perm(k)) for k in range(2))
    passed = regroup(near, far)
    along = [[(i, i ^ k) for i in range(4)] for k in range(1, 4)]
    landed = [near, far] + [lax.ppermute(part, "x", perm) for part, perm in zip(passed, along)]
    return assemble(at, landed + [lax.ppermute(part, "core", SWAP) for part in landed])


def solution(mesh):
    wide = Mesh(mesh.devices.reshape(SIZES), AXES)
    lat, lon = ("y_lo", "z"), ("y_hi", "x", "core")
    in_specs = (P(lon, lat, None), P(lat, None, None), P(), P(), P(), P())
    out_specs = P(lat, lon, None)
    return jax.shard_map(body, mesh=wide, in_specs=in_specs, out_specs=out_specs, check_vma=False)
```

```python
import jax
import jax.numpy as jnp
from jax import lax
from jax.experimental import pallas as pl
from jax.experimental.pallas import tpu as pltpu
from jax.sharding import Mesh, PartitionSpec as P

HEAD_DIM = 160
QKV = 3 * HEAD_DIM
ROWS = 8
WIN = 4
COLS = 128
HALF = COLS // 2
KEY_ROWS = ROWS + 2 * WIN
EPS = 1e-06
BIG = 1e30
LOG2E = 1.4426950408889634
LAT, LON = 16, 16
AXES = ("y_lo", "z", "y_hi", "x", "core")
SIZES = (2, 8, 2, 4, 2)
NT = (((1,), (1,)), ((), ()))
MIB = 1024 * 1024
SMEM = pl.BlockSpec(memory_space=pltpu.SMEM)
VMEM = pl.BlockSpec(memory_space=pltpu.VMEM)


def place_of(block):
    y_lo, rest = block // 8, block % 8
    side, k = rest // 4, rest % 4
    return y_lo, side ^ y_lo, k if side == 0 else 3 - k


def block_of(y_lo, y_hi, x):
    side = y_hi ^ y_lo
    return y_lo * 8 + side * 4 + jnp.where(side == 0, x, 3 - x)


def flat(*pairs):
    index = 0
    for coordinate, size in pairs:
        index = index * size + coordinate
    return index


def spread_perm():
    pairs = []
    for y_lo in range(2):
        for z in range(8):
            _, to_y_hi, to_x = place_of(y_lo * 8 + z)
            for s in range(8):
                for core in range(2):
                    to_z = (s + 2 * z + 4 * core) % 8
                    source = flat((y_lo, 2), (z, 8), (s, 8), (core, 2))
                    target = flat((y_lo, 2), (to_z, 8), (to_y_hi, 2), (to_x, 4), (core, 2))
                    pairs.append((source, target))
    return pairs


def ring_perm():
    pairs = []
    for z in range(8):
        for core in range(2):
            there = (z + 1 - 2 * core) % 8
            pairs.append((flat((z, 8), (core, 2)), flat((there, 8), (core, 2))))
    return pairs


def weight_perm():
    pairs = []
    for y in range(4):
        for core in range(2):
            there = (y + 1 - 2 * core) % 4
            source = flat((y % 2, 2), (y // 2, 2), (core, 2))
            pairs.append((source, flat((there % 2, 2), (there // 2, 2), (core, 2))))
    return pairs


def neighbour_perm():
    pairs = []
    for block in range(16):
        for core in range(2):
            if 0 <= block + 1 - 2 * core < 16:
                here, there = place_of(block), place_of(block + 1 - 2 * core)
                source = flat((here[0], 2), (here[1], 2), (here[2], 4), (core, 2))
                target = flat((there[0], 2), (there[1], 2), (there[2], 4), (core, 2))
                pairs.append((source, target))
    return pairs


def return_perm(k):
    pairs = []
    for y_lo in range(2):
        for y_hi in range(2):
            for core in range(2):
                source = flat((y_lo, 2), (y_hi, 2), (core, 2))
                pairs.append((source, flat((core, 2), (y_hi ^ k, 2), (y_lo, 2))))
    return pairs


SWAP = [(0, 1), (1, 0)]


def normalized(p):
    lane = lax.broadcasted_iota(jnp.int32, (1, QKV), 1)
    is_q = lane < HEAD_DIM
    is_k = (lane >= HEAD_DIM) & (lane < 2 * HEAD_DIM)
    squares = p * p
    q_mean = jnp.sum(jnp.where(is_q, squares, 0.0), axis=-1, keepdims=True) / HEAD_DIM
    k_mean = jnp.sum(jnp.where(is_k, squares, 0.0), axis=-1, keepdims=True) / HEAD_DIM
    scale = jnp.where(is_q, lax.rsqrt(q_mean + EPS), jnp.where(is_k, lax.rsqrt(k_mean + EPS), 1.0))
    groups = p.shape[0] // (8 * ROWS)
    p = (p * scale).reshape(groups, ROWS, 8, QKV)
    return [p[:, r].reshape(8 * groups, QKV).astype(jnp.bfloat16) for r in range(ROWS)]


def project_kernel(flags, *refs):
    pieces, (own, mine, theirs), (keep, send, edge, give, x_ref) = refs[:8], refs[8:11], refs[11:]
    for g, piece in enumerate(pieces):
        x_ref[64 * g : 64 * (g + 1), :] = piece[...]
    width = mine.shape[1]
    near = pl.ds(pl.multiple_of(flags[1] * width, width), width)
    far = pl.ds(pl.multiple_of((1 - flags[1]) * width, width), width)
    p = lax.dot_general(x_ref[...], own[...], NT, preferred_element_type=jnp.float32)
    own_rows = normalized(p)
    p = lax.dot_general(x_ref[:, near], mine[...], NT, preferred_element_type=jnp.float32)
    p += lax.dot_general(x_ref[:, far], theirs[...], NT, preferred_element_type=jnp.float32)
    other_rows = normalized(p)

    def store(first, second):
        for r in range(ROWS):
            keep[r] = first[r]
            send[r] = second[r]

    @pl.when(flags[0] == 1)
    def _():
        store(own_rows, other_rows)

    @pl.when(flags[0] != 1)
    def _():
        store(other_rows, own_rows)

    def store_edges(top, bottom):
        for r in range(ROWS):
            row = jnp.concatenate([keep[r][:, HEAD_DIM:], send[r][:, HEAD_DIM:]], axis=1)
            (top if r < WIN else bottom)[r % WIN] = row

    @pl.when(flags[1] == 0)
    def _():
        store_edges(give, edge)

    @pl.when(flags[1] != 0)
    def _():
        store_edges(edge, give)


def project(flags, pieces, own, mine, theirs):
    whole = jax.ShapeDtypeStruct((ROWS, HALF, QKV), jnp.bfloat16)
    part = jax.ShapeDtypeStruct((WIN, HALF, 4 * HEAD_DIM), jnp.bfloat16)
    return pl.pallas_call(
        project_kernel,
        out_shape=[whole, whole, part, part],
        in_specs=[SMEM] + [VMEM] * 11,
        out_specs=[VMEM] * 4,
        scratch_shapes=[pltpu.VMEM((512, own.shape[1]), jnp.bfloat16)],
        compiler_params=pltpu.CompilerParams(vmem_limit_bytes=20 * MIB),
        cost_estimate=pl.CostEstimate(
            flops=2 * 512 * 960 * 2560, bytes_accessed=8 * MIB, transcendentals=0
        ),
        name="project",
    )(flags, *pieces, own, mine, theirs)


def put(ks, vs, first, key, value):
    at = pl.ds(first, key.shape[0])
    ks[at, :] = key
    vs[at, :HEAD_DIM] = value
    is_one = lax.broadcasted_iota(jnp.int32, (key.shape[0], 256 - HEAD_DIM), 1) == 0
    vs[at, HEAD_DIM:] = jnp.where(is_one, 1.0, 0.0).astype(jnp.bfloat16)


def columns(base, core, shape, dim):
    at = lax.broadcasted_iota(jnp.int32, shape, dim)
    side = core ^ (at >> 6)
    g = (at >> 3) & 7
    j = (g + 1) >> 1
    ch = side ^ jnp.where(g == 0, 0, 1 - (g & 1))
    sector = (base + jnp.where(side == 1, j, -j) - 4 * ch) & 7
    return sector * 16 + ch * 8 + (at & 7)


def group_at(sector, ch, base, core):
    i = (sector - base + 4 * ch) & 7
    side = jnp.where((i & 3) == 0, ch, jnp.where(i < 4, 1, 0))
    j = jnp.minimum(i, 8 - i)
    g = jnp.where(i == 0, 0, 2 * j - jnp.where(ch == side, 1, 0))
    return 8 * (side ^ core) + g


def fill_masks(masks, first, query_base, key_base, core, radius):
    square = (COLS, COLS)
    gap = (columns(query_base, core, square, 0) - columns(key_base, core, square, 1) + radius) & (COLS - 1)
    near = jnp.where(gap <= 2 * radius, 1.0, 0.0)
    for d in range(WIN + 1):
        masks[first + d] = jnp.where(radius >= d, near, 0.0)


def shifts(usable, key_base, core):
    square = (COLS, COLS)
    there = lax.broadcasted_iota(jnp.int32, square, 0) == columns(key_base, core, square, 1)
    moved = jnp.dot(usable[...], jnp.where(there, 1.0, 0.0), preferred_element_type=jnp.float32)
    return jnp.where(moved > 0.5, 0.0, -BIG)


def query_of(parts, r):
    return jnp.concatenate([part[r][:, :HEAD_DIM] for part in parts], axis=0)


def scores_of(query, ks, row):
    keys = ks[row * COLS : (row + 1) * COLS, :]
    return lax.dot_general(query, keys, NT, preferred_element_type=jnp.float32)


def inner_kernel(ints, factor_ref, band, usable, *refs):
    parts, (zonal_ref, window_ref, masks_ref, shifts_ref, ks, vs, masks) = refs[:2], refs[2:]
    factor = factor_ref[0]
    start = 0
    for part in parts:
        for r in range(ROWS):
            whole = part[r]
            put(ks, vs, r * COLS + start, whole[:, HEAD_DIM : 2 * HEAD_DIM], whole[:, 2 * HEAD_DIM :])
        start += part.shape[1]
    base, core, radius = ints[0], ints[1], ints[2]
    fill_masks(masks, 0, base, base, core, radius)
    bias = shifts(usable, base, core)
    fill_masks(masks_ref, 0, base, base + 2, core, radius)
    fill_masks(masks_ref, WIN + 1, base, base - 2, core, radius)
    shifts_ref[0] = shifts(usable, base + 2, core)
    shifts_ref[1] = shifts(usable, base - 2, core)
    eye = lax.broadcasted_iota(jnp.int32, (COLS, COLS), 0) == lax.broadcasted_iota(jnp.int32, (COLS, COLS), 1)
    for r in range(ROWS):
        query = query_of(parts, r)
        low, high = max(0, r - WIN), min(ROWS, r + WIN + 1)
        zonal_parts, window_parts = [], []
        for row in range(ROWS):
            shift = bias[WIN + row : WIN + row + 1, :]
            if row == r:
                shift = jnp.where(eye, 0.0, shift)
            weights = jnp.exp2(scores_of(query, ks, row) * factor + shift)
            zonal_parts.append((weights * band[r * ROWS + row]).astype(jnp.bfloat16))
            if low <= row < high:
                window_parts.append((weights * masks[abs(row - r)]).astype(jnp.bfloat16))
        zonal = jnp.dot(jnp.concatenate(zonal_parts, axis=1), vs[...], preferred_element_type=jnp.float32)
        window_ref[r] = jnp.dot(
            jnp.concatenate(window_parts, axis=1),
            vs[low * COLS : high * COLS, :],
            preferred_element_type=jnp.float32,
        )
        zonal_ref[r] = (zonal[:, :HEAD_DIM] / zonal[:, HEAD_DIM : HEAD_DIM + 1]).astype(jnp.bfloat16)


def inner(ints, factor, band, usable, parts):
    return pl.pallas_call(
        inner_kernel,
        out_shape=[
            jax.ShapeDtypeStruct((ROWS, COLS, HEAD_DIM), jnp.bfloat16),
            jax.ShapeDtypeStruct((ROWS, COLS, 256), jnp.float32),
            jax.ShapeDtypeStruct((2 * WIN + 2, COLS, COLS), jnp.float32),
            jax.ShapeDtypeStruct((2, KEY_ROWS, COLS), jnp.float32),
        ],
        in_specs=[SMEM] * 3 + [VMEM] * 3,
        out_specs=[VMEM] * 4,
        scratch_shapes=[
            pltpu.VMEM((ROWS * COLS, HEAD_DIM), jnp.bfloat16),
            pltpu.VMEM((ROWS * COLS, 256), jnp.bfloat16),
            pltpu.VMEM((WIN + 1, COLS, COLS), jnp.float32),
        ],
        compiler_params=pltpu.CompilerParams(vmem_limit_bytes=16 * MIB),
        cost_estimate=pl.CostEstimate(flops=10**7, bytes_accessed=10**5, transcendentals=0),
        name="inner",
    )(ints, factor, band, usable, *parts)


def outer_kernel(ints, factor_ref, zonal_ref, window_ref, masks, shifts_ref, *refs):
    parts, (own, oth, far_own, far_oth), chunks, (ks, vs, out) = refs[:2], refs[2:6], refs[6:8], refs[8:]
    factor = factor_ref[0]
    core = ints[1]
    for edge, side, half, second in ((own, core, 0, 0), (oth, core, 1, 1), (far_own, 1 - core, 1, 1), (far_oth, 1 - core, 0, 0)):
        at = 2 * HEAD_DIM * second
        for r in range(WIN):
            whole = edge[r][:, at : at + 2 * HEAD_DIM]
            first = pl.multiple_of(side * (WIN * COLS) + r * COLS + half * HALF, HALF)
            put(ks, vs, first, whole[:, :HEAD_DIM], whole[:, HEAD_DIM:])
    above, below = shifts_ref[0], shifts_ref[1]
    for r in range(ROWS):
        query = query_of(parts, r)
        rows = range(r, WIN) if r < WIN else range(WIN, r + 1)
        window_parts = []
        for row in rows:
            gap = r + WIN - row if r < WIN else ROWS + row - WIN - r
            shift = above[row : row + 1, :] if r < WIN else below[row + ROWS : row + ROWS + 1, :]
            weights = jnp.exp2(scores_of(query, ks, row) * factor + shift)
            mask = masks[gap] if r < WIN else masks[WIN + 1 + gap]
            window_parts.append((weights * mask).astype(jnp.bfloat16))
        values = vs[rows[0] * COLS : (rows[-1] + 1) * COLS, :]
        window = window_ref[r] + jnp.dot(
            jnp.concatenate(window_parts, axis=1), values, preferred_element_type=jnp.float32
        )
        window = window[:, :HEAD_DIM] / window[:, HEAD_DIM : HEAD_DIM + 1]
        total = window + zonal_ref[r].astype(jnp.float32)
        out[:, :, r * HEAD_DIM : (r + 1) * HEAD_DIM] = total.reshape(16, 8, HEAD_DIM)
    for k in range(8):
        chunks[k // 4][k % 4, 0] = out[ints[3 + k]].astype(jnp.bfloat16)
        chunks[k // 4][k % 4, 1] = out[ints[11 + k]].astype(jnp.bfloat16)


def outer(ints, factor, inner_results, parts, edges):
    chunk = jax.ShapeDtypeStruct((4, 2, 8, ROWS * HEAD_DIM), jnp.bfloat16)
    return pl.pallas_call(
        outer_kernel,
        out_shape=[chunk] * 2,
        in_specs=[SMEM, SMEM] + [VMEM] * 10,
        out_specs=[VMEM] * 2,
        scratch_shapes=[
            pltpu.VMEM((2 * WIN * COLS, HEAD_DIM), jnp.bfloat16),
            pltpu.VMEM((2 * WIN * COLS, 256), jnp.bfloat16),
            pltpu.VMEM((16, 8, ROWS * HEAD_DIM), jnp.float32),
        ],
        compiler_params=pltpu.CompilerParams(vmem_limit_bytes=16 * MIB),
        cost_estimate=pl.CostEstimate(
            flops=10**9, bytes_accessed=4 * MIB, transcendentals=10**6
        ),
        name="outer",
    )(ints, factor, *inner_results, *parts, *edges)


def regroup_kernel(near, far, *parts):
    for k, part in enumerate(parts):
        part[0] = near[k + 1]
        part[1] = far[k + 1]


def regroup(near, far):
    part = jax.ShapeDtypeStruct((2, *near.shape[1:]), near.dtype)
    return pl.pallas_call(
        regroup_kernel,
        out_shape=[part] * 3,
        in_specs=[VMEM] * 2,
        out_specs=[VMEM] * 3,
        compiler_params=pltpu.CompilerParams(vmem_limit_bytes=4 * MIB),
        cost_estimate=pl.CostEstimate(flops=0, bytes_accessed=MIB, transcendentals=0),
        name="regroup",
    )(near, far)


def assemble_kernel(at, *refs):
    width, out = ROWS * HEAD_DIM, refs[10]
    for part in range(2):
        landed = refs[5 * part : 5 * part + 5]
        for k in range(8):
            kind, x = k // 4, k % 4
            value = landed[kind][0, part] if x == 0 else landed[x + 1][kind, part]
            out[0, :, pl.ds(pl.multiple_of(at[8 * part + k] * width, 128), width)] = value


def assemble(at, landed):
    return pl.pallas_call(
        assemble_kernel,
        out_shape=jax.ShapeDtypeStruct((1, 8, LAT * ROWS * HEAD_DIM), jnp.bfloat16),
        in_specs=[SMEM] + [VMEM] * 10,
        out_specs=VMEM,
        compiler_params=pltpu.CompilerParams(vmem_limit_bytes=4 * MIB),
        cost_estimate=pl.CostEstimate(flops=0, bytes_accessed=MIB, transcendentals=0),
        name="assemble",
    )(at, *landed)


def body(tokens, w_qkv, key_mask, band_of_row, radius, qk_scale):
    y_lo, z, y_hi, x, core = (lax.axis_index(a) for a in AXES)
    sector = y_hi * 4 + x
    block = block_of(y_lo, y_hi, x)
    head = core * 8 + z
    model = tokens.shape[-1]

    wide = tokens.astype(jnp.float32)
    normed = wide * lax.rsqrt(jnp.mean(wide * wide, axis=-1, keepdims=True) + EPS)
    normed = jnp.transpose(normed.astype(jnp.bfloat16), (1, 0, 2)).reshape(64, model)
    first = lax.ppermute(normed, AXES, spread_perm())

    own = w_qkv[0]
    half = lax.dynamic_slice_in_dim(own, core * (model // 2), model // 2, 1)
    mine = lax.ppermute(half, ("y_lo", "y_hi", "core"), weight_perm())

    base = (z - 2 * block) & 7
    padded = jnp.pad(key_mask, ((0, 0), (WIN, WIN)))
    usable = lax.dynamic_slice_in_dim(padded, block * ROWS, KEY_ROWS, 1)
    usable = jnp.transpose(usable).astype(jnp.float32)
    ids = lax.dynamic_slice_in_dim(band_of_row, block * ROWS, ROWS, 0)
    band = (ids[:, None] == ids[None, :]).astype(jnp.float32).reshape(ROWS * ROWS)
    groups = [
        group_at(sector ^ k, side, base, core) for side in (y_lo, 1 - y_lo) for k in range(8)
    ]
    reach = lax.dynamic_index_in_dim(radius, head, keepdims=False)
    ints = jnp.stack([base, core, reach] + groups).astype(jnp.int32)
    factor = lax.dynamic_slice_in_dim(qk_scale, head, 1, 0) / HEAD_DIM * LOG2E
    at = []
    for from_y_lo in (core, 1 - core):
        for k in range(8):
            source = sector ^ k
            at.append(block_of(from_y_lo, source >> 2, source & 3))
    at = jnp.stack(at).astype(jnp.int32)
    flags = jnp.stack([core == y_lo, core]).astype(jnp.int32)

    first, usable, band, ints, factor, at, flags = lax.optimization_barrier(
        (first, usable, band, ints, factor, at, flags)
    )

    a, b = first, lax.ppermute(first, "core", SWAP)
    pieces = [first]
    for k in range(1, 5):
        a = lax.ppermute(a, ("z", "core"), ring_perm())
        pieces.append(a)
        if k < 4:
            b = lax.ppermute(b, ("z", "core"), ring_perm())
            pieces.append(b)
    mine, *pieces[5:7] = lax.optimization_barrier((mine, *pieces[5:7]))
    theirs = lax.ppermute(mine, "core", SWAP)

    corners = ("y_lo", "y_hi", "x", "core")
    keep, send, edge, give = project(flags, pieces, own, mine, theirs)
    halo_own = lax.ppermute(edge, corners, neighbour_perm())
    halo_oth = lax.ppermute(lax.ppermute(give, "core", SWAP), corners, neighbour_perm())
    parts = keep, lax.ppermute(send, "core", SWAP)
    results = inner(ints, factor, band, usable, parts)
    halo_own, halo_oth, *results = lax.optimization_barrier((halo_own, halo_oth, *results))
    halos = [halo_own, halo_oth] + [lax.ppermute(halo, "core", SWAP) for halo in (halo_own, halo_oth)]
    chunks = outer(ints, factor, results, parts, halos)

    near, far = (lax.ppermute(chunks[k], ("y_lo", "y_hi", "core"), return_perm(k)) for k in range(2))
    passed = regroup(near, far)
    along = [[(i, i ^ k) for i in range(4)] for k in range(1, 4)]
    landed = [near, far] + [lax.ppermute(part, "x", perm) for part, perm in zip(passed, along)]
    return assemble(at, landed + [lax.ppermute(part, "core", SWAP) for part in landed])


def solution(mesh):
    wide = Mesh(mesh.devices.reshape(SIZES), AXES)
    lat, lon = ("y_lo", "z"), ("y_hi", "x", "core")
    in_specs = (P(lon, lat, None), P(lat, None, None), P(), P(), P(), P())
    out_specs = P(lat, lon, None)
    return jax.shard_map(body, mesh=wide, in_specs=in_specs, out_specs=out_specs, check_vma=False)
```

```python
import jax
import jax.numpy as jnp
from jax import lax
from jax.experimental import pallas as pl
from jax.experimental.pallas import tpu as pltpu
from jax.sharding import Mesh, PartitionSpec as P

HEAD_DIM = 160
QKV = 3 * HEAD_DIM
ROWS = 8
WIN = 4
COLS = 128
HALF = COLS // 2
KEY_ROWS = ROWS + 2 * WIN
EPS = 1e-06
BIG = 1e30
LOG2E = 1.4426950408889634
LAT, LON = 16, 16
AXES = ("y_lo", "z", "y_hi", "x", "core")
SIZES = (2, 8, 2, 4, 2)
NT = (((1,), (1,)), ((), ()))
MIB = 1024 * 1024
SMEM = pl.BlockSpec(memory_space=pltpu.SMEM)
VMEM = pl.BlockSpec(memory_space=pltpu.VMEM)


def place_of(block):
    y_lo, rest = block // 8, block % 8
    side, k = rest // 4, rest % 4
    return y_lo, side ^ y_lo, k if side == 0 else 3 - k


def block_of(y_lo, y_hi, x):
    side = y_hi ^ y_lo
    return y_lo * 8 + side * 4 + jnp.where(side == 0, x, 3 - x)


def flat(*pairs):
    index = 0
    for coordinate, size in pairs:
        index = index * size + coordinate
    return index


def spread_perm():
    pairs = []
    for y_lo in range(2):
        for z in range(8):
            _, to_y_hi, to_x = place_of(y_lo * 8 + z)
            for s in range(8):
                for core in range(2):
                    to_z = (s + 2 * z + 4 * core) % 8
                    source = flat((y_lo, 2), (z, 8), (s, 8), (core, 2))
                    target = flat((y_lo, 2), (to_z, 8), (to_y_hi, 2), (to_x, 4), (core, 2))
                    pairs.append((source, target))
    return pairs


def ring_perm(cross=0):
    pairs = []
    for z in range(8):
        for core in range(2):
            there = (z + 1 - 2 * core) % 8
            pairs.append((flat((z, 8), (core ^ cross, 2)), flat((there, 8), (core, 2))))
    return pairs


def weight_perm():
    pairs = []
    for y in range(4):
        for core in range(2):
            there = (y + 1 - 2 * core) % 4
            source = flat((y % 2, 2), (y // 2, 2), (core, 2))
            pairs.append((source, flat((there % 2, 2), (there // 2, 2), (core, 2))))
    return pairs


def neighbour_perm():
    pairs = []
    for block in range(16):
        for core in range(2):
            if 0 <= block + 1 - 2 * core < 16:
                here, there = place_of(block), place_of(block + 1 - 2 * core)
                source = flat((here[0], 2), (here[1], 2), (here[2], 4), (core, 2))
                target = flat((there[0], 2), (there[1], 2), (there[2], 4), (core, 2))
                pairs.append((source, target))
    return pairs


def return_perm(k):
    pairs = []
    for y_lo in range(2):
        for y_hi in range(2):
            for core in range(2):
                source = flat((y_lo, 2), (y_hi, 2), (core, 2))
                pairs.append((source, flat((core, 2), (y_hi ^ k, 2), (y_lo, 2))))
    return pairs


SWAP = [(0, 1), (1, 0)]


def normalized(p):
    lane = lax.broadcasted_iota(jnp.int32, (1, QKV), 1)
    is_q = lane < HEAD_DIM
    is_k = (lane >= HEAD_DIM) & (lane < 2 * HEAD_DIM)
    squares = p * p
    q_mean = jnp.sum(jnp.where(is_q, squares, 0.0), axis=-1, keepdims=True) / HEAD_DIM
    k_mean = jnp.sum(jnp.where(is_k, squares, 0.0), axis=-1, keepdims=True) / HEAD_DIM
    scale = jnp.where(is_q, lax.rsqrt(q_mean + EPS), jnp.where(is_k, lax.rsqrt(k_mean + EPS), 1.0))
    groups = p.shape[0] // (8 * ROWS)
    p = (p * scale).reshape(groups, ROWS, 8, QKV)
    return [p[:, r].reshape(8 * groups, QKV).astype(jnp.bfloat16) for r in range(ROWS)]


def project_kernel(flags, *refs):
    pieces, (own, partner), (keep, send, edge, give, x_ref) = refs[:8], refs[8:10], refs[10:]
    for g, piece in enumerate(pieces):
        x_ref[64 * g : 64 * (g + 1), :] = piece[...]
    p = lax.dot_general(x_ref[...], own[...], NT, preferred_element_type=jnp.float32)
    own_rows = normalized(p)
    p = lax.dot_general(x_ref[...], partner[...], NT, preferred_element_type=jnp.float32)
    other_rows = normalized(p)

    def store(first, second):
        for r in range(ROWS):
            keep[r] = first[r]
            send[r] = second[r]

    @pl.when(flags[0] == 1)
    def _():
        store(own_rows, other_rows)

    @pl.when(flags[0] != 1)
    def _():
        store(other_rows, own_rows)

    def store_edges(top, bottom):
        for r in range(ROWS):
            row = jnp.concatenate([keep[r][:, HEAD_DIM:], send[r][:, HEAD_DIM:]], axis=1)
            (top if r < WIN else bottom)[r % WIN] = row

    @pl.when(flags[1] == 0)
    def _():
        store_edges(give, edge)

    @pl.when(flags[1] != 0)
    def _():
        store_edges(edge, give)


def project(flags, pieces, own, partner):
    whole = jax.ShapeDtypeStruct((ROWS, HALF, QKV), jnp.bfloat16)
    part = jax.ShapeDtypeStruct((WIN, HALF, 4 * HEAD_DIM), jnp.bfloat16)
    return pl.pallas_call(
        project_kernel,
        out_shape=[whole, whole, part, part],
        in_specs=[SMEM] + [VMEM] * 10,
        out_specs=[VMEM] * 4,
        scratch_shapes=[pltpu.VMEM((512, own.shape[1]), jnp.bfloat16)],
        compiler_params=pltpu.CompilerParams(vmem_limit_bytes=20 * MIB),
        cost_estimate=pl.CostEstimate(
            flops=2 * 512 * 960 * 2560, bytes_accessed=8 * MIB, transcendentals=0
        ),
        name="project",
    )(flags, *pieces, own, partner)


def put(ks, vs, first, key, value):
    at = pl.ds(first, key.shape[0])
    ks[at, :] = key
    vs[at, :HEAD_DIM] = value
    is_one = lax.broadcasted_iota(jnp.int32, (key.shape[0], 256 - HEAD_DIM), 1) == 0
    vs[at, HEAD_DIM:] = jnp.where(is_one, 1.0, 0.0).astype(jnp.bfloat16)


def columns(base, core, shape, dim):
    at = lax.broadcasted_iota(jnp.int32, shape, dim)
    side = core ^ (at >> 6)
    g = (at >> 3) & 7
    j = (g + 1) >> 1
    ch = side ^ jnp.where(g == 0, 0, 1 - (g & 1))
    sector = (base + jnp.where(side == 1, j, -j) - 4 * ch) & 7
    return sector * 16 + ch * 8 + (at & 7)


def group_at(sector, ch, base, core):
    i = (sector - base + 4 * ch) & 7
    side = jnp.where((i & 3) == 0, ch, jnp.where(i < 4, 1, 0))
    j = jnp.minimum(i, 8 - i)
    g = jnp.where(i == 0, 0, 2 * j - jnp.where(ch == side, 1, 0))
    return 8 * (side ^ core) + g


def fill_masks(masks, first, query_base, key_base, core, radius):
    square = (COLS, COLS)
    gap = (columns(query_base, core, square, 0) - columns(key_base, core, square, 1) + radius) & (COLS - 1)
    near = jnp.where(gap <= 2 * radius, 1.0, 0.0)
    for d in range(WIN + 1):
        masks[first + d] = jnp.where(radius >= d, near, 0.0)


def shifts(usable, key_base, core):
    square = (COLS, COLS)
    there = lax.broadcasted_iota(jnp.int32, square, 0) == columns(key_base, core, square, 1)
    moved = jnp.dot(usable[...], jnp.where(there, 1.0, 0.0), preferred_element_type=jnp.float32)
    return jnp.where(moved > 0.5, 0.0, -BIG)


def query_of(parts, r):
    return jnp.concatenate([part[r][:, :HEAD_DIM] for part in parts], axis=0)


def scores_of(query, ks, row):
    keys = ks[row * COLS : (row + 1) * COLS, :]
    return lax.dot_general(query, keys, NT, preferred_element_type=jnp.float32)


def inner_kernel(ints, factor_ref, band, usable, *refs):
    parts, (zonal_ref, window_ref, masks_ref, shifts_ref, ks, vs, masks) = refs[:2], refs[2:]
    factor = factor_ref[0]
    start = 0
    for part in parts:
        for r in range(ROWS):
            whole = part[r]
            put(ks, vs, r * COLS + start, whole[:, HEAD_DIM : 2 * HEAD_DIM], whole[:, 2 * HEAD_DIM :])
        start += part.shape[1]
    base, core, radius = ints[0], ints[1], ints[2]
    fill_masks(masks, 0, base, base, core, radius)
    bias = shifts(usable, base, core)
    fill_masks(masks_ref, 0, base, base + 2, core, radius)
    fill_masks(masks_ref, WIN + 1, base, base - 2, core, radius)
    shifts_ref[0] = shifts(usable, base + 2, core)
    shifts_ref[1] = shifts(usable, base - 2, core)
    eye = lax.broadcasted_iota(jnp.int32, (COLS, COLS), 0) == lax.broadcasted_iota(jnp.int32, (COLS, COLS), 1)
    for r in range(ROWS):
        query = query_of(parts, r)
        low, high = max(0, r - WIN), min(ROWS, r + WIN + 1)
        zonal_parts, window_parts = [], []
        for row in range(ROWS):
            shift = bias[WIN + row : WIN + row + 1, :]
            if row == r:
                shift = jnp.where(eye, 0.0, shift)
            weights = jnp.exp2(scores_of(query, ks, row) * factor + shift)
            zonal_parts.append((weights * band[r * ROWS + row]).astype(jnp.bfloat16))
            if low <= row < high:
                window_parts.append((weights * masks[abs(row - r)]).astype(jnp.bfloat16))
        zonal = jnp.dot(jnp.concatenate(zonal_parts, axis=1), vs[...], preferred_element_type=jnp.float32)
        window_ref[r] = jnp.dot(
            jnp.concatenate(window_parts, axis=1),
            vs[low * COLS : high * COLS, :],
            preferred_element_type=jnp.float32,
        )
        zonal_ref[r] = (zonal[:, :HEAD_DIM] / zonal[:, HEAD_DIM : HEAD_DIM + 1]).astype(jnp.bfloat16)


def inner(ints, factor, band, usable, parts):
    return pl.pallas_call(
        inner_kernel,
        out_shape=[
            jax.ShapeDtypeStruct((ROWS, COLS, HEAD_DIM), jnp.bfloat16),
            jax.ShapeDtypeStruct((ROWS, COLS, 256), jnp.float32),
            jax.ShapeDtypeStruct((2 * WIN + 2, COLS, COLS), jnp.float32),
            jax.ShapeDtypeStruct((2, KEY_ROWS, COLS), jnp.float32),
        ],
        in_specs=[SMEM] * 3 + [VMEM] * 3,
        out_specs=[VMEM] * 4,
        scratch_shapes=[
            pltpu.VMEM((ROWS * COLS, HEAD_DIM), jnp.bfloat16),
            pltpu.VMEM((ROWS * COLS, 256), jnp.bfloat16),
            pltpu.VMEM((WIN + 1, COLS, COLS), jnp.float32),
        ],
        compiler_params=pltpu.CompilerParams(vmem_limit_bytes=16 * MIB),
        cost_estimate=pl.CostEstimate(flops=10**7, bytes_accessed=10**5, transcendentals=0),
        name="inner",
    )(ints, factor, band, usable, *parts)


def outer_kernel(ints, factor_ref, zonal_ref, window_ref, masks, shifts_ref, *refs):
    parts, (own, oth, far_own, far_oth), chunks, (ks, vs, out) = refs[:2], refs[2:6], refs[6:8], refs[8:]
    factor = factor_ref[0]
    core = ints[1]
    for edge, side, half, second in ((own, core, 0, 0), (oth, core, 1, 1), (far_own, 1 - core, 1, 1), (far_oth, 1 - core, 0, 0)):
        at = 2 * HEAD_DIM * second
        for r in range(WIN):
            whole = edge[r][:, at : at + 2 * HEAD_DIM]
            first = pl.multiple_of(side * (WIN * COLS) + r * COLS + half * HALF, HALF)
            put(ks, vs, first, whole[:, :HEAD_DIM], whole[:, HEAD_DIM:])
    above, below = shifts_ref[0], shifts_ref[1]
    for r in range(ROWS):
        query = query_of(parts, r)
        rows = range(r, WIN) if r < WIN else range(WIN, r + 1)
        window_parts = []
        for row in rows:
            gap = r + WIN - row if r < WIN else ROWS + row - WIN - r
            shift = above[row : row + 1, :] if r < WIN else below[row + ROWS : row + ROWS + 1, :]
            weights = jnp.exp2(scores_of(query, ks, row) * factor + shift)
            mask = masks[gap] if r < WIN else masks[WIN + 1 + gap]
            window_parts.append((weights * mask).astype(jnp.bfloat16))
        values = vs[rows[0] * COLS : (rows[-1] + 1) * COLS, :]
        window = window_ref[r] + jnp.dot(
            jnp.concatenate(window_parts, axis=1), values, preferred_element_type=jnp.float32
        )
        window = window[:, :HEAD_DIM] / window[:, HEAD_DIM : HEAD_DIM + 1]
        total = window + zonal_ref[r].astype(jnp.float32)
        out[:, :, r * HEAD_DIM : (r + 1) * HEAD_DIM] = total.reshape(16, 8, HEAD_DIM)
    for k in range(8):
        chunks[k // 4][k % 4, 0] = out[ints[3 + k]].astype(jnp.bfloat16)
        chunks[k // 4][k % 4, 1] = out[ints[11 + k]].astype(jnp.bfloat16)


def outer(ints, factor, inner_results, parts, edges):
    chunk = jax.ShapeDtypeStruct((4, 2, 8, ROWS * HEAD_DIM), jnp.bfloat16)
    return pl.pallas_call(
        outer_kernel,
        out_shape=[chunk] * 2,
        in_specs=[SMEM, SMEM] + [VMEM] * 10,
        out_specs=[VMEM] * 2,
        scratch_shapes=[
            pltpu.VMEM((2 * WIN * COLS, HEAD_DIM), jnp.bfloat16),
            pltpu.VMEM((2 * WIN * COLS, 256), jnp.bfloat16),
            pltpu.VMEM((16, 8, ROWS * HEAD_DIM), jnp.float32),
        ],
        compiler_params=pltpu.CompilerParams(vmem_limit_bytes=16 * MIB),
        cost_estimate=pl.CostEstimate(
            flops=10**9, bytes_accessed=4 * MIB, transcendentals=10**6
        ),
        name="outer",
    )(ints, factor, *inner_results, *parts, *edges)


def regroup_kernel(near, far, *parts):
    for k, part in enumerate(parts):
        part[0] = near[k + 1]
        part[1] = far[k + 1]


def regroup(near, far):
    part = jax.ShapeDtypeStruct((2, *near.shape[1:]), near.dtype)
    return pl.pallas_call(
        regroup_kernel,
        out_shape=[part] * 3,
        in_specs=[VMEM] * 2,
        out_specs=[VMEM] * 3,
        compiler_params=pltpu.CompilerParams(vmem_limit_bytes=4 * MIB),
        cost_estimate=pl.CostEstimate(flops=0, bytes_accessed=MIB, transcendentals=0),
        name="regroup",
    )(near, far)


def assemble_kernel(at, *refs):
    width, out = ROWS * HEAD_DIM, refs[10]
    for part in range(2):
        landed = refs[5 * part : 5 * part + 5]
        for k in range(8):
            kind, x = k // 4, k % 4
            value = landed[kind][0, part] if x == 0 else landed[x + 1][kind, part]
            out[0, :, pl.ds(pl.multiple_of(at[8 * part + k] * width, 128), width)] = value


def assemble(at, landed):
    return pl.pallas_call(
        assemble_kernel,
        out_shape=jax.ShapeDtypeStruct((1, 8, LAT * ROWS * HEAD_DIM), jnp.bfloat16),
        in_specs=[SMEM] + [VMEM] * 10,
        out_specs=VMEM,
        compiler_params=pltpu.CompilerParams(vmem_limit_bytes=4 * MIB),
        cost_estimate=pl.CostEstimate(flops=0, bytes_accessed=MIB, transcendentals=0),
        name="assemble",
    )(at, *landed)


def body(tokens, w_qkv, key_mask, band_of_row, radius, qk_scale):
    y_lo, z, y_hi, x, core = (lax.axis_index(a) for a in AXES)
    sector = y_hi * 4 + x
    block = block_of(y_lo, y_hi, x)
    head = core * 8 + z
    model = tokens.shape[-1]

    wide = tokens.astype(jnp.float32)
    normed = wide * lax.rsqrt(jnp.mean(wide * wide, axis=-1, keepdims=True) + EPS)
    normed = jnp.transpose(normed.astype(jnp.bfloat16), (1, 0, 2)).reshape(64, model)
    normed, own = lax.optimization_barrier((normed, w_qkv[0]))
    first = lax.ppermute(normed, AXES, spread_perm())

    partner = lax.ppermute(own, ("y_lo", "y_hi", "core"), weight_perm())

    base = (z - 2 * block) & 7
    padded = jnp.pad(key_mask, ((0, 0), (WIN, WIN)))
    usable = lax.dynamic_slice_in_dim(padded, block * ROWS, KEY_ROWS, 1)
    usable = jnp.transpose(usable).astype(jnp.float32)
    ids = lax.dynamic_slice_in_dim(band_of_row, block * ROWS, ROWS, 0)
    band = (ids[:, None] == ids[None, :]).astype(jnp.float32).reshape(ROWS * ROWS)
    groups = [
        group_at(sector ^ k, side, base, core) for side in (y_lo, 1 - y_lo) for k in range(8)
    ]
    reach = lax.dynamic_index_in_dim(radius, head, keepdims=False)
    ints = jnp.stack([base, core, reach] + groups).astype(jnp.int32)
    factor = lax.dynamic_slice_in_dim(qk_scale, head, 1, 0) / HEAD_DIM * LOG2E
    at = []
    for from_y_lo in (core, 1 - core):
        for k in range(8):
            source = sector ^ k
            at.append(block_of(from_y_lo, source >> 2, source & 3))
    at = jnp.stack(at).astype(jnp.int32)
    flags = jnp.stack([core == y_lo, core]).astype(jnp.int32)

    first, usable, band, ints, factor, at, flags = lax.optimization_barrier(
        (first, usable, band, ints, factor, at, flags)
    )

    a = b = first
    pieces = [first]
    for k in range(1, 5):
        a = lax.ppermute(a, ("z", "core"), ring_perm())
        pieces.append(a)
        if k < 4:
            b = lax.ppermute(b, ("z", "core"), ring_perm(cross=int(k == 1)))
            pieces.append(b)

    corners = ("y_lo", "y_hi", "x", "core")
    keep, send, edge, give = project(flags, pieces, own, partner)
    halo_own = lax.ppermute(edge, corners, neighbour_perm())
    halo_oth = lax.ppermute(lax.ppermute(give, "core", SWAP), corners, neighbour_perm())
    parts = keep, lax.ppermute(send, "core", SWAP)
    results = inner(ints, factor, band, usable, parts)
    halo_own, halo_oth, *results = lax.optimization_barrier((halo_own, halo_oth, *results))
    halos = [halo_own, halo_oth] + [lax.ppermute(halo, "core", SWAP) for halo in (halo_own, halo_oth)]
    chunks = outer(ints, factor, results, parts, halos)

    near, far = (lax.ppermute(chunks[k], ("y_lo", "y_hi", "core"), return_perm(k)) for k in range(2))
    passed = regroup(near, far)
    along = [[(i, i ^ k) for i in range(4)] for k in range(1, 4)]
    landed = [near, far] + [lax.ppermute(part, "x", perm) for part, perm in zip(passed, along)]
    return assemble(at, landed + [lax.ppermute(part, "core", SWAP) for part in landed])


def solution(mesh):
    wide = Mesh(mesh.devices.reshape(SIZES), AXES)
    lat, lon = ("y_lo", "z"), ("y_hi", "x", "core")
    in_specs = (P(lon, lat, None), P(lat, None, None), P(), P(), P(), P())
    out_specs = P(lat, lon, None)
    return jax.shard_map(body, mesh=wide, in_specs=in_specs, out_specs=out_specs, check_vma=False)
```

```python
import jax
import jax.numpy as jnp
from jax import lax
from jax.experimental import pallas as pl
from jax.experimental.pallas import tpu as pltpu
from jax.sharding import Mesh, PartitionSpec as P

HEAD_DIM = 160
QKV = 3 * HEAD_DIM
ROWS = 8
WIN = 4
COLS = 128
HALF = COLS // 2
KEY_ROWS = ROWS + 2 * WIN
EPS = 1e-06
BIG = 1e30
LOG2E = 1.4426950408889634
LAT, LON = 16, 16
AXES = ("y_lo", "z", "y_hi", "x", "core")
SIZES = (2, 8, 2, 4, 2)
NT = (((1,), (1,)), ((), ()))
MIB = 1024 * 1024
SMEM = pl.BlockSpec(memory_space=pltpu.SMEM)
VMEM = pl.BlockSpec(memory_space=pltpu.VMEM)


def place_of(block):
    y_lo, rest = block // 8, block % 8
    side, k = rest // 4, rest % 4
    return y_lo, side ^ y_lo, k if side == 0 else 3 - k


def block_of(y_lo, y_hi, x):
    side = y_hi ^ y_lo
    return y_lo * 8 + side * 4 + jnp.where(side == 0, x, 3 - x)


def flat(*pairs):
    index = 0
    for coordinate, size in pairs:
        index = index * size + coordinate
    return index


def spread_perm():
    pairs = []
    for y_lo in range(2):
        for z in range(8):
            _, to_y_hi, to_x = place_of(y_lo * 8 + z)
            for s in range(8):
                for core in range(2):
                    to_z = (s + 2 * z + 4 * core) % 8
                    source = flat((y_lo, 2), (z, 8), (s, 8), (core, 2))
                    target = flat((y_lo, 2), (to_z, 8), (to_y_hi, 2), (to_x, 4), (core, 2))
                    pairs.append((source, target))
    return pairs


def ring_perm(cross=0):
    pairs = []
    for z in range(8):
        for core in range(2):
            there = (z + 1 - 2 * core) % 8
            pairs.append((flat((z, 8), (core ^ cross, 2)), flat((there, 8), (core, 2))))
    return pairs


def weight_perm():
    pairs = []
    for y in range(4):
        for core in range(2):
            there = (y + 1 - 2 * core) % 4
            source = flat((y % 2, 2), (y // 2, 2), (core, 2))
            pairs.append((source, flat((there % 2, 2), (there // 2, 2), (core, 2))))
    return pairs


def neighbour_perm():
    pairs = []
    for block in range(16):
        for core in range(2):
            if 0 <= block + 1 - 2 * core < 16:
                here, there = place_of(block), place_of(block + 1 - 2 * core)
                source = flat((here[0], 2), (here[1], 2), (here[2], 4), (core, 2))
                target = flat((there[0], 2), (there[1], 2), (there[2], 4), (core, 2))
                pairs.append((source, target))
    return pairs


def return_perm(k):
    pairs = []
    for y_lo in range(2):
        for y_hi in range(2):
            for core in range(2):
                source = flat((y_lo, 2), (y_hi, 2), (core, 2))
                pairs.append((source, flat((core, 2), (y_hi ^ k, 2), (y_lo, 2))))
    return pairs


SWAP = [(0, 1), (1, 0)]


def normalized(p):
    lane = lax.broadcasted_iota(jnp.int32, (1, QKV), 1)
    is_q = lane < HEAD_DIM
    is_k = (lane >= HEAD_DIM) & (lane < 2 * HEAD_DIM)
    squares = p * p
    q_mean = jnp.sum(jnp.where(is_q, squares, 0.0), axis=-1, keepdims=True) / HEAD_DIM
    k_mean = jnp.sum(jnp.where(is_k, squares, 0.0), axis=-1, keepdims=True) / HEAD_DIM
    scale = jnp.where(is_q, lax.rsqrt(q_mean + EPS), jnp.where(is_k, lax.rsqrt(k_mean + EPS), 1.0))
    groups = p.shape[0] // (8 * ROWS)
    p = (p * scale).reshape(groups, ROWS, 8, QKV)
    return [p[:, r].reshape(8 * groups, QKV).astype(jnp.bfloat16) for r in range(ROWS)]


def project_kernel(flags, *refs):
    pieces, (own, partner), (keep, send, edge, give, x_ref, w_ref, sem) = refs[:8], refs[8:10], refs[10:]
    load = pltpu.make_async_copy(partner, w_ref, sem)
    load.start()
    for g, piece in enumerate(pieces):
        x_ref[64 * g : 64 * (g + 1), :] = piece[...]
    p = lax.dot_general(x_ref[...], own[...], NT, preferred_element_type=jnp.float32)
    own_rows = normalized(p)
    load.wait()
    p = lax.dot_general(x_ref[...], w_ref[...], NT, preferred_element_type=jnp.float32)
    other_rows = normalized(p)

    def store(first, second):
        for r in range(ROWS):
            keep[r] = first[r]
            send[r] = second[r]

    @pl.when(flags[0] == 1)
    def _():
        store(own_rows, other_rows)

    @pl.when(flags[0] != 1)
    def _():
        store(other_rows, own_rows)

    def store_edges(top, bottom):
        for r in range(ROWS):
            row = jnp.concatenate([keep[r][:, HEAD_DIM:], send[r][:, HEAD_DIM:]], axis=1)
            (top if r < WIN else bottom)[r % WIN] = row

    @pl.when(flags[1] == 0)
    def _():
        store_edges(give, edge)

    @pl.when(flags[1] != 0)
    def _():
        store_edges(edge, give)


def project(flags, pieces, own, partner):
    whole = jax.ShapeDtypeStruct((ROWS, HALF, QKV), jnp.bfloat16)
    part = jax.ShapeDtypeStruct((WIN, HALF, 4 * HEAD_DIM), jnp.bfloat16)
    return pl.pallas_call(
        project_kernel,
        out_shape=[whole, whole, part, part],
        in_specs=[SMEM] + [VMEM] * 9 + [pl.BlockSpec(memory_space=pl.ANY)],
        out_specs=[VMEM] * 4,
        scratch_shapes=[
            pltpu.VMEM((512, own.shape[1]), jnp.bfloat16),
            pltpu.VMEM(own.shape, jnp.bfloat16),
            pltpu.SemaphoreType.DMA,
        ],
        compiler_params=pltpu.CompilerParams(vmem_limit_bytes=20 * MIB),
        cost_estimate=pl.CostEstimate(
            flops=2 * 512 * 960 * 2560, bytes_accessed=8 * MIB, transcendentals=0
        ),
        name="project",
    )(flags, *pieces, own, partner)


def put(ks, vs, first, key, value):
    at = pl.ds(first, key.shape[0])
    ks[at, :] = key
    vs[at, :HEAD_DIM] = value
    is_one = lax.broadcasted_iota(jnp.int32, (key.shape[0], 256 - HEAD_DIM), 1) == 0
    vs[at, HEAD_DIM:] = jnp.where(is_one, 1.0, 0.0).astype(jnp.bfloat16)


def columns(base, core, shape, dim):
    at = lax.broadcasted_iota(jnp.int32, shape, dim)
    side = core ^ (at >> 6)
    g = (at >> 3) & 7
    j = (g + 1) >> 1
    ch = side ^ jnp.where(g == 0, 0, 1 - (g & 1))
    sector = (base + jnp.where(side == 1, j, -j) - 4 * ch) & 7
    return sector * 16 + ch * 8 + (at & 7)


def group_at(sector, ch, base, core):
    i = (sector - base + 4 * ch) & 7
    side = jnp.where((i & 3) == 0, ch, jnp.where(i < 4, 1, 0))
    j = jnp.minimum(i, 8 - i)
    g = jnp.where(i == 0, 0, 2 * j - jnp.where(ch == side, 1, 0))
    return 8 * (side ^ core) + g


def fill_masks(masks, first, query_base, key_base, core, radius):
    square = (COLS, COLS)
    gap = (columns(query_base, core, square, 0) - columns(key_base, core, square, 1) + radius) & (COLS - 1)
    near = jnp.where(gap <= 2 * radius, 1.0, 0.0)
    for d in range(WIN + 1):
        masks[first + d] = jnp.where(radius >= d, near, 0.0)


def shifts(usable, key_base, core):
    square = (COLS, COLS)
    there = lax.broadcasted_iota(jnp.int32, square, 0) == columns(key_base, core, square, 1)
    moved = jnp.dot(usable[...], jnp.where(there, 1.0, 0.0), preferred_element_type=jnp.float32)
    return jnp.where(moved > 0.5, 0.0, -BIG)


def query_of(parts, r):
    return jnp.concatenate([part[r][:, :HEAD_DIM] for part in parts], axis=0)


def scores_of(query, ks, row):
    keys = ks[row * COLS : (row + 1) * COLS, :]
    return lax.dot_general(query, keys, NT, preferred_element_type=jnp.float32)


def inner_kernel(ints, factor_ref, band, usable, *refs):
    parts, (zonal_ref, window_ref, masks_ref, shifts_ref, ks, vs, masks) = refs[:2], refs[2:]
    factor = factor_ref[0]
    start = 0
    for part in parts:
        for r in range(ROWS):
            whole = part[r]
            put(ks, vs, r * COLS + start, whole[:, HEAD_DIM : 2 * HEAD_DIM], whole[:, 2 * HEAD_DIM :])
        start += part.shape[1]
    base, core, radius = ints[0], ints[1], ints[2]
    fill_masks(masks, 0, base, base, core, radius)
    bias = shifts(usable, base, core)
    fill_masks(masks_ref, 0, base, base + 2, core, radius)
    fill_masks(masks_ref, WIN + 1, base, base - 2, core, radius)
    shifts_ref[0] = shifts(usable, base + 2, core)
    shifts_ref[1] = shifts(usable, base - 2, core)
    eye = lax.broadcasted_iota(jnp.int32, (COLS, COLS), 0) == lax.broadcasted_iota(jnp.int32, (COLS, COLS), 1)
    for r in range(ROWS):
        query = query_of(parts, r)
        low, high = max(0, r - WIN), min(ROWS, r + WIN + 1)
        zonal_parts, window_parts = [], []
        for row in range(ROWS):
            shift = bias[WIN + row : WIN + row + 1, :]
            if row == r:
                shift = jnp.where(eye, 0.0, shift)
            weights = jnp.exp2(scores_of(query, ks, row) * factor + shift)
            zonal_parts.append((weights * band[r * ROWS + row]).astype(jnp.bfloat16))
            if low <= row < high:
                window_parts.append((weights * masks[abs(row - r)]).astype(jnp.bfloat16))
        zonal = jnp.dot(jnp.concatenate(zonal_parts, axis=1), vs[...], preferred_element_type=jnp.float32)
        window_ref[r] = jnp.dot(
            jnp.concatenate(window_parts, axis=1),
            vs[low * COLS : high * COLS, :],
            preferred_element_type=jnp.float32,
        )
        zonal_ref[r] = (zonal[:, :HEAD_DIM] / zonal[:, HEAD_DIM : HEAD_DIM + 1]).astype(jnp.bfloat16)


def inner(ints, factor, band, usable, parts):
    return pl.pallas_call(
        inner_kernel,
        out_shape=[
            jax.ShapeDtypeStruct((ROWS, COLS, HEAD_DIM), jnp.bfloat16),
            jax.ShapeDtypeStruct((ROWS, COLS, 256), jnp.float32),
            jax.ShapeDtypeStruct((2 * WIN + 2, COLS, COLS), jnp.float32),
            jax.ShapeDtypeStruct((2, KEY_ROWS, COLS), jnp.float32),
        ],
        in_specs=[SMEM] * 3 + [VMEM] * 3,
        out_specs=[VMEM] * 4,
        scratch_shapes=[
            pltpu.VMEM((ROWS * COLS, HEAD_DIM), jnp.bfloat16),
            pltpu.VMEM((ROWS * COLS, 256), jnp.bfloat16),
            pltpu.VMEM((WIN + 1, COLS, COLS), jnp.float32),
        ],
        compiler_params=pltpu.CompilerParams(vmem_limit_bytes=16 * MIB),
        cost_estimate=pl.CostEstimate(flops=10**7, bytes_accessed=10**5, transcendentals=0),
        name="inner",
    )(ints, factor, band, usable, *parts)


def outer_kernel(ints, factor_ref, zonal_ref, window_ref, masks, shifts_ref, *refs):
    parts, (own, oth, far_own, far_oth), chunks, (ks, vs, out) = refs[:2], refs[2:6], refs[6:8], refs[8:]
    factor = factor_ref[0]
    core = ints[1]
    for edge, side, half, second in ((own, core, 0, 0), (oth, core, 1, 1), (far_own, 1 - core, 1, 1), (far_oth, 1 - core, 0, 0)):
        at = 2 * HEAD_DIM * second
        for r in range(WIN):
            whole = edge[r][:, at : at + 2 * HEAD_DIM]
            first = pl.multiple_of(side * (WIN * COLS) + r * COLS + half * HALF, HALF)
            put(ks, vs, first, whole[:, :HEAD_DIM], whole[:, HEAD_DIM:])
    above, below = shifts_ref[0], shifts_ref[1]
    for r in range(ROWS):
        query = query_of(parts, r)
        rows = range(r, WIN) if r < WIN else range(WIN, r + 1)
        window_parts = []
        for row in rows:
            gap = r + WIN - row if r < WIN else ROWS + row - WIN - r
            shift = above[row : row + 1, :] if r < WIN else below[row + ROWS : row + ROWS + 1, :]
            weights = jnp.exp2(scores_of(query, ks, row) * factor + shift)
            mask = masks[gap] if r < WIN else masks[WIN + 1 + gap]
            window_parts.append((weights * mask).astype(jnp.bfloat16))
        values = vs[rows[0] * COLS : (rows[-1] + 1) * COLS, :]
        window = window_ref[r] + jnp.dot(
            jnp.concatenate(window_parts, axis=1), values, preferred_element_type=jnp.float32
        )
        window = window[:, :HEAD_DIM] / window[:, HEAD_DIM : HEAD_DIM + 1]
        total = window + zonal_ref[r].astype(jnp.float32)
        out[:, :, r * HEAD_DIM : (r + 1) * HEAD_DIM] = total.reshape(16, 8, HEAD_DIM)
    for k in range(8):
        chunks[k // 4][k % 4, 0] = out[ints[3 + k]].astype(jnp.bfloat16)
        chunks[k // 4][k % 4, 1] = out[ints[11 + k]].astype(jnp.bfloat16)


def outer(ints, factor, inner_results, parts, edges):
    chunk = jax.ShapeDtypeStruct((4, 2, 8, ROWS * HEAD_DIM), jnp.bfloat16)
    return pl.pallas_call(
        outer_kernel,
        out_shape=[chunk] * 2,
        in_specs=[SMEM, SMEM] + [VMEM] * 10,
        out_specs=[VMEM] * 2,
        scratch_shapes=[
            pltpu.VMEM((2 * WIN * COLS, HEAD_DIM), jnp.bfloat16),
            pltpu.VMEM((2 * WIN * COLS, 256), jnp.bfloat16),
            pltpu.VMEM((16, 8, ROWS * HEAD_DIM), jnp.float32),
        ],
        compiler_params=pltpu.CompilerParams(vmem_limit_bytes=16 * MIB),
        cost_estimate=pl.CostEstimate(
            flops=10**9, bytes_accessed=4 * MIB, transcendentals=10**6
        ),
        name="outer",
    )(ints, factor, *inner_results, *parts, *edges)


def regroup_kernel(near, far, *parts):
    for k, part in enumerate(parts):
        part[0] = near[k + 1]
        part[1] = far[k + 1]


def regroup(near, far):
    part = jax.ShapeDtypeStruct((2, *near.shape[1:]), near.dtype)
    return pl.pallas_call(
        regroup_kernel,
        out_shape=[part] * 3,
        in_specs=[VMEM] * 2,
        out_specs=[VMEM] * 3,
        compiler_params=pltpu.CompilerParams(vmem_limit_bytes=4 * MIB),
        cost_estimate=pl.CostEstimate(flops=0, bytes_accessed=MIB, transcendentals=0),
        name="regroup",
    )(near, far)


def assemble_kernel(at, *refs):
    width, out = ROWS * HEAD_DIM, refs[10]
    for part in range(2):
        landed = refs[5 * part : 5 * part + 5]
        for k in range(8):
            kind, x = k // 4, k % 4
            value = landed[kind][0, part] if x == 0 else landed[x + 1][kind, part]
            out[0, :, pl.ds(pl.multiple_of(at[8 * part + k] * width, 128), width)] = value


def assemble(at, landed):
    return pl.pallas_call(
        assemble_kernel,
        out_shape=jax.ShapeDtypeStruct((1, 8, LAT * ROWS * HEAD_DIM), jnp.bfloat16),
        in_specs=[SMEM] + [VMEM] * 10,
        out_specs=VMEM,
        compiler_params=pltpu.CompilerParams(vmem_limit_bytes=4 * MIB),
        cost_estimate=pl.CostEstimate(flops=0, bytes_accessed=MIB, transcendentals=0),
        name="assemble",
    )(at, *landed)


def body(tokens, w_qkv, key_mask, band_of_row, radius, qk_scale):
    y_lo, z, y_hi, x, core = (lax.axis_index(a) for a in AXES)
    sector = y_hi * 4 + x
    block = block_of(y_lo, y_hi, x)
    head = core * 8 + z
    model = tokens.shape[-1]

    wide = tokens.astype(jnp.float32)
    normed = wide * lax.rsqrt(jnp.mean(wide * wide, axis=-1, keepdims=True) + EPS)
    normed = jnp.transpose(normed.astype(jnp.bfloat16), (1, 0, 2)).reshape(64, model)
    first = lax.ppermute(normed, AXES, spread_perm())

    base = (z - 2 * block) & 7
    padded = jnp.pad(key_mask, ((0, 0), (WIN, WIN)))
    usable = lax.dynamic_slice_in_dim(padded, block * ROWS, KEY_ROWS, 1)
    usable = jnp.transpose(usable).astype(jnp.float32)
    ids = lax.dynamic_slice_in_dim(band_of_row, block * ROWS, ROWS, 0)
    band = (ids[:, None] == ids[None, :]).astype(jnp.float32).reshape(ROWS * ROWS)
    groups = [
        group_at(sector ^ k, side, base, core) for side in (y_lo, 1 - y_lo) for k in range(8)
    ]
    reach = lax.dynamic_index_in_dim(radius, head, keepdims=False)
    ints = jnp.stack([base, core, reach] + groups).astype(jnp.int32)
    factor = lax.dynamic_slice_in_dim(qk_scale, head, 1, 0) / HEAD_DIM * LOG2E
    at = []
    for from_y_lo in (core, 1 - core):
        for k in range(8):
            source = sector ^ k
            at.append(block_of(from_y_lo, source >> 2, source & 3))
    at = jnp.stack(at).astype(jnp.int32)
    flags = jnp.stack([core == y_lo, core]).astype(jnp.int32)

    first, own, usable, band, ints, factor, at, flags = lax.optimization_barrier(
        (first, w_qkv[0], usable, band, ints, factor, at, flags)
    )

    partner = lax.ppermute(own, ("y_lo", "y_hi", "core"), weight_perm())

    a = b = first
    pieces = [first]
    for k in range(1, 5):
        a = lax.ppermute(a, ("z", "core"), ring_perm())
        pieces.append(a)
        if k < 4:
            b = lax.ppermute(b, ("z", "core"), ring_perm(cross=int(k == 1)))
            pieces.append(b)

    corners = ("y_lo", "y_hi", "x", "core")
    keep, send, edge, give = project(flags, pieces, own, partner)
    halo_own = lax.ppermute(edge, corners, neighbour_perm())
    halo_oth = lax.ppermute(lax.ppermute(give, "core", SWAP), corners, neighbour_perm())
    parts = keep, lax.ppermute(send, "core", SWAP)
    results = inner(ints, factor, band, usable, parts)
    halo_own, halo_oth, *results = lax.optimization_barrier((halo_own, halo_oth, *results))
    halos = [halo_own, halo_oth] + [lax.ppermute(halo, "core", SWAP) for halo in (halo_own, halo_oth)]
    chunks = outer(ints, factor, results, parts, halos)

    near, far = (lax.ppermute(chunks[k], ("y_lo", "y_hi", "core"), return_perm(k)) for k in range(2))
    passed = regroup(near, far)
    along = [[(i, i ^ k) for i in range(4)] for k in range(1, 4)]
    landed = [near, far] + [lax.ppermute(part, "x", perm) for part, perm in zip(passed, along)]
    return assemble(at, landed + [lax.ppermute(part, "core", SWAP) for part in landed])


def solution(mesh):
    wide = Mesh(mesh.devices.reshape(SIZES), AXES)
    lat, lon = ("y_lo", "z"), ("y_hi", "x", "core")
    in_specs = (P(lon, lat, None), P(lat, None, None), P(), P(), P(), P())
    out_specs = P(lat, lon, None)
    return jax.shard_map(body, mesh=wide, in_specs=in_specs, out_specs=out_specs, check_vma=False)
```

```python
import jax
import jax.numpy as jnp
from jax import lax
from jax.experimental import pallas as pl
from jax.experimental.pallas import tpu as pltpu
from jax.sharding import Mesh, PartitionSpec as P

HEAD_DIM = 160
QKV = 3 * HEAD_DIM
ROWS = 8
WIN = 4
COLS = 128
HALF = COLS // 2
KEY_ROWS = ROWS + 2 * WIN
EPS = 1e-06
BIG = 1e30
LOG2E = 1.4426950408889634
LAT, LON = 16, 16
AXES = ("y_lo", "z", "y_hi", "x", "core")
SIZES = (2, 8, 2, 4, 2)
NT = (((1,), (1,)), ((), ()))
MIB = 1024 * 1024
SMEM = pl.BlockSpec(memory_space=pltpu.SMEM)
VMEM = pl.BlockSpec(memory_space=pltpu.VMEM)


def place_of(block):
    y_lo, rest = block // 8, block % 8
    side, k = rest // 4, rest % 4
    return y_lo, side ^ y_lo, k if side == 0 else 3 - k


def block_of(y_lo, y_hi, x):
    side = y_hi ^ y_lo
    return y_lo * 8 + side * 4 + jnp.where(side == 0, x, 3 - x)


def flat(*pairs):
    index = 0
    for coordinate, size in pairs:
        index = index * size + coordinate
    return index


def spread_perm():
    pairs = []
    for y_lo in range(2):
        for z in range(8):
            _, to_y_hi, to_x = place_of(y_lo * 8 + z)
            for s in range(8):
                for core in range(2):
                    to_z = (s + 2 * z + 4 * core) % 8
                    source = flat((y_lo, 2), (z, 8), (s, 8), (core, 2))
                    target = flat((y_lo, 2), (to_z, 8), (to_y_hi, 2), (to_x, 4), (core, 2))
                    pairs.append((source, target))
    return pairs


def ring_perm():
    pairs = []
    for z in range(8):
        for core in range(2):
            there = (z + 1 - 2 * core) % 8
            pairs.append((flat((z, 8), (core, 2)), flat((there, 8), (core, 2))))
    return pairs


def weight_perm():
    pairs = []
    for y in range(4):
        for core in range(2):
            there = (y + 1 - 2 * core) % 4
            source = flat((y % 2, 2), (y // 2, 2), (core, 2))
            pairs.append((source, flat((there % 2, 2), (there // 2, 2), (core, 2))))
    return pairs


def neighbour_perm():
    pairs = []
    for block in range(16):
        for core in range(2):
            if 0 <= block + 1 - 2 * core < 16:
                here, there = place_of(block), place_of(block + 1 - 2 * core)
                source = flat((here[0], 2), (here[1], 2), (here[2], 4), (core, 2))
                target = flat((there[0], 2), (there[1], 2), (there[2], 4), (core, 2))
                pairs.append((source, target))
    return pairs


def return_perm(k):
    pairs = []
    for y_lo in range(2):
        for y_hi in range(2):
            for core in range(2):
                source = flat((y_lo, 2), (y_hi, 2), (core, 2))
                pairs.append((source, flat((core, 2), (y_hi ^ k, 2), (y_lo, 2))))
    return pairs


SWAP = [(0, 1), (1, 0)]


def normalized(p):
    lane = lax.broadcasted_iota(jnp.int32, (1, QKV), 1)
    is_q = lane < HEAD_DIM
    is_k = (lane >= HEAD_DIM) & (lane < 2 * HEAD_DIM)
    squares = p * p
    q_mean = jnp.sum(jnp.where(is_q, squares, 0.0), axis=-1, keepdims=True) / HEAD_DIM
    k_mean = jnp.sum(jnp.where(is_k, squares, 0.0), axis=-1, keepdims=True) / HEAD_DIM
    scale = jnp.where(is_q, lax.rsqrt(q_mean + EPS), jnp.where(is_k, lax.rsqrt(k_mean + EPS), 1.0))
    groups = p.shape[0] // (8 * ROWS)
    p = (p * scale).reshape(groups, ROWS, 8, QKV)
    return [p[:, r].reshape(8 * groups, QKV).astype(jnp.bfloat16) for r in range(ROWS)]


def project_kernel(flags, *refs):
    pieces, (own, partner), (keep, send, edge, give, x_ref, w_ref, sem) = refs[:8], refs[8:10], refs[10:]
    load = pltpu.make_async_copy(partner, w_ref, sem)
    load.start()
    for g, piece in enumerate(pieces):
        x_ref[64 * g : 64 * (g + 1), :] = piece[...]
    p = lax.dot_general(x_ref[...], own[...], NT, preferred_element_type=jnp.float32)
    own_rows = normalized(p)
    load.wait()
    p = lax.dot_general(x_ref[...], w_ref[...], NT, preferred_element_type=jnp.float32)
    other_rows = normalized(p)

    def store(first, second):
        for r in range(ROWS):
            keep[r] = first[r]
            send[r] = second[r]

    @pl.when(flags[0] == 1)
    def _():
        store(own_rows, other_rows)

    @pl.when(flags[0] != 1)
    def _():
        store(other_rows, own_rows)

    def store_edges(top, bottom):
        for r in range(ROWS):
            row = jnp.concatenate([keep[r][:, HEAD_DIM:], send[r][:, HEAD_DIM:]], axis=1)
            (top if r < WIN else bottom)[r % WIN] = row

    @pl.when(flags[1] == 0)
    def _():
        store_edges(give, edge)

    @pl.when(flags[1] != 0)
    def _():
        store_edges(edge, give)


def project(flags, pieces, own, partner):
    whole = jax.ShapeDtypeStruct((ROWS, HALF, QKV), jnp.bfloat16)
    part = jax.ShapeDtypeStruct((WIN, HALF, 4 * HEAD_DIM), jnp.bfloat16)
    return pl.pallas_call(
        project_kernel,
        out_shape=[whole, whole, part, part],
        in_specs=[SMEM] + [VMEM] * 9 + [pl.BlockSpec(memory_space=pl.ANY)],
        out_specs=[VMEM] * 4,
        scratch_shapes=[
            pltpu.VMEM((512, own.shape[1]), jnp.bfloat16),
            pltpu.VMEM(own.shape, jnp.bfloat16),
            pltpu.SemaphoreType.DMA,
        ],
        compiler_params=pltpu.CompilerParams(vmem_limit_bytes=20 * MIB),
        cost_estimate=pl.CostEstimate(
            flops=2 * 512 * 960 * 2560, bytes_accessed=8 * MIB, transcendentals=0
        ),
        name="project",
    )(flags, *pieces, own, partner)


def put(ks, vs, first, key, value):
    at = pl.ds(first, key.shape[0])
    ks[at, :] = key
    vs[at, :HEAD_DIM] = value
    is_one = lax.broadcasted_iota(jnp.int32, (key.shape[0], 256 - HEAD_DIM), 1) == 0
    vs[at, HEAD_DIM:] = jnp.where(is_one, 1.0, 0.0).astype(jnp.bfloat16)


def columns(base, core, shape, dim):
    at = lax.broadcasted_iota(jnp.int32, shape, dim)
    side = core ^ (at >> 6)
    g = (at >> 3) & 7
    j = (g + 1) >> 1
    ch = side ^ jnp.where(g == 0, 0, 1 - (g & 1))
    sector = (base + jnp.where(side == 1, j, -j) - 4 * ch) & 7
    return sector * 16 + ch * 8 + (at & 7)


def group_at(sector, ch, base, core):
    i = (sector - base + 4 * ch) & 7
    side = jnp.where((i & 3) == 0, ch, jnp.where(i < 4, 1, 0))
    j = jnp.minimum(i, 8 - i)
    g = jnp.where(i == 0, 0, 2 * j - jnp.where(ch == side, 1, 0))
    return 8 * (side ^ core) + g


def fill_masks(masks, first, query_base, key_base, core, radius):
    square = (COLS, COLS)
    gap = (columns(query_base, core, square, 0) - columns(key_base, core, square, 1) + radius) & (COLS - 1)
    near = jnp.where(gap <= 2 * radius, 1.0, 0.0)
    for d in range(WIN + 1):
        masks[first + d] = jnp.where(radius >= d, near, 0.0)


def shifts(usable, key_base, core):
    square = (COLS, COLS)
    there = lax.broadcasted_iota(jnp.int32, square, 0) == columns(key_base, core, square, 1)
    moved = jnp.dot(usable[...], jnp.where(there, 1.0, 0.0), preferred_element_type=jnp.float32)
    return jnp.where(moved > 0.5, 0.0, -BIG)


def query_of(parts, r):
    return jnp.concatenate([part[r][:, :HEAD_DIM] for part in parts], axis=0)


def scores_of(query, ks, row):
    keys = ks[row * COLS : (row + 1) * COLS, :]
    return lax.dot_general(query, keys, NT, preferred_element_type=jnp.float32)


def inner_kernel(ints, factor_ref, band, usable, *refs):
    parts, (zonal_ref, window_ref, masks_ref, shifts_ref, ks, vs, masks) = refs[:2], refs[2:]
    factor = factor_ref[0]
    start = 0
    for part in parts:
        for r in range(ROWS):
            whole = part[r]
            put(ks, vs, r * COLS + start, whole[:, HEAD_DIM : 2 * HEAD_DIM], whole[:, 2 * HEAD_DIM :])
        start += part.shape[1]
    base, core, radius = ints[0], ints[1], ints[2]
    fill_masks(masks, 0, base, base, core, radius)
    bias = shifts(usable, base, core)
    fill_masks(masks_ref, 0, base, base + 2, core, radius)
    fill_masks(masks_ref, WIN + 1, base, base - 2, core, radius)
    shifts_ref[0] = shifts(usable, base + 2, core)
    shifts_ref[1] = shifts(usable, base - 2, core)
    eye = lax.broadcasted_iota(jnp.int32, (COLS, COLS), 0) == lax.broadcasted_iota(jnp.int32, (COLS, COLS), 1)
    for r in range(ROWS):
        query = query_of(parts, r)
        low, high = max(0, r - WIN), min(ROWS, r + WIN + 1)
        zonal_parts, window_parts = [], []
        for row in range(ROWS):
            shift = bias[WIN + row : WIN + row + 1, :]
            if row == r:
                shift = jnp.where(eye, 0.0, shift)
            weights = jnp.exp2(scores_of(query, ks, row) * factor + shift)
            zonal_parts.append((weights * band[r * ROWS + row]).astype(jnp.bfloat16))
            if low <= row < high:
                window_parts.append((weights * masks[abs(row - r)]).astype(jnp.bfloat16))
        zonal = jnp.dot(jnp.concatenate(zonal_parts, axis=1), vs[...], preferred_element_type=jnp.float32)
        window_ref[r] = jnp.dot(
            jnp.concatenate(window_parts, axis=1),
            vs[low * COLS : high * COLS, :],
            preferred_element_type=jnp.float32,
        )
        zonal_ref[r] = (zonal[:, :HEAD_DIM] / zonal[:, HEAD_DIM : HEAD_DIM + 1]).astype(jnp.bfloat16)


def inner(ints, factor, band, usable, parts):
    return pl.pallas_call(
        inner_kernel,
        out_shape=[
            jax.ShapeDtypeStruct((ROWS, COLS, HEAD_DIM), jnp.bfloat16),
            jax.ShapeDtypeStruct((ROWS, COLS, 256), jnp.float32),
            jax.ShapeDtypeStruct((2 * WIN + 2, COLS, COLS), jnp.float32),
            jax.ShapeDtypeStruct((2, KEY_ROWS, COLS), jnp.float32),
        ],
        in_specs=[SMEM] * 3 + [VMEM] * 3,
        out_specs=[VMEM] * 4,
        scratch_shapes=[
            pltpu.VMEM((ROWS * COLS, HEAD_DIM), jnp.bfloat16),
            pltpu.VMEM((ROWS * COLS, 256), jnp.bfloat16),
            pltpu.VMEM((WIN + 1, COLS, COLS), jnp.float32),
        ],
        compiler_params=pltpu.CompilerParams(vmem_limit_bytes=16 * MIB),
        cost_estimate=pl.CostEstimate(flops=10**7, bytes_accessed=10**5, transcendentals=0),
        name="inner",
    )(ints, factor, band, usable, *parts)


def outer_kernel(ints, factor_ref, zonal_ref, window_ref, masks, shifts_ref, *refs):
    parts, (own, oth, far_own, far_oth), chunks, (ks, vs, out) = refs[:2], refs[2:6], refs[6:8], refs[8:]
    factor = factor_ref[0]
    core = ints[1]
    for edge, side, half, second in ((own, core, 0, 0), (oth, core, 1, 1), (far_own, 1 - core, 1, 1), (far_oth, 1 - core, 0, 0)):
        at = 2 * HEAD_DIM * second
        for r in range(WIN):
            whole = edge[r][:, at : at + 2 * HEAD_DIM]
            first = pl.multiple_of(side * (WIN * COLS) + r * COLS + half * HALF, HALF)
            put(ks, vs, first, whole[:, :HEAD_DIM], whole[:, HEAD_DIM:])
    above, below = shifts_ref[0], shifts_ref[1]
    for r in range(ROWS):
        query = query_of(parts, r)
        rows = range(r, WIN) if r < WIN else range(WIN, r + 1)
        window_parts = []
        for row in rows:
            gap = r + WIN - row if r < WIN else ROWS + row - WIN - r
            shift = above[row : row + 1, :] if r < WIN else below[row + ROWS : row + ROWS + 1, :]
            weights = jnp.exp2(scores_of(query, ks, row) * factor + shift)
            mask = masks[gap] if r < WIN else masks[WIN + 1 + gap]
            window_parts.append((weights * mask).astype(jnp.bfloat16))
        values = vs[rows[0] * COLS : (rows[-1] + 1) * COLS, :]
        window = window_ref[r] + jnp.dot(
            jnp.concatenate(window_parts, axis=1), values, preferred_element_type=jnp.float32
        )
        window = window[:, :HEAD_DIM] / window[:, HEAD_DIM : HEAD_DIM + 1]
        total = window + zonal_ref[r].astype(jnp.float32)
        out[:, :, r * HEAD_DIM : (r + 1) * HEAD_DIM] = total.reshape(16, 8, HEAD_DIM)
    for k in range(8):
        chunks[k // 4][k % 4, 0] = out[ints[3 + k]].astype(jnp.bfloat16)
        chunks[k // 4][k % 4, 1] = out[ints[11 + k]].astype(jnp.bfloat16)


def outer(ints, factor, inner_results, parts, edges):
    chunk = jax.ShapeDtypeStruct((4, 2, 8, ROWS * HEAD_DIM), jnp.bfloat16)
    return pl.pallas_call(
        outer_kernel,
        out_shape=[chunk] * 2,
        in_specs=[SMEM, SMEM] + [VMEM] * 10,
        out_specs=[VMEM] * 2,
        scratch_shapes=[
            pltpu.VMEM((2 * WIN * COLS, HEAD_DIM), jnp.bfloat16),
            pltpu.VMEM((2 * WIN * COLS, 256), jnp.bfloat16),
            pltpu.VMEM((16, 8, ROWS * HEAD_DIM), jnp.float32),
        ],
        compiler_params=pltpu.CompilerParams(vmem_limit_bytes=16 * MIB),
        cost_estimate=pl.CostEstimate(
            flops=10**9, bytes_accessed=4 * MIB, transcendentals=10**6
        ),
        name="outer",
    )(ints, factor, *inner_results, *parts, *edges)


def regroup_kernel(near, far, *parts):
    for k, part in enumerate(parts):
        part[0] = near[k + 1]
        part[1] = far[k + 1]


def regroup(near, far):
    part = jax.ShapeDtypeStruct((2, *near.shape[1:]), near.dtype)
    return pl.pallas_call(
        regroup_kernel,
        out_shape=[part] * 3,
        in_specs=[VMEM] * 2,
        out_specs=[VMEM] * 3,
        compiler_params=pltpu.CompilerParams(vmem_limit_bytes=4 * MIB),
        cost_estimate=pl.CostEstimate(flops=0, bytes_accessed=MIB, transcendentals=0),
        name="regroup",
    )(near, far)


def assemble_kernel(at, *refs):
    width, out = ROWS * HEAD_DIM, refs[10]
    for part in range(2):
        landed = refs[5 * part : 5 * part + 5]
        for k in range(8):
            kind, x = k // 4, k % 4
            value = landed[kind][0, part] if x == 0 else landed[x + 1][kind, part]
            out[0, :, pl.ds(pl.multiple_of(at[8 * part + k] * width, 128), width)] = value


def assemble(at, landed):
    return pl.pallas_call(
        assemble_kernel,
        out_shape=jax.ShapeDtypeStruct((1, 8, LAT * ROWS * HEAD_DIM), jnp.bfloat16),
        in_specs=[SMEM] + [VMEM] * 10,
        out_specs=VMEM,
        compiler_params=pltpu.CompilerParams(vmem_limit_bytes=4 * MIB),
        cost_estimate=pl.CostEstimate(flops=0, bytes_accessed=MIB, transcendentals=0),
        name="assemble",
    )(at, *landed)


def body(tokens, w_qkv, key_mask, band_of_row, radius, qk_scale):
    y_lo, z, y_hi, x, core = (lax.axis_index(a) for a in AXES)
    sector = y_hi * 4 + x
    block = block_of(y_lo, y_hi, x)
    head = core * 8 + z
    model = tokens.shape[-1]

    wide = tokens.astype(jnp.float32)
    normed = wide * lax.rsqrt(jnp.mean(wide * wide, axis=-1, keepdims=True) + EPS)
    normed = jnp.transpose(normed.astype(jnp.bfloat16), (1, 0, 2)).reshape(64, model)
    first = lax.ppermute(normed, AXES, spread_perm())

    base = (z - 2 * block) & 7
    padded = jnp.pad(key_mask, ((0, 0), (WIN, WIN)))
    usable = lax.dynamic_slice_in_dim(padded, block * ROWS, KEY_ROWS, 1)
    usable = jnp.transpose(usable).astype(jnp.float32)
    ids = lax.dynamic_slice_in_dim(band_of_row, block * ROWS, ROWS, 0)
    band = (ids[:, None] == ids[None, :]).astype(jnp.float32).reshape(ROWS * ROWS)
    groups = [
        group_at(sector ^ k, side, base, core) for side in (y_lo, 1 - y_lo) for k in range(8)
    ]
    reach = lax.dynamic_index_in_dim(radius, head, keepdims=False)
    ints = jnp.stack([base, core, reach] + groups).astype(jnp.int32)
    factor = lax.dynamic_slice_in_dim(qk_scale, head, 1, 0) / HEAD_DIM * LOG2E
    at = []
    for from_y_lo in (core, 1 - core):
        for k in range(8):
            source = sector ^ k
            at.append(block_of(from_y_lo, source >> 2, source & 3))
    at = jnp.stack(at).astype(jnp.int32)
    flags = jnp.stack([core == y_lo, core]).astype(jnp.int32)

    first, own, usable, band, ints, factor, at, flags = lax.optimization_barrier(
        (first, w_qkv[0], usable, band, ints, factor, at, flags)
    )

    partner = lax.ppermute(own, ("y_lo", "y_hi", "core"), weight_perm())

    a, b = first, lax.ppermute(first, "core", SWAP)
    pieces = [first]
    for k in range(1, 5):
        a = lax.ppermute(a, ("z", "core"), ring_perm())
        pieces.append(a)
        if k < 4:
            b = lax.ppermute(b, ("z", "core"), ring_perm())
            pieces.append(b)

    corners = ("y_lo", "y_hi", "x", "core")
    keep, send, edge, give = project(flags, pieces, own, partner)
    halo_own = lax.ppermute(edge, corners, neighbour_perm())
    halo_oth = lax.ppermute(lax.ppermute(give, "core", SWAP), corners, neighbour_perm())
    parts = keep, lax.ppermute(send, "core", SWAP)
    results = inner(ints, factor, band, usable, parts)
    halo_own, halo_oth, *results = lax.optimization_barrier((halo_own, halo_oth, *results))
    halos = [halo_own, halo_oth] + [lax.ppermute(halo, "core", SWAP) for halo in (halo_own, halo_oth)]
    chunks = outer(ints, factor, results, parts, halos)

    near, far = (lax.ppermute(chunks[k], ("y_lo", "y_hi", "core"), return_perm(k)) for k in range(2))
    passed = regroup(near, far)
    along = [[(i, i ^ k) for i in range(4)] for k in range(1, 4)]
    landed = [near, far] + [lax.ppermute(part, "x", perm) for part, perm in zip(passed, along)]
    return assemble(at, landed + [lax.ppermute(part, "core", SWAP) for part in landed])


def solution(mesh):
    wide = Mesh(mesh.devices.reshape(SIZES), AXES)
    lat, lon = ("y_lo", "z"), ("y_hi", "x", "core")
    in_specs = (P(lon, lat, None), P(lat, None, None), P(), P(), P(), P())
    out_specs = P(lat, lon, None)
    return jax.shard_map(body, mesh=wide, in_specs=in_specs, out_specs=out_specs, check_vma=False)
```

```python
import jax
import jax.numpy as jnp
from jax import lax
from jax.experimental import pallas as pl
from jax.experimental.pallas import tpu as pltpu
from jax.sharding import Mesh, PartitionSpec as P

HEAD_DIM = 160
QKV = 3 * HEAD_DIM
ROWS = 8
WIN = 4
COLS = 128
HALF = COLS // 2
KEY_ROWS = ROWS + 2 * WIN
EPS = 1e-06
BIG = 1e30
LOG2E = 1.4426950408889634
LAT, LON = 16, 16
AXES = ("y_lo", "z", "y_hi", "x", "core")
SIZES = (2, 8, 2, 4, 2)
NT = (((1,), (1,)), ((), ()))
MIB = 1024 * 1024
SMEM = pl.BlockSpec(memory_space=pltpu.SMEM)
VMEM = pl.BlockSpec(memory_space=pltpu.VMEM)


def place_of(block):
    y_lo, rest = block // 8, block % 8
    side, k = rest // 4, rest % 4
    return y_lo, side ^ y_lo, k if side == 0 else 3 - k


def block_of(y_lo, y_hi, x):
    side = y_hi ^ y_lo
    return y_lo * 8 + side * 4 + jnp.where(side == 0, x, 3 - x)


def flat(*pairs):
    index = 0
    for coordinate, size in pairs:
        index = index * size + coordinate
    return index


def spread_perm():
    pairs = []
    for y_lo in range(2):
        for z in range(8):
            _, to_y_hi, to_x = place_of(y_lo * 8 + z)
            for s in range(8):
                for core in range(2):
                    to_z = (s + 2 * z + 4 * core) % 8
                    source = flat((y_lo, 2), (z, 8), (s, 8), (core, 2))
                    target = flat((y_lo, 2), (to_z, 8), (to_y_hi, 2), (to_x, 4), (core, 2))
                    pairs.append((source, target))
    return pairs


def ring_perm():
    pairs = []
    for z in range(8):
        for core in range(2):
            there = (z + 1 - 2 * core) % 8
            pairs.append((flat((z, 8), (core, 2)), flat((there, 8), (core, 2))))
    return pairs


def weight_perm():
    pairs = []
    for y in range(4):
        for core in range(2):
            there = (y + 1 - 2 * core) % 4
            source = flat((y % 2, 2), (y // 2, 2), (core, 2))
            pairs.append((source, flat((there % 2, 2), (there // 2, 2), (core, 2))))
    return pairs


def neighbour_perm(cross):
    pairs = []
    for block in range(16):
        for core in range(2):
            if 0 <= block + 1 - 2 * core < 16:
                here, there = place_of(block), place_of(block + 1 - 2 * core)
                source = flat((here[0], 2), (here[1], 2), (here[2], 4), (core ^ cross, 2))
                target = flat((there[0], 2), (there[1], 2), (there[2], 4), (core, 2))
                pairs.append((source, target))
    return pairs


def return_perm(k):
    pairs = []
    for y_lo in range(2):
        for y_hi in range(2):
            for core in range(2):
                source = flat((y_lo, 2), (y_hi, 2), (core, 2))
                pairs.append((source, flat((core, 2), (y_hi ^ k, 2), (y_lo, 2))))
    return pairs


SWAP = [(0, 1), (1, 0)]


def normalized(p):
    lane = lax.broadcasted_iota(jnp.int32, (1, QKV), 1)
    is_q = lane < HEAD_DIM
    is_k = (lane >= HEAD_DIM) & (lane < 2 * HEAD_DIM)
    squares = p * p
    q_mean = jnp.sum(jnp.where(is_q, squares, 0.0), axis=-1, keepdims=True) / HEAD_DIM
    k_mean = jnp.sum(jnp.where(is_k, squares, 0.0), axis=-1, keepdims=True) / HEAD_DIM
    scale = jnp.where(is_q, lax.rsqrt(q_mean + EPS), jnp.where(is_k, lax.rsqrt(k_mean + EPS), 1.0))
    groups = p.shape[0] // (8 * ROWS)
    p = (p * scale).reshape(groups, ROWS, 8, QKV)
    return [p[:, r].reshape(8 * groups, QKV).astype(jnp.bfloat16) for r in range(ROWS)]


def project_kernel(flags, *refs):
    pieces, (own, partner), (keep, send, edge, give, x_ref) = refs[:8], refs[8:10], refs[10:]
    for g, piece in enumerate(pieces):
        x_ref[64 * g : 64 * (g + 1), :] = piece[...]
    p = lax.dot_general(x_ref[...], own[...], NT, preferred_element_type=jnp.float32)
    own_rows = normalized(p)
    p = lax.dot_general(x_ref[...], partner[...], NT, preferred_element_type=jnp.float32)
    other_rows = normalized(p)

    def store(first, second):
        for r in range(ROWS):
            keep[r] = first[r]
            send[r] = second[r]

    @pl.when(flags[0] == 1)
    def _():
        store(own_rows, other_rows)

    @pl.when(flags[0] != 1)
    def _():
        store(other_rows, own_rows)

    def store_edges(top, bottom):
        for r in range(ROWS):
            row = jnp.concatenate([keep[r][:, HEAD_DIM:], send[r][:, HEAD_DIM:]], axis=1)
            (top if r < WIN else bottom)[r % WIN] = row

    @pl.when(flags[1] == 0)
    def _():
        store_edges(give, edge)

    @pl.when(flags[1] != 0)
    def _():
        store_edges(edge, give)


def project(flags, pieces, own, partner):
    whole = jax.ShapeDtypeStruct((ROWS, HALF, QKV), jnp.bfloat16)
    part = jax.ShapeDtypeStruct((WIN, HALF, 4 * HEAD_DIM), jnp.bfloat16)
    return pl.pallas_call(
        project_kernel,
        out_shape=[whole, whole, part, part],
        in_specs=[SMEM] + [VMEM] * 10,
        out_specs=[VMEM] * 4,
        scratch_shapes=[pltpu.VMEM((512, own.shape[1]), jnp.bfloat16)],
        compiler_params=pltpu.CompilerParams(vmem_limit_bytes=20 * MIB),
        cost_estimate=pl.CostEstimate(
            flops=2 * 512 * 960 * 2560, bytes_accessed=8 * MIB, transcendentals=0
        ),
        name="project",
    )(flags, *pieces, own, partner)


def put(ks, vs, first, key, value):
    at = pl.ds(first, key.shape[0])
    ks[at, :] = key
    vs[at, :HEAD_DIM] = value
    is_one = lax.broadcasted_iota(jnp.int32, (key.shape[0], 256 - HEAD_DIM), 1) == 0
    vs[at, HEAD_DIM:] = jnp.where(is_one, 1.0, 0.0).astype(jnp.bfloat16)


def columns(base, core, shape, dim):
    at = lax.broadcasted_iota(jnp.int32, shape, dim)
    side = core ^ (at >> 6)
    g = (at >> 3) & 7
    j = (g + 1) >> 1
    ch = side ^ jnp.where(g == 0, 0, 1 - (g & 1))
    sector = (base + jnp.where(side == 1, j, -j) - 4 * ch) & 7
    return sector * 16 + ch * 8 + (at & 7)


def group_at(sector, ch, base, core):
    i = (sector - base + 4 * ch) & 7
    side = jnp.where((i & 3) == 0, ch, jnp.where(i < 4, 1, 0))
    j = jnp.minimum(i, 8 - i)
    g = jnp.where(i == 0, 0, 2 * j - jnp.where(ch == side, 1, 0))
    return 8 * (side ^ core) + g


def fill_masks(masks, first, query_base, key_base, core, radius):
    square = (COLS, COLS)
    gap = (columns(query_base, core, square, 0) - columns(key_base, core, square, 1) + radius) & (COLS - 1)
    near = jnp.where(gap <= 2 * radius, 1.0, 0.0)
    for d in range(WIN + 1):
        masks[first + d] = jnp.where(radius >= d, near, 0.0)


def shifts(usable, key_base, core):
    square = (COLS, COLS)
    there = lax.broadcasted_iota(jnp.int32, square, 0) == columns(key_base, core, square, 1)
    moved = jnp.dot(usable[...], jnp.where(there, 1.0, 0.0), preferred_element_type=jnp.float32)
    return jnp.where(moved > 0.5, 0.0, -BIG)


def query_of(parts, r):
    return jnp.concatenate([part[r][:, :HEAD_DIM] for part in parts], axis=0)


def scores_of(query, ks, row):
    keys = ks[row * COLS : (row + 1) * COLS, :]
    return lax.dot_general(query, keys, NT, preferred_element_type=jnp.float32)


def inner_kernel(ints, factor_ref, band, usable, *refs):
    parts, (zonal_ref, window_ref, masks_ref, shifts_ref, ks, vs, masks) = refs[:2], refs[2:]
    factor = factor_ref[0]
    start = 0
    for part in parts:
        for r in range(ROWS):
            whole = part[r]
            put(ks, vs, r * COLS + start, whole[:, HEAD_DIM : 2 * HEAD_DIM], whole[:, 2 * HEAD_DIM :])
        start += part.shape[1]
    base, core, radius = ints[0], ints[1], ints[2]
    fill_masks(masks, 0, base, base, core, radius)
    bias = shifts(usable, base, core)
    fill_masks(masks_ref, 0, base, base + 2, core, radius)
    fill_masks(masks_ref, WIN + 1, base, base - 2, core, radius)
    shifts_ref[0] = shifts(usable, base + 2, core)
    shifts_ref[1] = shifts(usable, base - 2, core)
    eye = lax.broadcasted_iota(jnp.int32, (COLS, COLS), 0) == lax.broadcasted_iota(jnp.int32, (COLS, COLS), 1)
    for r in range(ROWS):
        query = query_of(parts, r)
        low, high = max(0, r - WIN), min(ROWS, r + WIN + 1)
        zonal_parts, window_parts = [], []
        for row in range(ROWS):
            shift = bias[WIN + row : WIN + row + 1, :]
            if row == r:
                shift = jnp.where(eye, 0.0, shift)
            weights = jnp.exp2(scores_of(query, ks, row) * factor + shift)
            zonal_parts.append((weights * band[r * ROWS + row]).astype(jnp.bfloat16))
            if low <= row < high:
                window_parts.append((weights * masks[abs(row - r)]).astype(jnp.bfloat16))
        zonal = jnp.dot(jnp.concatenate(zonal_parts, axis=1), vs[...], preferred_element_type=jnp.float32)
        window_ref[r] = jnp.dot(
            jnp.concatenate(window_parts, axis=1),
            vs[low * COLS : high * COLS, :],
            preferred_element_type=jnp.float32,
        )
        zonal_ref[r] = (zonal[:, :HEAD_DIM] / zonal[:, HEAD_DIM : HEAD_DIM + 1]).astype(jnp.bfloat16)


def inner(ints, factor, band, usable, parts):
    return pl.pallas_call(
        inner_kernel,
        out_shape=[
            jax.ShapeDtypeStruct((ROWS, COLS, HEAD_DIM), jnp.bfloat16),
            jax.ShapeDtypeStruct((ROWS, COLS, 256), jnp.float32),
            jax.ShapeDtypeStruct((2 * WIN + 2, COLS, COLS), jnp.float32),
            jax.ShapeDtypeStruct((2, KEY_ROWS, COLS), jnp.float32),
        ],
        in_specs=[SMEM] * 3 + [VMEM] * 3,
        out_specs=[VMEM] * 4,
        scratch_shapes=[
            pltpu.VMEM((ROWS * COLS, HEAD_DIM), jnp.bfloat16),
            pltpu.VMEM((ROWS * COLS, 256), jnp.bfloat16),
            pltpu.VMEM((WIN + 1, COLS, COLS), jnp.float32),
        ],
        compiler_params=pltpu.CompilerParams(vmem_limit_bytes=16 * MIB),
        cost_estimate=pl.CostEstimate(flops=10**7, bytes_accessed=10**5, transcendentals=0),
        name="inner",
    )(ints, factor, band, usable, *parts)


def outer_kernel(ints, factor_ref, zonal_ref, window_ref, masks, shifts_ref, *refs):
    parts, (own, oth, far_own, far_oth), chunks, (ks, vs, out) = refs[:2], refs[2:6], refs[6:8], refs[8:]
    factor = factor_ref[0]
    core = ints[1]
    for edge, side, half, second in ((own, core, 0, 0), (oth, core, 1, 1), (far_own, 1 - core, 1, 1), (far_oth, 1 - core, 0, 0)):
        at = 2 * HEAD_DIM * second
        for r in range(WIN):
            whole = edge[r][:, at : at + 2 * HEAD_DIM]
            first = pl.multiple_of(side * (WIN * COLS) + r * COLS + half * HALF, HALF)
            put(ks, vs, first, whole[:, :HEAD_DIM], whole[:, HEAD_DIM:])
    above, below = shifts_ref[0], shifts_ref[1]
    for r in range(ROWS):
        query = query_of(parts, r)
        rows = range(r, WIN) if r < WIN else range(WIN, r + 1)
        window_parts = []
        for row in rows:
            gap = r + WIN - row if r < WIN else ROWS + row - WIN - r
            shift = above[row : row + 1, :] if r < WIN else below[row + ROWS : row + ROWS + 1, :]
            weights = jnp.exp2(scores_of(query, ks, row) * factor + shift)
            mask = masks[gap] if r < WIN else masks[WIN + 1 + gap]
            window_parts.append((weights * mask).astype(jnp.bfloat16))
        values = vs[rows[0] * COLS : (rows[-1] + 1) * COLS, :]
        window = window_ref[r] + jnp.dot(
            jnp.concatenate(window_parts, axis=1), values, preferred_element_type=jnp.float32
        )
        window = window[:, :HEAD_DIM] / window[:, HEAD_DIM : HEAD_DIM + 1]
        total = window + zonal_ref[r].astype(jnp.float32)
        out[:, :, r * HEAD_DIM : (r + 1) * HEAD_DIM] = total.reshape(16, 8, HEAD_DIM)
    for k in range(8):
        chunks[k // 4][k % 4, 0] = out[ints[3 + k]].astype(jnp.bfloat16)
        chunks[k // 4][k % 4, 1] = out[ints[11 + k]].astype(jnp.bfloat16)


def outer(ints, factor, inner_results, parts, edges):
    chunk = jax.ShapeDtypeStruct((4, 2, 8, ROWS * HEAD_DIM), jnp.bfloat16)
    return pl.pallas_call(
        outer_kernel,
        out_shape=[chunk] * 2,
        in_specs=[SMEM, SMEM] + [VMEM] * 10,
        out_specs=[VMEM] * 2,
        scratch_shapes=[
            pltpu.VMEM((2 * WIN * COLS, HEAD_DIM), jnp.bfloat16),
            pltpu.VMEM((2 * WIN * COLS, 256), jnp.bfloat16),
            pltpu.VMEM((16, 8, ROWS * HEAD_DIM), jnp.float32),
        ],
        compiler_params=pltpu.CompilerParams(vmem_limit_bytes=16 * MIB),
        cost_estimate=pl.CostEstimate(
            flops=10**9, bytes_accessed=4 * MIB, transcendentals=10**6
        ),
        name="outer",
    )(ints, factor, *inner_results, *parts, *edges)


def regroup_kernel(far, near, *parts):
    for k, part in enumerate(parts):
        part[0] = near[k + 1]
        part[1] = far[k + 1]


def regroup(far, near):
    part = jax.ShapeDtypeStruct((2, *near.shape[1:]), near.dtype)
    return pl.pallas_call(
        regroup_kernel,
        out_shape=[part] * 3,
        in_specs=[VMEM] * 2,
        out_specs=[VMEM] * 3,
        compiler_params=pltpu.CompilerParams(vmem_limit_bytes=4 * MIB),
        cost_estimate=pl.CostEstimate(flops=0, bytes_accessed=MIB, transcendentals=0),
        name="regroup",
    )(far, near)


def assemble_kernel(at, *refs):
    width, out = ROWS * HEAD_DIM, refs[10]
    for part in range(2):
        landed = refs[5 * part : 5 * part + 5]
        for k in range(8):
            kind, x = k // 4, k % 4
            value = landed[1 - kind][0, part] if x == 0 else landed[(0, 3, 2, 4)[x]][kind, part]
            out[0, :, pl.ds(pl.multiple_of(at[8 * part + k] * width, 128), width)] = value


def assemble(at, landed):
    return pl.pallas_call(
        assemble_kernel,
        out_shape=jax.ShapeDtypeStruct((1, 8, LAT * ROWS * HEAD_DIM), jnp.bfloat16),
        in_specs=[SMEM] + [VMEM] * 10,
        out_specs=VMEM,
        compiler_params=pltpu.CompilerParams(vmem_limit_bytes=4 * MIB),
        cost_estimate=pl.CostEstimate(flops=0, bytes_accessed=MIB, transcendentals=0),
        name="assemble",
    )(at, *landed)


def body(tokens, w_qkv, key_mask, band_of_row, radius, qk_scale):
    y_lo, z, y_hi, x, core = (lax.axis_index(a) for a in AXES)
    sector = y_hi * 4 + x
    block = block_of(y_lo, y_hi, x)
    head = core * 8 + z
    model = tokens.shape[-1]

    wide = tokens.astype(jnp.float32)
    normed = wide * lax.rsqrt(jnp.mean(wide * wide, axis=-1, keepdims=True) + EPS)
    normed = jnp.transpose(normed.astype(jnp.bfloat16), (1, 0, 2)).reshape(64, model)
    first = lax.ppermute(normed, AXES, spread_perm())

    base = (z - 2 * block) & 7
    padded = jnp.pad(key_mask, ((0, 0), (WIN, WIN)))
    usable = lax.dynamic_slice_in_dim(padded, block * ROWS, KEY_ROWS, 1)
    usable = jnp.transpose(usable).astype(jnp.float32)
    ids = lax.dynamic_slice_in_dim(band_of_row, block * ROWS, ROWS, 0)
    band = (ids[:, None] == ids[None, :]).astype(jnp.float32).reshape(ROWS * ROWS)
    groups = [
        group_at(sector ^ k, side, base, core) for side in (y_lo, 1 - y_lo) for k in range(8)
    ]
    reach = lax.dynamic_index_in_dim(radius, head, keepdims=False)
    ints = jnp.stack([base, core, reach] + groups).astype(jnp.int32)
    factor = lax.dynamic_slice_in_dim(qk_scale, head, 1, 0) / HEAD_DIM * LOG2E
    at = []
    for from_y_lo in (core, 1 - core):
        for k in range(8):
            source = sector ^ k
            at.append(block_of(from_y_lo, source >> 2, source & 3))
    at = jnp.stack(at).astype(jnp.int32)
    flags = jnp.stack([core == y_lo, core]).astype(jnp.int32)

    first, own, usable, band, ints, factor, at, flags = lax.optimization_barrier(
        (first, w_qkv[0], usable, band, ints, factor, at, flags)
    )

    partner = lax.ppermute(own, ("y_lo", "y_hi", "core"), weight_perm())

    a, b = first, lax.ppermute(first, "core", SWAP)
    pieces = [first]
    for k in range(1, 5):
        a = lax.ppermute(a, ("z", "core"), ring_perm())
        pieces.append(a)
        if k < 4:
            b = lax.ppermute(b, ("z", "core"), ring_perm())
            pieces.append(b)

    corners = ("y_lo", "y_hi", "x", "core")
    keep, send, edge, give = project(flags, pieces, own, partner)
    halo_own = lax.ppermute(edge, corners, neighbour_perm(0))
    halo_oth = lax.ppermute(give, corners, neighbour_perm(1))
    parts = keep, lax.ppermute(send, "core", SWAP)
    results = inner(ints, factor, band, usable, parts)
    halo_own, halo_oth, *results = lax.optimization_barrier((halo_own, halo_oth, *results))
    halos = [halo_own, halo_oth] + [lax.ppermute(halo, "core", SWAP) for halo in (halo_own, halo_oth)]
    chunks = outer(ints, factor, results, parts, halos)

    far, near = (lax.ppermute(chunks[k], ("y_lo", "y_hi", "core"), return_perm(k)) for k in (1, 0))
    passed = regroup(far, near)
    landed = [far, near]
    for k in (2, 1, 3):
        landed.append(lax.ppermute(passed[k - 1], "x", [(i, i ^ k) for i in range(4)]))
    return assemble(at, landed + [lax.ppermute(part, "core", SWAP) for part in landed])


def solution(mesh):
    wide = Mesh(mesh.devices.reshape(SIZES), AXES)
    lat, lon = ("y_lo", "z"), ("y_hi", "x", "core")
    in_specs = (P(lon, lat, None), P(lat, None, None), P(), P(), P(), P())
    out_specs = P(lat, lon, None)
    return jax.shard_map(body, mesh=wide, in_specs=in_specs, out_specs=out_specs, check_vma=False)
```

```python
import jax
import jax.numpy as jnp
from jax import lax
from jax.experimental import pallas as pl
from jax.experimental.pallas import tpu as pltpu
from jax.sharding import Mesh, PartitionSpec as P

HEAD_DIM = 160
QKV = 3 * HEAD_DIM
ROWS = 8
WIN = 4
COLS = 128
HALF = COLS // 2
KEY_ROWS = ROWS + 2 * WIN
EARLY = 6
EPS = 1e-06
BIG = 1e30
LOG2E = 1.4426950408889634
LAT, LON = 16, 16
AXES = ("y_lo", "z", "y_hi", "x", "core")
SIZES = (2, 8, 2, 4, 2)
NT = (((1,), (1,)), ((), ()))
MIB = 1024 * 1024
SMEM = pl.BlockSpec(memory_space=pltpu.SMEM)
VMEM = pl.BlockSpec(memory_space=pltpu.VMEM)


def place_of(block):
    y_lo, rest = block // 8, block % 8
    side, k = rest // 4, rest % 4
    return y_lo, side ^ y_lo, k if side == 0 else 3 - k


def block_of(y_lo, y_hi, x):
    side = y_hi ^ y_lo
    return y_lo * 8 + side * 4 + jnp.where(side == 0, x, 3 - x)


def flat(*pairs):
    index = 0
    for coordinate, size in pairs:
        index = index * size + coordinate
    return index


def spread_perm():
    pairs = []
    for y_lo in range(2):
        for z in range(8):
            _, to_y_hi, to_x = place_of(y_lo * 8 + z)
            for s in range(8):
                for core in range(2):
                    to_z = (s + 2 * z + 4 * core) % 8
                    source = flat((y_lo, 2), (z, 8), (s, 8), (core, 2))
                    target = flat((y_lo, 2), (to_z, 8), (to_y_hi, 2), (to_x, 4), (core, 2))
                    pairs.append((source, target))
    return pairs


def ring_perm():
    pairs = []
    for z in range(8):
        for core in range(2):
            there = (z + 1 - 2 * core) % 8
            pairs.append((flat((z, 8), (core, 2)), flat((there, 8), (core, 2))))
    return pairs


def weight_perm():
    pairs = []
    for y in range(4):
        for core in range(2):
            there = (y + 1 - 2 * core) % 4
            source = flat((y % 2, 2), (y // 2, 2), (core, 2))
            pairs.append((source, flat((there % 2, 2), (there // 2, 2), (core, 2))))
    return pairs


def neighbour_perm(cross):
    pairs = []
    for block in range(16):
        for core in range(2):
            if 0 <= block + 1 - 2 * core < 16:
                here, there = place_of(block), place_of(block + 1 - 2 * core)
                source = flat((here[0], 2), (here[1], 2), (here[2], 4), (core ^ cross, 2))
                target = flat((there[0], 2), (there[1], 2), (there[2], 4), (core, 2))
                pairs.append((source, target))
    return pairs


def return_perm(k):
    pairs = []
    for y_lo in range(2):
        for y_hi in range(2):
            for core in range(2):
                source = flat((y_lo, 2), (y_hi, 2), (core, 2))
                pairs.append((source, flat((core, 2), (y_hi ^ k, 2), (y_lo, 2))))
    return pairs


SWAP = [(0, 1), (1, 0)]


def normalized(p):
    lane = lax.broadcasted_iota(jnp.int32, (1, QKV), 1)
    is_q = lane < HEAD_DIM
    is_k = (lane >= HEAD_DIM) & (lane < 2 * HEAD_DIM)
    squares = p * p
    q_mean = jnp.sum(jnp.where(is_q, squares, 0.0), axis=-1, keepdims=True) / HEAD_DIM
    k_mean = jnp.sum(jnp.where(is_k, squares, 0.0), axis=-1, keepdims=True) / HEAD_DIM
    scale = jnp.where(is_q, lax.rsqrt(q_mean + EPS), jnp.where(is_k, lax.rsqrt(k_mean + EPS), 1.0))
    groups = p.shape[0] // (8 * ROWS)
    p = (p * scale).reshape(groups, ROWS, 8, QKV)
    return [p[:, r].reshape(8 * groups, QKV).astype(jnp.bfloat16) for r in range(ROWS)]


def products(flags, pieces, own, partner, x_ref):
    for g, piece in enumerate(pieces):
        x_ref[64 * g : 64 * (g + 1), :] = piece[...]
    return [
        normalized(lax.dot_general(x_ref[...], w[...], NT, preferred_element_type=jnp.float32))
        for w in (own, partner)
    ]


def by_head(flags, rows, store):
    @pl.when(flags[0] == 1)
    def _():
        store(rows[0], rows[1])

    @pl.when(flags[0] != 1)
    def _():
        store(rows[1], rows[0])


def project_first_kernel(flags, *refs):
    pieces, (own, partner, keep, send, x_ref) = refs[:EARLY], refs[EARLY:]

    def store(first, second):
        for r in range(ROWS):
            keep[r] = first[r]
            send[r] = second[r]

    by_head(flags, products(flags, pieces, own, partner, x_ref), store)


def project_last_kernel(flags, *refs):
    pieces, (own, partner, keep_0, send_0, keep, send, edge, give, x_ref) = refs[: 8 - EARLY], refs[8 - EARLY :]
    early = 8 * EARLY
    for r in range(ROWS):
        keep[r, :early] = keep_0[r]
        send[r, :early] = send_0[r]

    def store(first, second):
        for r in range(ROWS):
            keep[r, early:] = first[r]
            send[r, early:] = second[r]

    by_head(flags, products(flags, pieces, own, partner, x_ref), store)

    def store_edges(top, bottom):
        for r in range(ROWS):
            row = jnp.concatenate([keep[r][:, HEAD_DIM:], send[r][:, HEAD_DIM:]], axis=1)
            (top if r < WIN else bottom)[r % WIN] = row

    @pl.when(flags[1] == 0)
    def _():
        store_edges(give, edge)

    @pl.when(flags[1] != 0)
    def _():
        store_edges(edge, give)


def project(flags, pieces, own, partner):
    def call(kernel, shapes, pieces, extra, cost, name):
        return pl.pallas_call(
            kernel,
            out_shape=[jax.ShapeDtypeStruct(shape, jnp.bfloat16) for shape in shapes],
            in_specs=[SMEM] + [VMEM] * (len(pieces) + 2 + len(extra)),
            out_specs=[VMEM] * len(shapes),
            scratch_shapes=[pltpu.VMEM((64 * len(pieces), own.shape[1]), jnp.bfloat16)],
            compiler_params=pltpu.CompilerParams(vmem_limit_bytes=20 * MIB),
            cost_estimate=pl.CostEstimate(flops=cost, bytes_accessed=MIB, transcendentals=0),
            name=name,
        )(flags, *pieces, own, partner, *extra)

    some, whole = (ROWS, 8 * EARLY, QKV), (ROWS, HALF, QKV)
    part = (WIN, HALF, 4 * HEAD_DIM)
    first = call(project_first_kernel, [some] * 2, pieces[:EARLY], [], 2 * 10**10, "project_first")
    return call(project_last_kernel, [whole] * 2 + [part] * 2, pieces[EARLY:], first, 10**8, "project_last")


def put(ks, vs, first, key, value):
    at = pl.ds(first, key.shape[0])
    ks[at, :] = key
    vs[at, :HEAD_DIM] = value
    is_one = lax.broadcasted_iota(jnp.int32, (key.shape[0], 256 - HEAD_DIM), 1) == 0
    vs[at, HEAD_DIM:] = jnp.where(is_one, 1.0, 0.0).astype(jnp.bfloat16)


def columns(base, core, shape, dim):
    at = lax.broadcasted_iota(jnp.int32, shape, dim)
    side = core ^ (at >> 6)
    g = (at >> 3) & 7
    j = (g + 1) >> 1
    ch = side ^ jnp.where(g == 0, 0, 1 - (g & 1))
    sector = (base + jnp.where(side == 1, j, -j) - 4 * ch) & 7
    return sector * 16 + ch * 8 + (at & 7)


def group_at(sector, ch, base, core):
    i = (sector - base + 4 * ch) & 7
    side = jnp.where((i & 3) == 0, ch, jnp.where(i < 4, 1, 0))
    j = jnp.minimum(i, 8 - i)
    g = jnp.where(i == 0, 0, 2 * j - jnp.where(ch == side, 1, 0))
    return 8 * (side ^ core) + g


def fill_masks(masks, first, query_base, key_base, core, radius):
    square = (COLS, COLS)
    gap = (columns(query_base, core, square, 0) - columns(key_base, core, square, 1) + radius) & (COLS - 1)
    near = jnp.where(gap <= 2 * radius, 1.0, 0.0)
    for d in range(WIN + 1):
        masks[first + d] = jnp.where(radius >= d, near, 0.0)


def shifts(usable, key_base, core):
    square = (COLS, COLS)
    there = lax.broadcasted_iota(jnp.int32, square, 0) == columns(key_base, core, square, 1)
    moved = jnp.dot(usable[...], jnp.where(there, 1.0, 0.0), preferred_element_type=jnp.float32)
    return jnp.where(moved > 0.5, 0.0, -BIG)


def query_of(parts, r):
    return jnp.concatenate([part[r][:, :HEAD_DIM] for part in parts], axis=0)


def scores_of(query, ks, row):
    keys = ks[row * COLS : (row + 1) * COLS, :]
    return lax.dot_general(query, keys, NT, preferred_element_type=jnp.float32)


def inner_kernel(ints, factor_ref, band, usable, *refs):
    parts, (zonal_ref, window_ref, masks_ref, shifts_ref, ks, vs, masks) = refs[:2], refs[2:]
    factor = factor_ref[0]
    start = 0
    for part in parts:
        for r in range(ROWS):
            whole = part[r]
            put(ks, vs, r * COLS + start, whole[:, HEAD_DIM : 2 * HEAD_DIM], whole[:, 2 * HEAD_DIM :])
        start += part.shape[1]
    base, core, radius = ints[0], ints[1], ints[2]
    fill_masks(masks, 0, base, base, core, radius)
    bias = shifts(usable, base, core)
    fill_masks(masks_ref, 0, base, base + 2, core, radius)
    fill_masks(masks_ref, WIN + 1, base, base - 2, core, radius)
    shifts_ref[0] = shifts(usable, base + 2, core)
    shifts_ref[1] = shifts(usable, base - 2, core)
    eye = lax.broadcasted_iota(jnp.int32, (COLS, COLS), 0) == lax.broadcasted_iota(jnp.int32, (COLS, COLS), 1)
    for r in range(ROWS):
        query = query_of(parts, r)
        low, high = max(0, r - WIN), min(ROWS, r + WIN + 1)
        zonal_parts, window_parts = [], []
        for row in range(ROWS):
            shift = bias[WIN + row : WIN + row + 1, :]
            if row == r:
                shift = jnp.where(eye, 0.0, shift)
            weights = jnp.exp2(scores_of(query, ks, row) * factor + shift)
            zonal_parts.append((weights * band[r * ROWS + row]).astype(jnp.bfloat16))
            if low <= row < high:
                window_parts.append((weights * masks[abs(row - r)]).astype(jnp.bfloat16))
        zonal = jnp.dot(jnp.concatenate(zonal_parts, axis=1), vs[...], preferred_element_type=jnp.float32)
        window_ref[r] = jnp.dot(
            jnp.concatenate(window_parts, axis=1),
            vs[low * COLS : high * COLS, :],
            preferred_element_type=jnp.float32,
        )
        zonal_ref[r] = (zonal[:, :HEAD_DIM] / zonal[:, HEAD_DIM : HEAD_DIM + 1]).astype(jnp.bfloat16)


def inner(ints, factor, band, usable, parts):
    return pl.pallas_call(
        inner_kernel,
        out_shape=[
            jax.ShapeDtypeStruct((ROWS, COLS, HEAD_DIM), jnp.bfloat16),
            jax.ShapeDtypeStruct((ROWS, COLS, 256), jnp.float32),
            jax.ShapeDtypeStruct((2 * WIN + 2, COLS, COLS), jnp.float32),
            jax.ShapeDtypeStruct((2, KEY_ROWS, COLS), jnp.float32),
        ],
        in_specs=[SMEM] * 3 + [VMEM] * 3,
        out_specs=[VMEM] * 4,
        scratch_shapes=[
            pltpu.VMEM((ROWS * COLS, HEAD_DIM), jnp.bfloat16),
            pltpu.VMEM((ROWS * COLS, 256), jnp.bfloat16),
            pltpu.VMEM((WIN + 1, COLS, COLS), jnp.float32),
        ],
        compiler_params=pltpu.CompilerParams(vmem_limit_bytes=16 * MIB),
        cost_estimate=pl.CostEstimate(flops=10**7, bytes_accessed=10**5, transcendentals=0),
        name="inner",
    )(ints, factor, band, usable, *parts)


def outer_kernel(ints, factor_ref, zonal_ref, window_ref, masks, shifts_ref, *refs):
    parts, (own, oth, far_own, far_oth), chunks, (ks, vs, out) = refs[:2], refs[2:6], refs[6:8], refs[8:]
    factor = factor_ref[0]
    core = ints[1]
    for edge, side, half, second in ((own, core, 0, 0), (oth, core, 1, 1), (far_own, 1 - core, 1, 1), (far_oth, 1 - core, 0, 0)):
        at = 2 * HEAD_DIM * second
        for r in range(WIN):
            whole = edge[r][:, at : at + 2 * HEAD_DIM]
            first = pl.multiple_of(side * (WIN * COLS) + r * COLS + half * HALF, HALF)
            put(ks, vs, first, whole[:, :HEAD_DIM], whole[:, HEAD_DIM:])
    above, below = shifts_ref[0], shifts_ref[1]
    for r in range(ROWS):
        query = query_of(parts, r)
        rows = range(r, WIN) if r < WIN else range(WIN, r + 1)
        window_parts = []
        for row in rows:
            gap = r + WIN - row if r < WIN else ROWS + row - WIN - r
            shift = above[row : row + 1, :] if r < WIN else below[row + ROWS : row + ROWS + 1, :]
            weights = jnp.exp2(scores_of(query, ks, row) * factor + shift)
            mask = masks[gap] if r < WIN else masks[WIN + 1 + gap]
            window_parts.append((weights * mask).astype(jnp.bfloat16))
        values = vs[rows[0] * COLS : (rows[-1] + 1) * COLS, :]
        window = window_ref[r] + jnp.dot(
            jnp.concatenate(window_parts, axis=1), values, preferred_element_type=jnp.float32
        )
        window = window[:, :HEAD_DIM] / window[:, HEAD_DIM : HEAD_DIM + 1]
        total = window + zonal_ref[r].astype(jnp.float32)
        out[:, :, r * HEAD_DIM : (r + 1) * HEAD_DIM] = total.reshape(16, 8, HEAD_DIM)
    for k in range(8):
        chunks[k // 4][k % 4, 0] = out[ints[3 + k]].astype(jnp.bfloat16)
        chunks[k // 4][k % 4, 1] = out[ints[11 + k]].astype(jnp.bfloat16)


def outer(ints, factor, inner_results, parts, edges):
    chunk = jax.ShapeDtypeStruct((4, 2, 8, ROWS * HEAD_DIM), jnp.bfloat16)
    return pl.pallas_call(
        outer_kernel,
        out_shape=[chunk] * 2,
        in_specs=[SMEM, SMEM] + [VMEM] * 10,
        out_specs=[VMEM] * 2,
        scratch_shapes=[
            pltpu.VMEM((2 * WIN * COLS, HEAD_DIM), jnp.bfloat16),
            pltpu.VMEM((2 * WIN * COLS, 256), jnp.bfloat16),
            pltpu.VMEM((16, 8, ROWS * HEAD_DIM), jnp.float32),
        ],
        compiler_params=pltpu.CompilerParams(vmem_limit_bytes=16 * MIB),
        cost_estimate=pl.CostEstimate(
            flops=10**9, bytes_accessed=4 * MIB, transcendentals=10**6
        ),
        name="outer",
    )(ints, factor, *inner_results, *parts, *edges)


def regroup_kernel(far, near, *parts):
    for k, part in enumerate(parts):
        part[0] = near[k + 1]
        part[1] = far[k + 1]


def regroup(far, near):
    part = jax.ShapeDtypeStruct((2, *near.shape[1:]), near.dtype)
    return pl.pallas_call(
        regroup_kernel,
        out_shape=[part] * 3,
        in_specs=[VMEM] * 2,
        out_specs=[VMEM] * 3,
        compiler_params=pltpu.CompilerParams(vmem_limit_bytes=4 * MIB),
        cost_estimate=pl.CostEstimate(flops=0, bytes_accessed=MIB, transcendentals=0),
        name="regroup",
    )(far, near)


def assemble_kernel(at, *refs):
    width, out = ROWS * HEAD_DIM, refs[10]
    for part in range(2):
        landed = refs[5 * part : 5 * part + 5]
        for k in range(8):
            kind, x = k // 4, k % 4
            value = landed[1 - kind][0, part] if x == 0 else landed[(0, 3, 2, 4)[x]][kind, part]
            out[0, :, pl.ds(pl.multiple_of(at[8 * part + k] * width, 128), width)] = value


def assemble(at, landed):
    return pl.pallas_call(
        assemble_kernel,
        out_shape=jax.ShapeDtypeStruct((1, 8, LAT * ROWS * HEAD_DIM), jnp.bfloat16),
        in_specs=[SMEM] + [VMEM] * 10,
        out_specs=VMEM,
        compiler_params=pltpu.CompilerParams(vmem_limit_bytes=4 * MIB),
        cost_estimate=pl.CostEstimate(flops=0, bytes_accessed=MIB, transcendentals=0),
        name="assemble",
    )(at, *landed)


def body(tokens, w_qkv, key_mask, band_of_row, radius, qk_scale):
    y_lo, z, y_hi, x, core = (lax.axis_index(a) for a in AXES)
    sector = y_hi * 4 + x
    block = block_of(y_lo, y_hi, x)
    head = core * 8 + z
    model = tokens.shape[-1]

    wide = tokens.astype(jnp.float32)
    normed = wide * lax.rsqrt(jnp.mean(wide * wide, axis=-1, keepdims=True) + EPS)
    normed = jnp.transpose(normed.astype(jnp.bfloat16), (1, 0, 2)).reshape(64, model)
    first = lax.ppermute(normed, AXES, spread_perm())

    base = (z - 2 * block) & 7
    padded = jnp.pad(key_mask, ((0, 0), (WIN, WIN)))
    usable = lax.dynamic_slice_in_dim(padded, block * ROWS, KEY_ROWS, 1)
    usable = jnp.transpose(usable).astype(jnp.float32)
    ids = lax.dynamic_slice_in_dim(band_of_row, block * ROWS, ROWS, 0)
    band = (ids[:, None] == ids[None, :]).astype(jnp.float32).reshape(ROWS * ROWS)
    groups = [
        group_at(sector ^ k, side, base, core) for side in (y_lo, 1 - y_lo) for k in range(8)
    ]
    reach = lax.dynamic_index_in_dim(radius, head, keepdims=False)
    ints = jnp.stack([base, core, reach] + groups).astype(jnp.int32)
    factor = lax.dynamic_slice_in_dim(qk_scale, head, 1, 0) / HEAD_DIM * LOG2E
    at = []
    for from_y_lo in (core, 1 - core):
        for k in range(8):
            source = sector ^ k
            at.append(block_of(from_y_lo, source >> 2, source & 3))
    at = jnp.stack(at).astype(jnp.int32)
    flags = jnp.stack([core == y_lo, core]).astype(jnp.int32)

    first, own, usable, band, ints, factor, at, flags = lax.optimization_barrier(
        (first, w_qkv[0], usable, band, ints, factor, at, flags)
    )

    partner = lax.ppermute(own, ("y_lo", "y_hi", "core"), weight_perm())

    a, b = first, lax.ppermute(first, "core", SWAP)
    pieces = [first]
    for k in range(1, 5):
        a = lax.ppermute(a, ("z", "core"), ring_perm())
        pieces.append(a)
        if k < 4:
            b = lax.ppermute(b, ("z", "core"), ring_perm())
            pieces.append(b)

    corners = ("y_lo", "y_hi", "x", "core")
    keep, send, edge, give = project(flags, pieces, own, partner)
    halo_own = lax.ppermute(edge, corners, neighbour_perm(0))
    halo_oth = lax.ppermute(give, corners, neighbour_perm(1))
    parts = keep, lax.ppermute(send, "core", SWAP)
    results = inner(ints, factor, band, usable, parts)
    halo_own, halo_oth, *results = lax.optimization_barrier((halo_own, halo_oth, *results))
    halos = [halo_own, halo_oth] + [lax.ppermute(halo, "core", SWAP) for halo in (halo_own, halo_oth)]
    chunks = outer(ints, factor, results, parts, halos)

    far, near = (lax.ppermute(chunks[k], ("y_lo", "y_hi", "core"), return_perm(k)) for k in (1, 0))
    passed = regroup(far, near)
    landed = [far, near]
    for k in (2, 1, 3):
        landed.append(lax.ppermute(passed[k - 1], "x", [(i, i ^ k) for i in range(4)]))
    return assemble(at, landed + [lax.ppermute(part, "core", SWAP) for part in landed])


def solution(mesh):
    wide = Mesh(mesh.devices.reshape(SIZES), AXES)
    lat, lon = ("y_lo", "z"), ("y_hi", "x", "core")
    in_specs = (P(lon, lat, None), P(lat, None, None), P(), P(), P(), P())
    out_specs = P(lat, lon, None)
    return jax.shard_map(body, mesh=wide, in_specs=in_specs, out_specs=out_specs, check_vma=False)
```

```python
import jax
import jax.numpy as jnp
from jax import lax
from jax.experimental import pallas as pl
from jax.experimental.pallas import tpu as pltpu
from jax.sharding import Mesh, PartitionSpec as P

HEAD_DIM = 160
QKV = 3 * HEAD_DIM
ROWS = 8
WIN = 4
COLS = 128
HALF = COLS // 2
KEY_ROWS = ROWS + 2 * WIN
EARLY = 6
EPS = 1e-06
BIG = 1e30
LOG2E = 1.4426950408889634
LAT, LON = 16, 16
AXES = ("y_lo", "z", "y_hi", "x", "core")
SIZES = (2, 8, 2, 4, 2)
NT = (((1,), (1,)), ((), ()))
MIB = 1024 * 1024
SMEM = pl.BlockSpec(memory_space=pltpu.SMEM)
VMEM = pl.BlockSpec(memory_space=pltpu.VMEM)


def place_of(block):
    y_lo, rest = block // 8, block % 8
    side, k = rest // 4, rest % 4
    return y_lo, side ^ y_lo, k if side == 0 else 3 - k


def block_of(y_lo, y_hi, x):
    side = y_hi ^ y_lo
    return y_lo * 8 + side * 4 + jnp.where(side == 0, x, 3 - x)


def flat(*pairs):
    index = 0
    for coordinate, size in pairs:
        index = index * size + coordinate
    return index


def spread_perm():
    pairs = []
    for y_lo in range(2):
        for z in range(8):
            _, to_y_hi, to_x = place_of(y_lo * 8 + z)
            for s in range(8):
                for core in range(2):
                    to_z = (s + 2 * z + 4 * core) % 8
                    source = flat((y_lo, 2), (z, 8), (s, 8), (core, 2))
                    target = flat((y_lo, 2), (to_z, 8), (to_y_hi, 2), (to_x, 4), (core, 2))
                    pairs.append((source, target))
    return pairs


def ring_perm():
    pairs = []
    for z in range(8):
        for core in range(2):
            there = (z + 1 - 2 * core) % 8
            pairs.append((flat((z, 8), (core, 2)), flat((there, 8), (core, 2))))
    return pairs


def weight_perm():
    pairs = []
    for y in range(4):
        for core in range(2):
            there = (y + 1 - 2 * core) % 4
            source = flat((y % 2, 2), (y // 2, 2), (core, 2))
            pairs.append((source, flat((there % 2, 2), (there // 2, 2), (core, 2))))
    return pairs


def neighbour_perm(cross):
    pairs = []
    for block in range(16):
        for core in range(2):
            if 0 <= block + 1 - 2 * core < 16:
                here, there = place_of(block), place_of(block + 1 - 2 * core)
                source = flat((here[0], 2), (here[1], 2), (here[2], 4), (core ^ cross, 2))
                target = flat((there[0], 2), (there[1], 2), (there[2], 4), (core, 2))
                pairs.append((source, target))
    return pairs


def return_perm(k):
    pairs = []
    for y_lo in range(2):
        for y_hi in range(2):
            for core in range(2):
                source = flat((y_lo, 2), (y_hi, 2), (core, 2))
                pairs.append((source, flat((core, 2), (y_hi ^ k, 2), (y_lo, 2))))
    return pairs


SWAP = [(0, 1), (1, 0)]


def normalize_kernel(tokens, normed):
    wide = tokens[...].astype(jnp.float32)
    wide = wide * lax.rsqrt(jnp.mean(wide * wide, axis=-1, keepdims=True) + EPS)
    for r in range(0, ROWS, 2):
        pair = jnp.concatenate([wide[:, r], wide[:, r + 1]], axis=0)
        normed[8 * r : 8 * r + 16, :] = pair.astype(jnp.bfloat16)


def normalize(tokens):
    columns, rows, model = tokens.shape
    return pl.pallas_call(
        normalize_kernel,
        out_shape=jax.ShapeDtypeStruct((columns * rows, model), jnp.bfloat16),
        in_specs=[VMEM],
        out_specs=VMEM,
        compiler_params=pltpu.CompilerParams(vmem_limit_bytes=8 * MIB),
        name="normalize",
    )(tokens)


def normalized(p):
    lane = lax.broadcasted_iota(jnp.int32, (1, QKV), 1)
    is_q = lane < HEAD_DIM
    is_k = (lane >= HEAD_DIM) & (lane < 2 * HEAD_DIM)
    squares = p * p
    q_mean = jnp.sum(jnp.where(is_q, squares, 0.0), axis=-1, keepdims=True) / HEAD_DIM
    k_mean = jnp.sum(jnp.where(is_k, squares, 0.0), axis=-1, keepdims=True) / HEAD_DIM
    scale = jnp.where(is_q, lax.rsqrt(q_mean + EPS), jnp.where(is_k, lax.rsqrt(k_mean + EPS), 1.0))
    groups = p.shape[0] // (8 * ROWS)
    p = (p * scale).reshape(groups, ROWS, 8, QKV)
    return [p[:, r].reshape(8 * groups, QKV).astype(jnp.bfloat16) for r in range(ROWS)]


def products(flags, pieces, own, partner, x_ref):
    for g, piece in enumerate(pieces):
        x_ref[64 * g : 64 * (g + 1), :] = piece[...]
    return [
        normalized(lax.dot_general(x_ref[...], w[...], NT, preferred_element_type=jnp.float32))
        for w in (own, partner)
    ]


def by_head(flags, rows, store):
    @pl.when(flags[0] == 1)
    def _():
        store(rows[0], rows[1])

    @pl.when(flags[0] != 1)
    def _():
        store(rows[1], rows[0])


def project_first_kernel(flags, *refs):
    pieces, (own, partner, keep, send, x_ref) = refs[:EARLY], refs[EARLY:]

    def store(first, second):
        for r in range(ROWS):
            keep[r] = first[r]
            send[r] = second[r]

    by_head(flags, products(flags, pieces, own, partner, x_ref), store)


def project_last_kernel(flags, *refs):
    pieces, (own, partner, keep_0, send_0, keep, send, edge, give, x_ref) = refs[: 8 - EARLY], refs[8 - EARLY :]
    early = 8 * EARLY
    for r in range(ROWS):
        keep[r, :early] = keep_0[r]
        send[r, :early] = send_0[r]

    def store(first, second):
        for r in range(ROWS):
            keep[r, early:] = first[r]
            send[r, early:] = second[r]

    by_head(flags, products(flags, pieces, own, partner, x_ref), store)

    def store_edges(top, bottom):
        for r in range(ROWS):
            row = jnp.concatenate([keep[r][:, HEAD_DIM:], send[r][:, HEAD_DIM:]], axis=1)
            (top if r < WIN else bottom)[r % WIN] = row

    @pl.when(flags[1] == 0)
    def _():
        store_edges(give, edge)

    @pl.when(flags[1] != 0)
    def _():
        store_edges(edge, give)


def project(flags, pieces, own, partner):
    def call(kernel, shapes, pieces, extra, cost, name):
        return pl.pallas_call(
            kernel,
            out_shape=[jax.ShapeDtypeStruct(shape, jnp.bfloat16) for shape in shapes],
            in_specs=[SMEM] + [VMEM] * (len(pieces) + 2 + len(extra)),
            out_specs=[VMEM] * len(shapes),
            scratch_shapes=[pltpu.VMEM((64 * len(pieces), own.shape[1]), jnp.bfloat16)],
            compiler_params=pltpu.CompilerParams(vmem_limit_bytes=20 * MIB),
            cost_estimate=pl.CostEstimate(flops=cost, bytes_accessed=MIB, transcendentals=0),
            name=name,
        )(flags, *pieces, own, partner, *extra)

    some, whole = (ROWS, 8 * EARLY, QKV), (ROWS, HALF, QKV)
    part = (WIN, HALF, 4 * HEAD_DIM)
    first = call(project_first_kernel, [some] * 2, pieces[:EARLY], [], 2 * 10**10, "project_first")
    return call(project_last_kernel, [whole] * 2 + [part] * 2, pieces[EARLY:], first, 10**8, "project_last")


def put(ks, vs, first, key, value):
    at = pl.ds(first, key.shape[0])
    ks[at, :] = key
    vs[at, :HEAD_DIM] = value
    is_one = lax.broadcasted_iota(jnp.int32, (key.shape[0], 256 - HEAD_DIM), 1) == 0
    vs[at, HEAD_DIM:] = jnp.where(is_one, 1.0, 0.0).astype(jnp.bfloat16)


def columns(base, core, shape, dim):
    at = lax.broadcasted_iota(jnp.int32, shape, dim)
    side = core ^ (at >> 6)
    g = (at >> 3) & 7
    j = (g + 1) >> 1
    ch = side ^ jnp.where(g == 0, 0, 1 - (g & 1))
    sector = (base + jnp.where(side == 1, j, -j) - 4 * ch) & 7
    return sector * 16 + ch * 8 + (at & 7)


def group_at(sector, ch, base, core):
    i = (sector - base + 4 * ch) & 7
    side = jnp.where((i & 3) == 0, ch, jnp.where(i < 4, 1, 0))
    j = jnp.minimum(i, 8 - i)
    g = jnp.where(i == 0, 0, 2 * j - jnp.where(ch == side, 1, 0))
    return 8 * (side ^ core) + g


def fill_masks(masks, first, query_base, key_base, core, radius):
    square = (COLS, COLS)
    gap = (columns(query_base, core, square, 0) - columns(key_base, core, square, 1) + radius) & (COLS - 1)
    near = jnp.where(gap <= 2 * radius, 1.0, 0.0)
    for d in range(WIN + 1):
        masks[first + d] = jnp.where(radius >= d, near, 0.0)


def shifts(usable, key_base, core):
    square = (COLS, COLS)
    there = lax.broadcasted_iota(jnp.int32, square, 0) == columns(key_base, core, square, 1)
    moved = jnp.dot(usable[...], jnp.where(there, 1.0, 0.0), preferred_element_type=jnp.float32)
    return jnp.where(moved > 0.5, 0.0, -BIG)


def query_of(parts, r):
    return jnp.concatenate([part[r][:, :HEAD_DIM] for part in parts], axis=0)


def scores_of(query, ks, row):
    keys = ks[row * COLS : (row + 1) * COLS, :]
    return lax.dot_general(query, keys, NT, preferred_element_type=jnp.float32)


def inner_kernel(ints, factor_ref, band, usable, *refs):
    parts, (zonal_ref, window_ref, masks_ref, shifts_ref, ks, vs, masks) = refs[:2], refs[2:]
    factor = factor_ref[0]
    start = 0
    for part in parts:
        for r in range(ROWS):
            whole = part[r]
            put(ks, vs, r * COLS + start, whole[:, HEAD_DIM : 2 * HEAD_DIM], whole[:, 2 * HEAD_DIM :])
        start += part.shape[1]
    base, core, radius = ints[0], ints[1], ints[2]
    fill_masks(masks, 0, base, base, core, radius)
    bias = shifts(usable, base, core)
    fill_masks(masks_ref, 0, base, base + 2, core, radius)
    fill_masks(masks_ref, WIN + 1, base, base - 2, core, radius)
    shifts_ref[0] = shifts(usable, base + 2, core)
    shifts_ref[1] = shifts(usable, base - 2, core)
    eye = lax.broadcasted_iota(jnp.int32, (COLS, COLS), 0) == lax.broadcasted_iota(jnp.int32, (COLS, COLS), 1)
    for r in range(ROWS):
        query = query_of(parts, r)
        low, high = max(0, r - WIN), min(ROWS, r + WIN + 1)
        zonal_parts, window_parts = [], []
        for row in range(ROWS):
            shift = bias[WIN + row : WIN + row + 1, :]
            if row == r:
                shift = jnp.where(eye, 0.0, shift)
            weights = jnp.exp2(scores_of(query, ks, row) * factor + shift)
            zonal_parts.append((weights * band[r * ROWS + row]).astype(jnp.bfloat16))
            if low <= row < high:
                window_parts.append((weights * masks[abs(row - r)]).astype(jnp.bfloat16))
        zonal = jnp.dot(jnp.concatenate(zonal_parts, axis=1), vs[...], preferred_element_type=jnp.float32)
        window_ref[r] = jnp.dot(
            jnp.concatenate(window_parts, axis=1),
            vs[low * COLS : high * COLS, :],
            preferred_element_type=jnp.float32,
        )
        zonal_ref[r] = (zonal[:, :HEAD_DIM] / zonal[:, HEAD_DIM : HEAD_DIM + 1]).astype(jnp.bfloat16)


def inner(ints, factor, band, usable, parts):
    return pl.pallas_call(
        inner_kernel,
        out_shape=[
            jax.ShapeDtypeStruct((ROWS, COLS, HEAD_DIM), jnp.bfloat16),
            jax.ShapeDtypeStruct((ROWS, COLS, 256), jnp.float32),
            jax.ShapeDtypeStruct((2 * WIN + 2, COLS, COLS), jnp.float32),
            jax.ShapeDtypeStruct((2, KEY_ROWS, COLS), jnp.float32),
        ],
        in_specs=[SMEM] * 3 + [VMEM] * 3,
        out_specs=[VMEM] * 4,
        scratch_shapes=[
            pltpu.VMEM((ROWS * COLS, HEAD_DIM), jnp.bfloat16),
            pltpu.VMEM((ROWS * COLS, 256), jnp.bfloat16),
            pltpu.VMEM((WIN + 1, COLS, COLS), jnp.float32),
        ],
        compiler_params=pltpu.CompilerParams(vmem_limit_bytes=16 * MIB),
        cost_estimate=pl.CostEstimate(flops=10**7, bytes_accessed=10**5, transcendentals=0),
        name="inner",
    )(ints, factor, band, usable, *parts)


def outer_kernel(ints, factor_ref, zonal_ref, window_ref, masks, shifts_ref, *refs):
    parts, (own, oth, far_own, far_oth), chunks, (ks, vs, out) = refs[:2], refs[2:6], refs[6:8], refs[8:]
    factor = factor_ref[0]
    core = ints[1]
    for edge, side, half, second in ((own, core, 0, 0), (oth, core, 1, 1), (far_own, 1 - core, 1, 1), (far_oth, 1 - core, 0, 0)):
        at = 2 * HEAD_DIM * second
        for r in range(WIN):
            whole = edge[r][:, at : at + 2 * HEAD_DIM]
            first = pl.multiple_of(side * (WIN * COLS) + r * COLS + half * HALF, HALF)
            put(ks, vs, first, whole[:, :HEAD_DIM], whole[:, HEAD_DIM:])
    above, below = shifts_ref[0], shifts_ref[1]
    for r in range(ROWS):
        query = query_of(parts, r)
        rows = range(r, WIN) if r < WIN else range(WIN, r + 1)
        window_parts = []
        for row in rows:
            gap = r + WIN - row if r < WIN else ROWS + row - WIN - r
            shift = above[row : row + 1, :] if r < WIN else below[row + ROWS : row + ROWS + 1, :]
            weights = jnp.exp2(scores_of(query, ks, row) * factor + shift)
            mask = masks[gap] if r < WIN else masks[WIN + 1 + gap]
            window_parts.append((weights * mask).astype(jnp.bfloat16))
        values = vs[rows[0] * COLS : (rows[-1] + 1) * COLS, :]
        window = window_ref[r] + jnp.dot(
            jnp.concatenate(window_parts, axis=1), values, preferred_element_type=jnp.float32
        )
        window = window[:, :HEAD_DIM] / window[:, HEAD_DIM : HEAD_DIM + 1]
        total = window + zonal_ref[r].astype(jnp.float32)
        out[:, :, r * HEAD_DIM : (r + 1) * HEAD_DIM] = total.reshape(16, 8, HEAD_DIM)
    for k in range(8):
        chunks[k // 4][k % 4, 0] = out[ints[3 + k]].astype(jnp.bfloat16)
        chunks[k // 4][k % 4, 1] = out[ints[11 + k]].astype(jnp.bfloat16)


def outer(ints, factor, inner_results, parts, edges):
    chunk = jax.ShapeDtypeStruct((4, 2, 8, ROWS * HEAD_DIM), jnp.bfloat16)
    return pl.pallas_call(
        outer_kernel,
        out_shape=[chunk] * 2,
        in_specs=[SMEM, SMEM] + [VMEM] * 10,
        out_specs=[VMEM] * 2,
        scratch_shapes=[
            pltpu.VMEM((2 * WIN * COLS, HEAD_DIM), jnp.bfloat16),
            pltpu.VMEM((2 * WIN * COLS, 256), jnp.bfloat16),
            pltpu.VMEM((16, 8, ROWS * HEAD_DIM), jnp.float32),
        ],
        compiler_params=pltpu.CompilerParams(vmem_limit_bytes=16 * MIB),
        cost_estimate=pl.CostEstimate(
            flops=10**9, bytes_accessed=4 * MIB, transcendentals=10**6
        ),
        name="outer",
    )(ints, factor, *inner_results, *parts, *edges)


def regroup_kernel(far, near, *parts):
    for k, part in enumerate(parts):
        part[0] = near[k + 1]
        part[1] = far[k + 1]


def regroup(far, near):
    part = jax.ShapeDtypeStruct((2, *near.shape[1:]), near.dtype)
    return pl.pallas_call(
        regroup_kernel,
        out_shape=[part] * 3,
        in_specs=[VMEM] * 2,
        out_specs=[VMEM] * 3,
        compiler_params=pltpu.CompilerParams(vmem_limit_bytes=4 * MIB),
        cost_estimate=pl.CostEstimate(flops=0, bytes_accessed=MIB, transcendentals=0),
        name="regroup",
    )(far, near)


def assemble_kernel(at, *refs):
    width, out = ROWS * HEAD_DIM, refs[10]
    for part in range(2):
        landed = refs[5 * part : 5 * part + 5]
        for k in range(8):
            kind, x = k // 4, k % 4
            value = landed[1 - kind][0, part] if x == 0 else landed[(0, 3, 2, 4)[x]][kind, part]
            out[0, :, pl.ds(pl.multiple_of(at[8 * part + k] * width, 128), width)] = value


def assemble(at, landed):
    return pl.pallas_call(
        assemble_kernel,
        out_shape=jax.ShapeDtypeStruct((1, 8, LAT * ROWS * HEAD_DIM), jnp.bfloat16),
        in_specs=[SMEM] + [VMEM] * 10,
        out_specs=VMEM,
        compiler_params=pltpu.CompilerParams(vmem_limit_bytes=4 * MIB),
        cost_estimate=pl.CostEstimate(flops=0, bytes_accessed=MIB, transcendentals=0),
        name="assemble",
    )(at, *landed)


def body(tokens, w_qkv, key_mask, band_of_row, radius, qk_scale):
    y_lo, z, y_hi, x, core = (lax.axis_index(a) for a in AXES)
    sector = y_hi * 4 + x
    block = block_of(y_lo, y_hi, x)
    head = core * 8 + z

    normed = normalize(tokens)
    first = lax.ppermute(normed, AXES, spread_perm())

    base = (z - 2 * block) & 7
    padded = jnp.pad(key_mask, ((0, 0), (WIN, WIN)))
    usable = lax.dynamic_slice_in_dim(padded, block * ROWS, KEY_ROWS, 1)
    usable = jnp.transpose(usable).astype(jnp.float32)
    ids = lax.dynamic_slice_in_dim(band_of_row, block * ROWS, ROWS, 0)
    band = (ids[:, None] == ids[None, :]).astype(jnp.float32).reshape(ROWS * ROWS)
    groups = [
        group_at(sector ^ k, side, base, core) for side in (y_lo, 1 - y_lo) for k in range(8)
    ]
    reach = lax.dynamic_index_in_dim(radius, head, keepdims=False)
    ints = jnp.stack([base, core, reach] + groups).astype(jnp.int32)
    factor = lax.dynamic_slice_in_dim(qk_scale, head, 1, 0) / HEAD_DIM * LOG2E
    at = []
    for from_y_lo in (core, 1 - core):
        for k in range(8):
            source = sector ^ k
            at.append(block_of(from_y_lo, source >> 2, source & 3))
    at = jnp.stack(at).astype(jnp.int32)
    flags = jnp.stack([core == y_lo, core]).astype(jnp.int32)

    first, own, usable, band, ints, factor, at, flags = lax.optimization_barrier(
        (first, w_qkv[0], usable, band, ints, factor, at, flags)
    )

    partner = lax.ppermute(own, ("y_lo", "y_hi", "core"), weight_perm())

    a, b = first, lax.ppermute(first, "core", SWAP)
    pieces = [first]
    for k in range(1, 5):
        a = lax.ppermute(a, ("z", "core"), ring_perm())
        pieces.append(a)
        if k < 4:
            b = lax.ppermute(b, ("z", "core"), ring_perm())
            pieces.append(b)

    corners = ("y_lo", "y_hi", "x", "core")
    keep, send, edge, give = project(flags, pieces, own, partner)
    halo_own = lax.ppermute(edge, corners, neighbour_perm(0))
    halo_oth = lax.ppermute(give, corners, neighbour_perm(1))
    parts = keep, lax.ppermute(send, "core", SWAP)
    results = inner(ints, factor, band, usable, parts)
    halos, far = [], []
    for halo in (halo_own, halo_oth):
        halo, *results = lax.optimization_barrier((halo, *results))
        halos.append(halo)
        far.append(lax.ppermute(halo, "core", SWAP))
    halos += far
    chunks = outer(ints, factor, results, parts, halos)

    far, near = (lax.ppermute(chunks[k], ("y_lo", "y_hi", "core"), return_perm(k)) for k in (1, 0))
    passed = regroup(far, near)
    landed = [far, near]
    for k in (2, 1, 3):
        landed.append(lax.ppermute(passed[k - 1], "x", [(i, i ^ k) for i in range(4)]))
    return assemble(at, landed + [lax.ppermute(part, "core", SWAP) for part in landed])


def solution(mesh):
    wide = Mesh(mesh.devices.reshape(SIZES), AXES)
    lat, lon = ("y_lo", "z"), ("y_hi", "x", "core")
    in_specs = (P(lon, lat, None), P(lat, None, None), P(), P(), P(), P())
    out_specs = P(lat, lon, None)
    return jax.shard_map(body, mesh=wide, in_specs=in_specs, out_specs=out_specs, check_vma=False)
```

```python
import jax
import jax.numpy as jnp
from jax import lax
from jax.experimental import pallas as pl
from jax.experimental.pallas import tpu as pltpu
from jax.sharding import Mesh, PartitionSpec as P

HEAD_DIM = 160
QKV = 3 * HEAD_DIM
ROWS = 8
WIN = 4
COLS = 128
HALF = COLS // 2
KEY_ROWS = ROWS + 2 * WIN
EARLY = 6
EPS = 1e-06
BIG = 1e30
LOG2E = 1.4426950408889634
LAT, LON = 16, 16
AXES = ("y_lo", "z", "y_hi", "x", "core")
SIZES = (2, 8, 2, 4, 2)
NT = (((1,), (1,)), ((), ()))
MIB = 1024 * 1024
SMEM = pl.BlockSpec(memory_space=pltpu.SMEM)
VMEM = pl.BlockSpec(memory_space=pltpu.VMEM)


def place_of(block):
    y_lo, rest = block // 8, block % 8
    side, k = rest // 4, rest % 4
    return y_lo, side ^ y_lo, k if side == 0 else 3 - k


def block_of(y_lo, y_hi, x):
    side = y_hi ^ y_lo
    return y_lo * 8 + side * 4 + jnp.where(side == 0, x, 3 - x)


def flat(*pairs):
    index = 0
    for coordinate, size in pairs:
        index = index * size + coordinate
    return index


def spread_perm():
    pairs = []
    for y_lo in range(2):
        for z in range(8):
            _, to_y_hi, to_x = place_of(y_lo * 8 + z)
            for s in range(8):
                for core in range(2):
                    to_z = (s + 2 * z + 4 * core) % 8
                    source = flat((y_lo, 2), (z, 8), (s, 8), (core, 2))
                    target = flat((y_lo, 2), (to_z, 8), (to_y_hi, 2), (to_x, 4), (core, 2))
                    pairs.append((source, target))
    return pairs


def ring_perm():
    pairs = []
    for z in range(8):
        for core in range(2):
            there = (z + 1 - 2 * core) % 8
            pairs.append((flat((z, 8), (core, 2)), flat((there, 8), (core, 2))))
    return pairs


def weight_perm():
    pairs = []
    for y in range(4):
        for core in range(2):
            there = (y + 1 - 2 * core) % 4
            source = flat((y % 2, 2), (y // 2, 2), (core, 2))
            pairs.append((source, flat((there % 2, 2), (there // 2, 2), (core, 2))))
    return pairs


def neighbour_perm(cross):
    pairs = []
    for block in range(16):
        for core in range(2):
            if 0 <= block + 1 - 2 * core < 16:
                here, there = place_of(block), place_of(block + 1 - 2 * core)
                source = flat((here[0], 2), (here[1], 2), (here[2], 4), (core ^ cross, 2))
                target = flat((there[0], 2), (there[1], 2), (there[2], 4), (core, 2))
                pairs.append((source, target))
    return pairs


def return_perm(k):
    pairs = []
    for y_lo in range(2):
        for y_hi in range(2):
            for core in range(2):
                source = flat((y_lo, 2), (y_hi, 2), (core, 2))
                pairs.append((source, flat((core, 2), (y_hi ^ k, 2), (y_lo, 2))))
    return pairs


SWAP = [(0, 1), (1, 0)]


def normalize_kernel(tokens, normed):
    wide = tokens[...].astype(jnp.float32)
    wide = wide * lax.rsqrt(jnp.mean(wide * wide, axis=-1, keepdims=True) + EPS)
    for r in range(0, ROWS, 2):
        pair = jnp.concatenate([wide[:, r], wide[:, r + 1]], axis=0)
        normed[8 * r : 8 * r + 16, :] = pair.astype(jnp.bfloat16)


def normalize(tokens):
    columns, rows, model = tokens.shape
    return pl.pallas_call(
        normalize_kernel,
        out_shape=jax.ShapeDtypeStruct((columns * rows, model), jnp.bfloat16),
        in_specs=[VMEM],
        out_specs=VMEM,
        compiler_params=pltpu.CompilerParams(vmem_limit_bytes=8 * MIB),
        name="normalize",
    )(tokens)


def normalized(p):
    lane = lax.broadcasted_iota(jnp.int32, (1, QKV), 1)
    is_q = lane < HEAD_DIM
    is_k = (lane >= HEAD_DIM) & (lane < 2 * HEAD_DIM)
    squares = p * p
    q_mean = jnp.sum(jnp.where(is_q, squares, 0.0), axis=-1, keepdims=True) / HEAD_DIM
    k_mean = jnp.sum(jnp.where(is_k, squares, 0.0), axis=-1, keepdims=True) / HEAD_DIM
    scale = jnp.where(is_q, lax.rsqrt(q_mean + EPS), jnp.where(is_k, lax.rsqrt(k_mean + EPS), 1.0))
    groups = p.shape[0] // (8 * ROWS)
    p = (p * scale).reshape(groups, ROWS, 8, QKV)
    return [p[:, r].reshape(8 * groups, QKV).astype(jnp.bfloat16) for r in range(ROWS)]


def gather(pieces, x_ref):
    for g, piece in enumerate(pieces):
        x_ref[64 * g : 64 * (g + 1), :] = piece[...]


def product(x, w):
    return normalized(lax.dot_general(x, w[...], NT, preferred_element_type=jnp.float32))


def project_first_kernel(*refs):
    pieces, (own, rows, x_ref) = refs[:EARLY], refs[EARLY:]
    gather(pieces, x_ref)
    for r, row in enumerate(product(x_ref[...], own)):
        rows[r] = row


def project_last_kernel(flags, *refs):
    pieces, (own, partner, own_0, keep, send, edge, give, x_ref) = refs[:8], refs[8:]
    early = 8 * EARLY
    gather(pieces, x_ref)
    partner_rows = product(x_ref[...], partner)
    own_rows = product(x_ref[64 * EARLY :, :], own)

    def store(of_own, of_partner):
        for r in range(ROWS):
            of_own[r, :early] = own_0[r]
            of_own[r, early:] = own_rows[r]
            of_partner[r] = partner_rows[r]

    @pl.when(flags[0] == 1)
    def _():
        store(keep, send)

    @pl.when(flags[0] != 1)
    def _():
        store(send, keep)

    def store_edges(top, bottom):
        for r in range(ROWS):
            row = jnp.concatenate([keep[r][:, HEAD_DIM:], send[r][:, HEAD_DIM:]], axis=1)
            (top if r < WIN else bottom)[r % WIN] = row

    @pl.when(flags[1] == 0)
    def _():
        store_edges(give, edge)

    @pl.when(flags[1] != 0)
    def _():
        store_edges(edge, give)


def project(flags, pieces, own, partner):
    def call(kernel, shapes, tokens, operands, specs, cost, name):
        return pl.pallas_call(
            kernel,
            out_shape=[jax.ShapeDtypeStruct(shape, jnp.bfloat16) for shape in shapes],
            in_specs=specs + [VMEM] * (len(operands) - len(specs)),
            out_specs=[VMEM] * len(shapes),
            scratch_shapes=[pltpu.VMEM((tokens, own.shape[1]), jnp.bfloat16)],
            compiler_params=pltpu.CompilerParams(vmem_limit_bytes=20 * MIB),
            cost_estimate=pl.CostEstimate(flops=cost, bytes_accessed=MIB, transcendentals=0),
            name=name,
        )(*operands)

    some, whole = (ROWS, 8 * EARLY, QKV), (ROWS, HALF, QKV)
    part = (WIN, HALF, 4 * HEAD_DIM)
    operands = [*pieces[:EARLY], own]
    (own_0,) = call(project_first_kernel, [some], 64 * EARLY, operands, [], 3 * 10**9, "project_first")
    operands = [flags, *pieces, own, partner, own_0]
    return call(project_last_kernel, [whole] * 2 + [part] * 2, 512, operands, [SMEM], 10**8, "project_last")


def put(ks, vs, first, key, value):
    at = pl.ds(first, key.shape[0])
    ks[at, :] = key
    vs[at, :HEAD_DIM] = value
    is_one = lax.broadcasted_iota(jnp.int32, (key.shape[0], 256 - HEAD_DIM), 1) == 0
    vs[at, HEAD_DIM:] = jnp.where(is_one, 1.0, 0.0).astype(jnp.bfloat16)


def columns(base, core, shape, dim):
    at = lax.broadcasted_iota(jnp.int32, shape, dim)
    side = core ^ (at >> 6)
    g = (at >> 3) & 7
    j = (g + 1) >> 1
    ch = side ^ jnp.where(g == 0, 0, 1 - (g & 1))
    sector = (base + jnp.where(side == 1, j, -j) - 4 * ch) & 7
    return sector * 16 + ch * 8 + (at & 7)


def group_at(sector, ch, base, core):
    i = (sector - base + 4 * ch) & 7
    side = jnp.where((i & 3) == 0, ch, jnp.where(i < 4, 1, 0))
    j = jnp.minimum(i, 8 - i)
    g = jnp.where(i == 0, 0, 2 * j - jnp.where(ch == side, 1, 0))
    return 8 * (side ^ core) + g


def fill_masks(masks, first, query_base, key_base, core, radius):
    square = (COLS, COLS)
    gap = (columns(query_base, core, square, 0) - columns(key_base, core, square, 1) + radius) & (COLS - 1)
    near = jnp.where(gap <= 2 * radius, 1.0, 0.0)
    for d in range(WIN + 1):
        masks[first + d] = jnp.where(radius >= d, near, 0.0)


def shifts(usable, key_base, core):
    square = (COLS, COLS)
    there = lax.broadcasted_iota(jnp.int32, square, 0) == columns(key_base, core, square, 1)
    moved = jnp.dot(usable[...], jnp.where(there, 1.0, 0.0), preferred_element_type=jnp.float32)
    return jnp.where(moved > 0.5, 0.0, -BIG)


def query_of(parts, r):
    return jnp.concatenate([part[r][:, :HEAD_DIM] for part in parts], axis=0)


def scores_of(query, ks, row):
    keys = ks[row * COLS : (row + 1) * COLS, :]
    return lax.dot_general(query, keys, NT, preferred_element_type=jnp.float32)


def inner_kernel(ints, factor_ref, band, usable, *refs):
    parts, (zonal_ref, window_ref, masks_ref, shifts_ref, ks, vs, masks) = refs[:2], refs[2:]
    factor = factor_ref[0]
    start = 0
    for part in parts:
        for r in range(ROWS):
            whole = part[r]
            put(ks, vs, r * COLS + start, whole[:, HEAD_DIM : 2 * HEAD_DIM], whole[:, 2 * HEAD_DIM :])
        start += part.shape[1]
    base, core, radius = ints[0], ints[1], ints[2]
    fill_masks(masks, 0, base, base, core, radius)
    bias = shifts(usable, base, core)
    fill_masks(masks_ref, 0, base, base + 2, core, radius)
    fill_masks(masks_ref, WIN + 1, base, base - 2, core, radius)
    shifts_ref[0] = shifts(usable, base + 2, core)
    shifts_ref[1] = shifts(usable, base - 2, core)
    eye = lax.broadcasted_iota(jnp.int32, (COLS, COLS), 0) == lax.broadcasted_iota(jnp.int32, (COLS, COLS), 1)
    for r in range(ROWS):
        query = query_of(parts, r)
        low, high = max(0, r - WIN), min(ROWS, r + WIN + 1)
        zonal_parts, window_parts = [], []
        for row in range(ROWS):
            shift = bias[WIN + row : WIN + row + 1, :]
            if row == r:
                shift = jnp.where(eye, 0.0, shift)
            weights = jnp.exp2(scores_of(query, ks, row) * factor + shift)
            zonal_parts.append((weights * band[r * ROWS + row]).astype(jnp.bfloat16))
            if low <= row < high:
                window_parts.append((weights * masks[abs(row - r)]).astype(jnp.bfloat16))
        zonal = jnp.dot(jnp.concatenate(zonal_parts, axis=1), vs[...], preferred_element_type=jnp.float32)
        window_ref[r] = jnp.dot(
            jnp.concatenate(window_parts, axis=1),
            vs[low * COLS : high * COLS, :],
            preferred_element_type=jnp.float32,
        )
        zonal_ref[r] = (zonal[:, :HEAD_DIM] / zonal[:, HEAD_DIM : HEAD_DIM + 1]).astype(jnp.bfloat16)


def inner(ints, factor, band, usable, parts):
    return pl.pallas_call(
        inner_kernel,
        out_shape=[
            jax.ShapeDtypeStruct((ROWS, COLS, HEAD_DIM), jnp.bfloat16),
            jax.ShapeDtypeStruct((ROWS, COLS, 256), jnp.float32),
            jax.ShapeDtypeStruct((2 * WIN + 2, COLS, COLS), jnp.float32),
            jax.ShapeDtypeStruct((2, KEY_ROWS, COLS), jnp.float32),
        ],
        in_specs=[SMEM] * 3 + [VMEM] * 3,
        out_specs=[VMEM] * 4,
        scratch_shapes=[
            pltpu.VMEM((ROWS * COLS, HEAD_DIM), jnp.bfloat16),
            pltpu.VMEM((ROWS * COLS, 256), jnp.bfloat16),
            pltpu.VMEM((WIN + 1, COLS, COLS), jnp.float32),
        ],
        compiler_params=pltpu.CompilerParams(vmem_limit_bytes=16 * MIB),
        cost_estimate=pl.CostEstimate(flops=10**7, bytes_accessed=10**5, transcendentals=0),
        name="inner",
    )(ints, factor, band, usable, *parts)


def outer_kernel(ints, factor_ref, zonal_ref, window_ref, masks, shifts_ref, *refs):
    parts, (own, oth, far_own, far_oth), chunks, (ks, vs, out) = refs[:2], refs[2:6], refs[6:8], refs[8:]
    factor = factor_ref[0]
    core = ints[1]
    for edge, side, half, second in ((own, core, 0, 0), (oth, core, 1, 1), (far_own, 1 - core, 1, 1), (far_oth, 1 - core, 0, 0)):
        at = 2 * HEAD_DIM * second
        for r in range(WIN):
            whole = edge[r][:, at : at + 2 * HEAD_DIM]
            first = pl.multiple_of(side * (WIN * COLS) + r * COLS + half * HALF, HALF)
            put(ks, vs, first, whole[:, :HEAD_DIM], whole[:, HEAD_DIM:])
    above, below = shifts_ref[0], shifts_ref[1]
    for r in range(ROWS):
        query = query_of(parts, r)
        rows = range(r, WIN) if r < WIN else range(WIN, r + 1)
        window_parts = []
        for row in rows:
            gap = r + WIN - row if r < WIN else ROWS + row - WIN - r
            shift = above[row : row + 1, :] if r < WIN else below[row + ROWS : row + ROWS + 1, :]
            weights = jnp.exp2(scores_of(query, ks, row) * factor + shift)
            mask = masks[gap] if r < WIN else masks[WIN + 1 + gap]
            window_parts.append((weights * mask).astype(jnp.bfloat16))
        values = vs[rows[0] * COLS : (rows[-1] + 1) * COLS, :]
        window = window_ref[r] + jnp.dot(
            jnp.concatenate(window_parts, axis=1), values, preferred_element_type=jnp.float32
        )
        window = window[:, :HEAD_DIM] / window[:, HEAD_DIM : HEAD_DIM + 1]
        total = window + zonal_ref[r].astype(jnp.float32)
        out[:, :, r * HEAD_DIM : (r + 1) * HEAD_DIM] = total.reshape(16, 8, HEAD_DIM)
    for k in range(8):
        chunks[k // 4][k % 4, 0] = out[ints[3 + k]].astype(jnp.bfloat16)
        chunks[k // 4][k % 4, 1] = out[ints[11 + k]].astype(jnp.bfloat16)


def outer(ints, factor, inner_results, parts, edges):
    chunk = jax.ShapeDtypeStruct((4, 2, 8, ROWS * HEAD_DIM), jnp.bfloat16)
    return pl.pallas_call(
        outer_kernel,
        out_shape=[chunk] * 2,
        in_specs=[SMEM, SMEM] + [VMEM] * 10,
        out_specs=[VMEM] * 2,
        scratch_shapes=[
            pltpu.VMEM((2 * WIN * COLS, HEAD_DIM), jnp.bfloat16),
            pltpu.VMEM((2 * WIN * COLS, 256), jnp.bfloat16),
            pltpu.VMEM((16, 8, ROWS * HEAD_DIM), jnp.float32),
        ],
        compiler_params=pltpu.CompilerParams(vmem_limit_bytes=16 * MIB),
        cost_estimate=pl.CostEstimate(
            flops=10**9, bytes_accessed=4 * MIB, transcendentals=10**6
        ),
        name="outer",
    )(ints, factor, *inner_results, *parts, *edges)


def regroup_kernel(far, near, *parts):
    for k, part in enumerate(parts):
        part[0] = near[k + 1]
        part[1] = far[k + 1]


def regroup(far, near):
    part = jax.ShapeDtypeStruct((2, *near.shape[1:]), near.dtype)
    return pl.pallas_call(
        regroup_kernel,
        out_shape=[part] * 3,
        in_specs=[VMEM] * 2,
        out_specs=[VMEM] * 3,
        compiler_params=pltpu.CompilerParams(vmem_limit_bytes=4 * MIB),
        cost_estimate=pl.CostEstimate(flops=0, bytes_accessed=MIB, transcendentals=0),
        name="regroup",
    )(far, near)


def assemble_kernel(at, *refs):
    width, out = ROWS * HEAD_DIM, refs[10]
    for part in range(2):
        landed = refs[5 * part : 5 * part + 5]
        for k in range(8):
            kind, x = k // 4, k % 4
            value = landed[1 - kind][0, part] if x == 0 else landed[(0, 3, 2, 4)[x]][kind, part]
            out[0, :, pl.ds(pl.multiple_of(at[8 * part + k] * width, 128), width)] = value


def assemble(at, landed):
    return pl.pallas_call(
        assemble_kernel,
        out_shape=jax.ShapeDtypeStruct((1, 8, LAT * ROWS * HEAD_DIM), jnp.bfloat16),
        in_specs=[SMEM] + [VMEM] * 10,
        out_specs=VMEM,
        compiler_params=pltpu.CompilerParams(vmem_limit_bytes=4 * MIB),
        cost_estimate=pl.CostEstimate(flops=0, bytes_accessed=MIB, transcendentals=0),
        name="assemble",
    )(at, *landed)


def body(tokens, w_qkv, key_mask, band_of_row, radius, qk_scale):
    y_lo, z, y_hi, x, core = (lax.axis_index(a) for a in AXES)
    sector = y_hi * 4 + x
    block = block_of(y_lo, y_hi, x)
    head = core * 8 + z

    normed = normalize(tokens)
    first = lax.ppermute(normed, AXES, spread_perm())

    base = (z - 2 * block) & 7
    padded = jnp.pad(key_mask, ((0, 0), (WIN, WIN)))
    usable = lax.dynamic_slice_in_dim(padded, block * ROWS, KEY_ROWS, 1)
    usable = jnp.transpose(usable).astype(jnp.float32)
    ids = lax.dynamic_slice_in_dim(band_of_row, block * ROWS, ROWS, 0)
    band = (ids[:, None] == ids[None, :]).astype(jnp.float32).reshape(ROWS * ROWS)
    groups = [
        group_at(sector ^ k, side, base, core) for side in (y_lo, 1 - y_lo) for k in range(8)
    ]
    reach = lax.dynamic_index_in_dim(radius, head, keepdims=False)
    ints = jnp.stack([base, core, reach] + groups).astype(jnp.int32)
    factor = lax.dynamic_slice_in_dim(qk_scale, head, 1, 0) / HEAD_DIM * LOG2E
    at = []
    for from_y_lo in (core, 1 - core):
        for k in range(8):
            source = sector ^ k
            at.append(block_of(from_y_lo, source >> 2, source & 3))
    at = jnp.stack(at).astype(jnp.int32)
    flags = jnp.stack([core == y_lo, core]).astype(jnp.int32)

    first, own, usable, band, ints, factor, at, flags = lax.optimization_barrier(
        (first, w_qkv[0], usable, band, ints, factor, at, flags)
    )

    partner = lax.ppermute(own, ("y_lo", "y_hi", "core"), weight_perm())

    a, b = first, lax.ppermute(first, "core", SWAP)
    pieces = [first]
    for k in range(1, 5):
        a = lax.ppermute(a, ("z", "core"), ring_perm())
        pieces.append(a)
        if k < 4:
            b = lax.ppermute(b, ("z", "core"), ring_perm())
            pieces.append(b)

    corners = ("y_lo", "y_hi", "x", "core")
    keep, send, edge, give = project(flags, pieces, own, partner)
    halo_own = lax.ppermute(edge, corners, neighbour_perm(0))
    halo_oth = lax.ppermute(give, corners, neighbour_perm(1))
    parts = keep, lax.ppermute(send, "core", SWAP)
    results = inner(ints, factor, band, usable, parts)
    halos, far = [], []
    for halo in (halo_own, halo_oth):
        halo, *results = lax.optimization_barrier((halo, *results))
        halos.append(halo)
        far.append(lax.ppermute(halo, "core", SWAP))
    halos += far
    chunks = outer(ints, factor, results, parts, halos)

    far, near = (lax.ppermute(chunks[k], ("y_lo", "y_hi", "core"), return_perm(k)) for k in (1, 0))
    passed = regroup(far, near)
    landed = [far, near]
    for k in (2, 1, 3):
        landed.append(lax.ppermute(passed[k - 1], "x", [(i, i ^ k) for i in range(4)]))
    return assemble(at, landed + [lax.ppermute(part, "core", SWAP) for part in landed])


def solution(mesh):
    wide = Mesh(mesh.devices.reshape(SIZES), AXES)
    lat, lon = ("y_lo", "z"), ("y_hi", "x", "core")
    in_specs = (P(lon, lat, None), P(lat, None, None), P(), P(), P(), P())
    out_specs = P(lat, lon, None)
    return jax.shard_map(body, mesh=wide, in_specs=in_specs, out_specs=out_specs, check_vma=False)
```
